256 devices in a mesh: row: 16 (over y, z_lo, core), col: 16 (over x, z_hi).
Axes of the slice: x: 4, y: 4, z: 8 (z_hi: 4, z_lo: 2; z = z_hi * 2 + z_lo), core: 2. Of those that a mesh axis runs over, the one named last changes fastest.
Arguments:
- features: bfloat16 [65536, 512], P('col', 'row'), may hold values from -6 to 6
- weight: bfloat16 [512, 512], replicated, may hold values from -0.25 to 0.25
- degrees: int32 [65536], replicated, may hold values from 4 to 64
- tile_values: bfloat16 [16, 16, 128, 128, 128], P('row', 'col'), may hold values from 0 to 1
- tile_row: int32 [16, 16, 128], P('row', 'col'), may hold values from 0 to 31
- tile_col: int32 [16, 16, 128], P('row', 'col'), may hold values from 0 to 31
- tile_count: int32 [16, 16], P('row', 'col'), may hold values from 16 to 128, as said below
- cotangent: bfloat16 [65536, 512], P('row', 'col'), may hold values from -6 to 6
Outputs:
- output: bfloat16 [65536, 512], P('row', 'col')
- grad_features: bfloat16 [65536, 512], P('col', 'row')
- grad_weight: float32 [512, 512], P(None, 'row')
The draws below stay inside these ranges and needn't reach their ends.
Inputs may be any that keep to these rules, and one draw needn't show every extreme that they name: tile_count equals 128 on some device in every draw.
All inputs are finite; a program needn't handle non-finite values.
Results may differ from the reference program's by a relative error of at most 0.03.
Values may be sent and summed in bfloat16 or wider, within the bound.
A program may use at most 128 MiB of HBM per device.

```python
import jax
import jax.numpy as jnp
from jax import lax

FEAT = 512
HIDDEN_SIZE = 512
TILE = 128
SEG = 256
TCAP = 128
NODES = 65536
N_ROW = 16
N_COL = 16


def draw_tile_count(key, part):
    key = jax.random.fold_in(key, 7)
    first, second, third = jax.random.split(key, 3)
    base = jax.random.randint(first, (N_ROW, N_COL), TCAP // 2, TCAP + 1)
    shifts = jax.random.randint(second, (N_ROW, N_COL), 0, 3)
    counts = jnp.maximum(base // jnp.power(2, shifts), 1).reshape(-1)
    chosen = jax.random.randint(third, (), 0, N_ROW * N_COL)
    counts = jnp.where(jnp.arange(N_ROW * N_COL) == chosen, TCAP, counts)
    return counts.reshape(N_ROW, N_COL).astype(jnp.int32)


def touch_ends(entries, rng, smallest, high):
    longest = entries.shape.index(max(entries.shape))
    spots = []
    for shift in (0, 1):
        where = [jax.random.randint(jax.random.fold_in(rng, axis), (), 0, length) for axis, length in enumerate(entries.shape)]
        where[longest] = (where[longest] + shift) % entries.shape[longest]
        spots.append(tuple(where))
    return entries.at[spots[0]].set(smallest).at[spots[1]].set(high)


def levels(key, dims, cuts, smallest, high):
    def one(dim, parts):
        steps = jax.random.uniform(jax.random.fold_in(jax.random.fold_in(key, 6), dim), (parts,), jnp.float32, smallest / len(cuts), high / len(cuts))
        return jnp.repeat(jnp.exp(steps), dims[dim] // parts).reshape((-1,) + (1,) * (len(dims) - dim - 1))

    gain = one(*cuts[0])
    for cut in cuts[1:]:
        gain = gain * one(*cut)
    return gain


def gaussian(stream_key, dims, scale, bound, cuts=(), kind=jnp.bfloat16):
    level = levels(stream_key, dims, cuts, -0.22, 0.18) if cuts else 1.0
    result = jax.random.normal(stream_key, dims, jnp.float32) * scale * level
    return jnp.minimum(jnp.maximum(result, -bound), bound).astype(kind)


def setup_inputs(seed: int = 0) -> dict:
    keys = jax.random.split(jax.random.key(seed), 9)
    features = gaussian(keys[0], (NODES, FEAT), 1.0, 6.0, ((0, 16), (1, 16)))
    weight = gaussian(keys[1], (FEAT, HIDDEN_SIZE), FEAT ** -0.5, 0.25)
    degrees = touch_ends(jax.random.randint(keys[2], (NODES,), 4, 65), jax.random.fold_in(keys[2], 1), 4, 64).astype(jnp.int32)
    tile_values = jnp.clip(1.0 * jax.random.uniform(keys[3], (N_ROW, N_COL, TCAP, TILE, TILE), jnp.float32) ** levels(keys[3], (N_ROW, N_COL, TCAP, TILE, TILE), ((0, 16), (1, 16)), -0.2, 0.2), 0.0, 1.0).astype(jnp.bfloat16)
    tile_row = touch_ends(jax.random.randint(keys[4], (N_ROW, N_COL, TCAP), 0, SEG * N_COL // TILE), jax.random.fold_in(keys[4], 1), 0, (SEG * N_COL // TILE) - 1).astype(jnp.int32)
    tile_col = touch_ends(jax.random.randint(keys[5], (N_ROW, N_COL, TCAP), 0, SEG * N_ROW // TILE), jax.random.fold_in(keys[5], 1), 0, (SEG * N_ROW // TILE) - 1).astype(jnp.int32)
    tile_count = draw_tile_count(jax.random.fold_in(keys[8], 71), 0)
    cotangent = gaussian(keys[7], (NODES, HIDDEN_SIZE), 1.0, 6.0, ((0, 16), (1, 16)))
    return {"features": features, "weight": weight, "degrees": degrees, "tile_values": tile_values, "tile_row": tile_row, "tile_col": tile_col, "tile_count": tile_count, "cotangent": cotangent}


def tile_forward(tiles, rows_of, cols_of, count, dense, blocks_out):
    pieces = dense.reshape(-1, TILE, dense.shape[1])[cols_of]
    product = jnp.einsum('tab,tbf->taf', tiles.astype(jnp.float32), pieces.astype(jnp.float32))
    target = jnp.where(jnp.arange(rows_of.shape[0]) < count, rows_of, blocks_out)
    summed = jax.ops.segment_sum(product, target, num_segments=blocks_out)
    return summed.reshape(blocks_out * TILE, dense.shape[1])

def tile_backward(tiles, rows_of, cols_of, count, dense, blocks_out):
    pieces = dense.reshape(-1, TILE, dense.shape[1])[rows_of]
    product = jnp.einsum('tab,taf->tbf', tiles.astype(jnp.float32), pieces.astype(jnp.float32))
    target = jnp.where(jnp.arange(cols_of.shape[0]) < count, cols_of, blocks_out)
    summed = jax.ops.segment_sum(product, target, num_segments=blocks_out)
    return summed.reshape(blocks_out * TILE, dense.shape[1])

def reference(features, weight, degrees, tile_values, tile_row, tile_col, tile_count, cotangent):
    row_span = SEG * N_COL
    col_span = SEG * N_ROW
    scale = lax.rsqrt(degrees.astype(jnp.float32))
    projected = (jnp.dot(features, weight, preferred_element_type=jnp.float32) * scale[:, None]).astype(jnp.bfloat16)

    def forward_group(group):

        def accumulate(total, column):
            dense = lax.dynamic_slice_in_dim(projected, (column * col_span).astype(jnp.int32), col_span, 0)
            term = tile_forward(tile_values[group, column], tile_row[group, column], tile_col[group, column], tile_count[group, column], dense, row_span // TILE)
            rounded = lax.optimization_barrier(term.astype(jnp.bfloat16))
            return (total + rounded.astype(jnp.float32), None)
        total, unused = lax.scan(accumulate, jnp.zeros((row_span, HIDDEN_SIZE), jnp.float32), jnp.arange(N_COL, dtype=jnp.int32))
        return total
    summed = lax.map(forward_group, jnp.arange(N_ROW, dtype=jnp.int32)).reshape(NODES, HIDDEN_SIZE)
    hidden_in = summed * scale[:, None]
    output = jax.nn.silu(hidden_in).astype(jnp.bfloat16)
    sigma = jax.nn.sigmoid(hidden_in)
    grad_in = (cotangent.astype(jnp.float32) * sigma * (1.0 + hidden_in * (1.0 - sigma)) * scale[:, None]).astype(jnp.bfloat16)

    def backward_group(column):

        def accumulate(total, group):
            dense = lax.dynamic_slice_in_dim(grad_in, (group * row_span).astype(jnp.int32), row_span, 0)
            term = tile_backward(tile_values[group, column], tile_row[group, column], tile_col[group, column], tile_count[group, column], dense, col_span // TILE)
            rounded = lax.optimization_barrier(term.astype(jnp.bfloat16))
            return (total + rounded.astype(jnp.float32), None)
        total, unused = lax.scan(accumulate, jnp.zeros((col_span, HIDDEN_SIZE), jnp.float32), jnp.arange(N_ROW, dtype=jnp.int32))
        return total
    back_sum = lax.map(backward_group, jnp.arange(N_COL, dtype=jnp.int32)).reshape(NODES, HIDDEN_SIZE)
    grad_proj = (back_sum * scale[:, None]).astype(jnp.bfloat16)
    grad_features = lax.dot_general(grad_proj, weight, (((1,), (1,)), ((), ())), preferred_element_type=jnp.float32).astype(jnp.bfloat16)
    grad_weight = lax.dot_general(features, grad_proj, (((0,), (0,)), ((), ())), preferred_element_type=jnp.float32)
    return (output, grad_features, grad_weight)
```

```python
import functools

import jax
import jax.numpy as jnp
from jax import lax
from jax.experimental import pallas as pl
from jax.experimental.pallas import tpu as pltpu
from jax.sharding import PartitionSpec as P

TILE = 128
N_Y, N_ZL, N_CORE = 4, 2, 2
N_X, N_ZH = 4, 4
VMEM_BYTES = 60 * 1024 * 1024
BF16, F32 = jnp.bfloat16, jnp.float32
MESH = pl.DeviceIdType.MESH


class Links:
    def __init__(self, send_sems, recv_sems):
        self.send_sems, self.recv_sems, self.used, self.open = send_sems, recv_sems, 0, []

    def start(self, src, dst, device):
        copy = pltpu.make_async_remote_copy(
            src_ref=src,
            dst_ref=dst,
            send_sem=self.send_sems.at[self.used],
            recv_sem=self.recv_sems.at[self.used],
            device_id=device,
            device_id_type=MESH,
        )
        self.used += 1
        copy.start()
        self.open.append(copy)
        return copy

    def drain(self):
        for copy in self.open:
            copy.wait_send()


def greet(peers):
    barrier = pltpu.get_barrier_semaphore()
    for peer in peers:
        pl.semaphore_signal(barrier, inc=1, device_id=peer, device_id_type=MESH)
    pl.semaphore_wait(barrier, len(peers))


def pipeline(stages, chunks):
    for step in range(chunks + len(stages) - 1):
        for stage in range(len(stages)):
            if 0 <= step - stage < chunks:
                stages[stage](step - stage)


def row_peers():
    g, h = lax.axis_index("row"), lax.axis_index("col")
    y, zl, core = g // (N_ZL * N_CORE), (g // N_CORE) % N_ZL, g % N_CORE

    def at(y_of, zl_of, core_of):
        return (y_of * N_ZL + zl_of) * N_CORE + core_of

    return g, h, y, zl, core, at


def add(left, right):
    return (left.astype(F32) + right.astype(F32)).astype(BF16)


AG_CHUNKS = 4
AG_SENDS = 17


def project_kernel(x_ref, wt_ref, scale_ref, all_ref, proj_ref, send_sems, recv_sems):
    links = Links(send_sems, recv_sems)
    g, h, y, zl, core, at = row_peers()
    up, down, far = (y + 1) % N_Y, (y + N_Y - 1) % N_Y, (y + 2) % N_Y
    zp = 1 - zl
    right, left = (at(up, zl, core), h), (at(down, zl, core), h)
    z_peer, c_peer = (at(y, zp, core), h), (at(y, zl, 1 - core), h)
    greet([right, left, z_peer, c_peer])
    span = x_ref.shape[1] // AG_CHUNKS
    depth = x_ref.shape[0]
    half = depth // 2
    all_ref[g] = x_ref[...]
    sent = {}

    def lanes(q):
        return pl.ds(q * span, span)

    def block(owner, q, rows=slice(None)):
        return all_ref.at[owner, rows, lanes(q)]

    def forward(owner, q, device, rows=slice(None)):
        return links.start(block(owner, q, rows), block(owner, q, rows), device)

    first, second = pl.ds(0, half), pl.ds(half, half)

    def stage_own(q):
        src = x_ref.at[:, lanes(q)]
        for name, device in (("z", z_peer), ("r", right), ("l", left), ("c0", c_peer)):
            sent[name, q] = links.start(src, block(g, q), device)

    def stage_z(q):
        sent["z", q].wait_recv()
        owner = at(y, zp, core)
        for name, device in (("zr", right), ("zl", left), ("c1", c_peer)):
            sent[name, q] = forward(owner, q, device)

    def stage_y(q):
        sent["r", q].wait_recv()
        sent["fr", q] = forward(at(down, zl, core), q, right, first)
        sent["l", q].wait_recv()
        sent["fl", q] = forward(at(up, zl, core), q, left, second)
        sent["c2", q] = forward(at(down, zl, core), q, c_peer)
        sent["c3", q] = forward(at(up, zl, core), q, c_peer)

    def stage_zy(q):
        sent["zr", q].wait_recv()
        sent["gr", q] = forward(at(down, zp, core), q, right, first)
        sent["zl", q].wait_recv()
        sent["gl", q] = forward(at(up, zp, core), q, left, second)
        sent["c4", q] = forward(at(down, zp, core), q, c_peer)
        sent["c5", q] = forward(at(up, zp, core), q, c_peer)

    def stage_far(q):
        sent["fr", q].wait_recv()
        sent["fl", q].wait_recv()
        sent["c6", q] = forward(at(far, zl, core), q, c_peer)
        sent["gr", q].wait_recv()
        sent["gl", q].wait_recv()
        sent["c7", q] = forward(at(far, zp, core), q, c_peer)

    def stage_project(q):
        for i in range(8):
            sent["c%d" % i, q].wait_recv()
        wide = min(span, 256)

        @pl.loop(0, span // wide)
        def one(j):
            where = pl.ds(pl.multiple_of(q * span + j * wide, wide), wide)
            x = all_ref[:, :, where].reshape(-1, wide)
            value = jnp.dot(wt_ref[...], x, preferred_element_type=F32)
            proj_ref[:, where] = (value * scale_ref[:, where]).astype(BF16)

    pipeline([stage_own, stage_z, stage_y, stage_zy, stage_far, stage_project], AG_CHUNKS)
    links.drain()


def gather_project(x, wt, scale):
    depth, span = x.shape
    hidden = wt.shape[0]
    vmem = pl.BlockSpec(memory_space=pltpu.VMEM)
    count = AG_CHUNKS * AG_SENDS
    return pl.pallas_call(
        project_kernel,
        out_shape=(
            jax.ShapeDtypeStruct((N_Y * N_ZL * N_CORE, depth, span), BF16),
            jax.ShapeDtypeStruct((hidden, span), BF16),
        ),
        in_specs=[vmem] * 3,
        out_specs=(vmem, vmem),
        scratch_shapes=[pltpu.SemaphoreType.DMA((count,)), pltpu.SemaphoreType.DMA((count,))],
        compiler_params=pltpu.CompilerParams(
            collective_id=0, has_side_effects=True, vmem_limit_bytes=VMEM_BYTES
        ),
        name="gather_project",
    )(x, wt, scale)


GROUP = 4


def spmm_kernel(transpose, gather_ref, target_ref, count_ref, tiles_ref, dense_ref, out_ref, acc_ref):
    blocks = out_ref.shape[1] // TILE
    contract = (((1,), (1,)), ((), ())) if transpose else (((1,), (0,)), ((), ()))

    @pl.loop(0, blocks)
    def clear(j):
        acc_ref[:, pl.ds(pl.multiple_of(j * TILE, TILE), TILE)] = jnp.zeros(
            (acc_ref.shape[0], TILE), F32
        )

    count = count_ref[0]

    @pl.loop(0, (count + GROUP - 1) // GROUP)
    def step(i):
        products, targets = [], []
        for j in range(GROUP):
            t = i * GROUP + j
            source = pl.multiple_of(gather_ref[t] * TILE, TILE)
            products.append(
                lax.dot_general(
                    dense_ref[:, pl.ds(source, TILE)],
                    tiles_ref[t],
                    contract,
                    preferred_element_type=F32,
                )
            )
            place = jnp.where(t < count, target_ref[t], blocks)
            targets.append(pl.multiple_of(place * TILE, TILE))
        for product, place in zip(products, targets):
            acc_ref[:, pl.ds(place, TILE)] += product

    @pl.loop(0, blocks)
    def finish(j):
        where = pl.ds(pl.multiple_of(j * TILE, TILE), TILE)
        out_ref[:, where] = acc_ref[:, where].astype(BF16)


def spmm(transpose, gather_of, target_of, count, tiles, dense):
    smem = pl.BlockSpec(memory_space=pltpu.SMEM)
    vmem = pl.BlockSpec(memory_space=pltpu.VMEM)
    hidden, span = dense.shape
    return pl.pallas_call(
        functools.partial(spmm_kernel, transpose),
        out_shape=jax.ShapeDtypeStruct((hidden, span), BF16),
        in_specs=[smem, smem, smem, vmem, vmem],
        out_specs=vmem,
        scratch_shapes=[pltpu.VMEM((hidden, span + TILE), F32)],
        compiler_params=pltpu.CompilerParams(vmem_limit_bytes=VMEM_BYTES),
        name="spmm_t" if transpose else "spmm",
    )(gather_of, target_of, count, tiles, dense)


MID_CHUNKS = 4
MID_SENDS = 4 + 2 + 3 + 3 + 2 + 2


def middle_kernel(
    part_ref, cot_ref, scale_ref, grad_ref, out_ref,
    in_ref, merge_ref, sum_ref, z_ref, send_sems, recv_sems,
):
    links = Links(send_sems, recv_sems)
    g, h = lax.axis_index("row"), lax.axis_index("col")
    x, zh = h // N_ZH, h % N_ZH
    up, down, far = (x + 1) % N_X, (x + N_X - 1) % N_X, (x + 2) % N_X
    right, left = (g, up * N_ZH + zh), (g, down * N_ZH + zh)
    z_peers = [(g, x * N_ZH + (zh + d) % N_ZH) for d in range(1, N_ZH)]
    greet([right, left] + z_peers)
    nodes = part_ref.shape[1]
    span = nodes // MID_CHUNKS
    own = cot_ref.shape[0]
    group = own * N_ZH
    half = group // 2
    sent = {}

    def lanes(q):
        return pl.ds(q * span, span)

    def part(x_of, side, q):
        start = pl.multiple_of(x_of * group + side * half, half)
        return part_ref.at[pl.ds(start, half), lanes(q)]

    def slot(i, q):
        return in_ref.at[i, :, lanes(q)]

    def reduce_out(q):
        sent["f0", q] = links.start(part(far, 0, q), slot(0, q), right)
        sent["f1", q] = links.start(part(far, 1, q), slot(1, q), left)
        sent["d0", q] = links.start(part(up, 1, q), slot(2, q), right)
        sent["d1", q] = links.start(part(down, 0, q), slot(3, q), left)

    def reduce_merge(q):
        sent["f0", q].wait_recv()
        merge_ref[0, :, lanes(q)] = add(slot(0, q)[...], part(up, 0, q)[...])
        sent["m0", q] = links.start(merge_ref.at[0, :, lanes(q)], slot(4, q), right)
        sent["f1", q].wait_recv()
        merge_ref[1, :, lanes(q)] = add(slot(1, q)[...], part(down, 1, q)[...])
        sent["m1", q] = links.start(merge_ref.at[1, :, lanes(q)], slot(5, q), left)

    def reduce_z(q):
        for name in ("d0", "d1", "m0", "m1"):
            sent[name, q].wait_recv()
        for side, (merged, direct) in enumerate(((4, 3), (5, 2))):
            total = slot(merged, q)[...].astype(F32) + slot(direct, q)[...].astype(F32)
            total = total + part(x, side, q)[...].astype(F32)
            sum_ref[pl.ds(side * half, half), lanes(q)] = total.astype(BF16)
        for d in range(1, N_ZH):
            rows = pl.ds(pl.multiple_of(((zh + d) % N_ZH) * own, own), own)
            sent["z", d, q] = links.start(
                sum_ref.at[rows, lanes(q)], z_ref.at[d - 1, :, lanes(q)], z_peers[d - 1]
            )

    def activate(q):
        value = sum_ref[pl.ds(pl.multiple_of(zh * own, own), own), lanes(q)].astype(F32)
        for d in range(1, N_ZH):
            sent["z", d, q].wait_recv()
            value = value + z_ref[d - 1, :, lanes(q)].astype(F32)
        scale = scale_ref[:, lanes(q)]
        hidden = value * scale
        sigma = 1.0 / (1.0 + jnp.exp(-hidden))
        out_ref[:, lanes(q)] = (hidden * sigma).astype(BF16)
        grad = cot_ref[:, lanes(q)].astype(F32) * sigma * (1.0 + hidden * (1.0 - sigma)) * scale
        grad_ref[h, :, lanes(q)] = grad.astype(BF16)
        mine = grad_ref.at[h, :, lanes(q)]
        for d in range(1, N_ZH):
            sent["g", d, q] = links.start(mine, mine, z_peers[d - 1])

    def gather_x(q):
        for d in range(1, N_ZH):
            sent["g", d, q].wait_recv()
        mine = grad_ref.at[pl.ds(x * N_ZH, N_ZH), :, lanes(q)]
        sent["gr", q] = links.start(mine, mine, right)
        sent["gl", q] = links.start(mine, mine, left)

    def gather_far(q):
        sent["gr", q].wait_recv()
        first = grad_ref.at[pl.ds(down * N_ZH, N_ZH // 2), :, lanes(q)]
        sent["hr", q] = links.start(first, first, right)
        sent["gl", q].wait_recv()
        second = grad_ref.at[pl.ds(up * N_ZH + N_ZH // 2, N_ZH // 2), :, lanes(q)]
        sent["hl", q] = links.start(second, second, left)

    def gather_end(q):
        sent["hr", q].wait_recv()
        sent["hl", q].wait_recv()

    pipeline(
        [reduce_out, reduce_merge, reduce_z, activate, gather_x, gather_far, gather_end],
        MID_CHUNKS,
    )
    links.drain()


def middle(part, cot, scale):
    hidden, span = part.shape
    own = cot.shape[0]
    half = own * N_ZH // 2
    vmem = pl.BlockSpec(memory_space=pltpu.VMEM)
    count = MID_CHUNKS * MID_SENDS
    return pl.pallas_call(
        middle_kernel,
        out_shape=(
            jax.ShapeDtypeStruct((N_X * N_ZH, own, span), BF16),
            jax.ShapeDtypeStruct((own, span), BF16),
        ),
        in_specs=[vmem] * 3,
        out_specs=(vmem, vmem),
        scratch_shapes=[
            pltpu.VMEM((6, half, span), BF16),
            pltpu.VMEM((2, half, span), BF16),
            pltpu.VMEM((2 * half, span), BF16),
            pltpu.VMEM((N_ZH - 1, own, span), BF16),
            pltpu.SemaphoreType.DMA((count,)),
            pltpu.SemaphoreType.DMA((count,)),
        ],
        compiler_params=pltpu.CompilerParams(
            collective_id=1, has_side_effects=True, vmem_limit_bytes=VMEM_BYTES
        ),
        name="middle",
    )(part, cot, scale)


END_CHUNKS = 4
END_SENDS = 1 + 4 + 2 + 1


def final_kernel(
    back_ref, x_ref, w_ref, scale_ref, gf_ref, gw_ref,
    core_ref, half_ref, in_ref, merge_ref, sum_ref, z_ref, gp_ref, gft_ref, gpa_ref,
    lw_ref, px_ref, pz_ref, send_sems, recv_sems,
):
    links = Links(send_sems, recv_sems)
    g, h, y, zl, core, at = row_peers()
    rows_in_all = N_Y * N_ZL * N_CORE
    x, zh = h // N_ZH, h % N_ZH
    up, down, far = (y + 1) % N_Y, (y + N_Y - 1) % N_Y, (y + 2) % N_Y
    zp = 1 - zl
    right, left = (at(up, zl, core), h), (at(down, zl, core), h)
    z_peer, c_peer = (at(y, zp, core), h), (at(y, zl, 1 - core), h)
    row_group = [((g + d) % rows_in_all, h) for d in range(1, rows_in_all)]
    x_group = [(g, ((x + d) % N_X) * N_ZH + zh) for d in range(1, N_X)]
    zh_group = [(g, x * N_ZH + (zh + d) % N_ZH) for d in range(1, N_ZH)]
    greet(row_group + x_group + zh_group)
    hidden, nodes = back_ref.shape
    rows = hidden // END_CHUNKS
    mine = nodes // rows_in_all
    side_nodes = nodes // N_CORE
    y_nodes = mine * N_ZL
    half = rows // 2
    sent = {}

    def chunk(q, start=0, size=rows):
        return pl.ds(q * rows + start, size)

    def core_out(q):
        there = pl.ds(pl.multiple_of((1 - core) * side_nodes, side_nodes), side_nodes)
        sent["c", q] = links.start(back_ref.at[chunk(q), there], core_ref.at[chunk(q), :], c_peer)

    def y_part(y_of, side, q):
        lanes = pl.ds(pl.multiple_of(y_of * y_nodes, y_nodes), y_nodes)
        return half_ref.at[chunk(q, side * half, half), lanes]

    def slot(i, q):
        return in_ref.at[i, pl.ds(q * half, half), :]

    def y_out(q):
        sent["c", q].wait_recv()
        wide = min(side_nodes, 512)

        @pl.loop(0, side_nodes // wide)
        def one(j):
            offset = pl.multiple_of(j * wide, wide)
            there = pl.ds(pl.multiple_of(core * side_nodes + j * wide, wide), wide)
            half_ref[chunk(q), pl.ds(offset, wide)] = add(
                back_ref[chunk(q), there], core_ref[chunk(q), pl.ds(offset, wide)]
            )

        sent["f0", q] = links.start(y_part(far, 0, q), slot(0, q), right)
        sent["f1", q] = links.start(y_part(far, 1, q), slot(1, q), left)
        sent["d0", q] = links.start(y_part(up, 1, q), slot(2, q), right)
        sent["d1", q] = links.start(y_part(down, 0, q), slot(3, q), left)

    def y_merge(q):
        sent["f0", q].wait_recv()
        merge_ref[0, pl.ds(q * half, half), :] = add(slot(0, q)[...], y_part(up, 0, q)[...])
        sent["m0", q] = links.start(merge_ref.at[0, pl.ds(q * half, half), :], slot(4, q), right)
        sent["f1", q].wait_recv()
        merge_ref[1, pl.ds(q * half, half), :] = add(slot(1, q)[...], y_part(down, 1, q)[...])
        sent["m1", q] = links.start(merge_ref.at[1, pl.ds(q * half, half), :], slot(5, q), left)

    def z_out(q):
        for name in ("d0", "d1", "m0", "m1"):
            sent[name, q].wait_recv()
        for side, (merged, direct) in enumerate(((4, 3), (5, 2))):
            total = slot(merged, q)[...].astype(F32) + slot(direct, q)[...].astype(F32)
            total = total + y_part(y, side, q)[...].astype(F32)
            sum_ref[chunk(q, side * half, half), :] = total.astype(BF16)
        there = pl.ds(pl.multiple_of(zp * mine, mine), mine)
        sent["z", q] = links.start(sum_ref.at[chunk(q), there], z_ref.at[chunk(q), :], z_peer)

    def scaled(q):
        sent["z", q].wait_recv()
        here = pl.ds(pl.multiple_of(zl * mine, mine), mine)
        value = sum_ref[chunk(q), here].astype(F32) + z_ref[chunk(q), :].astype(F32)
        gp_ref[chunk(q), :] = (value * scale_ref[...]).astype(BF16)

    pipeline([core_out, y_out, y_merge, z_out, scaled], END_CHUNKS)

    own = hidden // rows_in_all
    place = pl.ds(pl.multiple_of(core * side_nodes + (y * N_ZL + zl) * mine, mine), mine)

    def spread(src_ref, dst_ref):
        copies = []
        for d in range(1, rows_in_all):
            other = pl.ds(pl.multiple_of(((g + d) % rows_in_all) * own, own), own)
            copies.append(links.start(src_ref.at[other, :], dst_ref.at[:, place], row_group[d - 1]))
        dst_ref[:, place] = src_ref[pl.ds(pl.multiple_of(g * own, own), own), :]
        return copies

    grads = spread(gp_ref, gpa_ref)
    gft_ref[...] = jnp.dot(w_ref[...], gp_ref[...], preferred_element_type=F32).astype(BF16)
    outs = spread(gft_ref, gf_ref)
    for copy in grads:
        copy.wait_recv()
    feats = x_ref.shape[0]
    wide = min(nodes, 512)
    total = jnp.zeros((own, feats), F32)
    for j in range(nodes // wide):
        where = pl.ds(j * wide, wide)
        total = total + lax.dot_general(
            gpa_ref[:, where], x_ref[:, where], (((1,), (1,)), ((), ())), preferred_element_type=F32
        )

    def share(total, buffer, index, group):
        lw_ref[index] = total.astype(BF16)
        copies = [
            links.start(lw_ref.at[index], buffer.at[i], peer) for i, peer in enumerate(group)
        ]
        for i, copy in enumerate(copies):
            copy.wait_recv()
            total = total + buffer[i].astype(F32)
        return total

    total = share(total, px_ref, 0, x_group)
    gw_ref[...] = share(total, pz_ref, 1, zh_group)
    for copy in outs:
        copy.wait_recv()
    links.drain()


def final(back, x_all, w, scale):
    hidden, span = back.shape
    feats = x_all.shape[0]
    rows_in_all = N_Y * N_ZL * N_CORE
    own = hidden // rows_in_all
    mine = span // rows_in_all
    vmem = pl.BlockSpec(memory_space=pltpu.VMEM)
    count = END_CHUNKS * END_SENDS + 2 * (rows_in_all - 1) + (N_X - 1) + (N_ZH - 1)
    y_nodes = mine * N_ZL
    return pl.pallas_call(
        final_kernel,
        out_shape=(
            jax.ShapeDtypeStruct((own, span), BF16),
            jax.ShapeDtypeStruct((own, feats), F32),
        ),
        in_specs=[vmem] * 4,
        out_specs=(vmem, vmem),
        scratch_shapes=[
            pltpu.VMEM((hidden, span // N_CORE), BF16),
            pltpu.VMEM((hidden, span // N_CORE), BF16),
            pltpu.VMEM((6, hidden // 2, y_nodes), BF16),
            pltpu.VMEM((2, hidden // 2, y_nodes), BF16),
            pltpu.VMEM((hidden, y_nodes), BF16),
            pltpu.VMEM((hidden, mine), BF16),
            pltpu.VMEM((hidden, mine), BF16),
            pltpu.VMEM((feats, mine), BF16),
            pltpu.VMEM((own, span), BF16),
            pltpu.VMEM((2, own, feats), BF16),
            pltpu.VMEM((N_X - 1, own, feats), BF16),
            pltpu.VMEM((N_ZH - 1, own, feats), BF16),
            pltpu.SemaphoreType.DMA((count,)),
            pltpu.SemaphoreType.DMA((count,)),
        ],
        compiler_params=pltpu.CompilerParams(
            collective_id=2, has_side_effects=True, vmem_limit_bytes=VMEM_BYTES
        ),
        name="final",
    )(back, x_all, w, scale)


def shards(features, weight, degrees, tile_values, tile_row, tile_col, tile_count, cotangent):
    g = lax.axis_index("row")
    h = lax.axis_index("col")
    tiles, rows_of, cols_of = tile_values[0, 0], tile_row[0, 0], tile_col[0, 0]
    count = tile_count[0]
    nodes = features.shape[0]
    scale_of = lambda start, size: lax.rsqrt(
        lax.dynamic_slice_in_dim(degrees, start, size, 0).astype(F32)
    )[None, :]
    col_scale = scale_of(h * nodes, nodes)
    row_scale = scale_of(g * nodes, nodes)
    mine = nodes // (N_Y * N_ZL * N_CORE)
    place = (g % N_CORE) * (nodes // N_CORE) + (g // N_CORE) * mine
    mine_scale = scale_of(h * nodes + place, mine)
    x_all, projected = gather_project(features.T, weight.T, col_scale)
    part = spmm(True, cols_of, rows_of, count, tiles, projected)
    grad_in, output = middle(part, cotangent.T, row_scale)
    back = spmm(False, rows_of, cols_of, count, tiles, grad_in.reshape(part.shape))
    grad_features, grad_weight = final(
        back, x_all.reshape(-1, nodes), weight, mine_scale
    )
    return (output.T, grad_features.T, grad_weight.T)


def solution(mesh):
    in_specs = (
        P("col", "row"),
        P(),
        P(),
        P("row", "col", None, None, None),
        P("row", "col", None),
        P("row", "col", None),
        P("row", "col"),
        P("row", "col"),
    )
    out_specs = (P("row", "col"), P("col", "row"), P(None, "row"))
    return jax.shard_map(shards, mesh=mesh, in_specs=in_specs, out_specs=out_specs, check_vma=False)
```

```python
import jax
import jax.numpy as jnp
from jax import lax
from jax.experimental import pallas as pl
from jax.experimental.pallas import tpu as pltpu
from jax.sharding import PartitionSpec as P

TILE = 128
PARTS = 2
N_Y, N_ZL, N_CORE = 4, 2, 2
N_X, N_ZH = 4, 4
N_ROW, N_COL = N_Y * N_ZL * N_CORE, N_X * N_ZH
AG_CHUNKS = 4
MID_CHUNKS = 4
END_CHUNKS = 2
GROUP = 4
VMEM_BYTES = 60 * 1024 * 1024
BF16, F32, I32 = jnp.bfloat16, jnp.float32, jnp.int32
MESH = pl.DeviceIdType.MESH
SENDS = (
    AG_CHUNKS * 17
    + PARTS * MID_CHUNKS * 16
    + PARTS * END_CHUNKS * 8
    + (PARTS + 1) * (N_ROW - 1)
    + PARTS * (N_X - 1 + N_ZH - 1)
)


class Links:
    def __init__(self, send_sems, recv_sems):
        self.send_sems, self.recv_sems, self.used, self.open = send_sems, recv_sems, 0, []

    def start(self, src, dst, device):
        copy = pltpu.make_async_remote_copy(
            src_ref=src,
            dst_ref=dst,
            send_sem=self.send_sems.at[self.used],
            recv_sem=self.recv_sems.at[self.used],
            device_id=device,
            device_id_type=MESH,
        )
        self.used += 1
        copy.start()
        self.open.append(copy)
        return copy

    def drain(self):
        for copy in self.open:
            copy.wait_send()


def greet(peers):
    barrier = pltpu.get_barrier_semaphore()
    for peer in peers:
        pl.semaphore_signal(barrier, inc=1, device_id=peer, device_id_type=MESH)
    pl.semaphore_wait(barrier, len(peers))


def add(left, right):
    return (left.astype(F32) + right.astype(F32)).astype(BF16)


def sorted_by(key, gather):
    shape = (TILE, TILE)
    i = lax.broadcasted_iota(I32, shape, 0)
    j = lax.broadcasted_iota(I32, shape, 1)
    across = jnp.broadcast_to(key, shape)
    down = across.T
    before = (down < across) | ((down == across) & (i < j))
    rank = jnp.broadcast_to(jnp.sum(before.astype(I32), axis=0, keepdims=True), shape).T

    def total(where, value):
        return jnp.sum(jnp.where(where, value, 0), axis=0, keepdims=True)

    order = total(rank == j, i)
    source = total(rank == j, jnp.broadcast_to(gather, shape).T)
    same = (total(rank == j, down) == total(rank == j - 1, down)).astype(I32)
    last = jnp.maximum(total(down <= j, 1) - 1, 0)
    some = jnp.minimum(total(down == j, 1), 1)
    return [order, source, last, same, some]


def plan_kernel(rows_ref, cols_ref, count_ref, table_ref):
    live = lax.broadcasted_iota(I32, (1, TILE), 1) < count_ref[0, 0]
    rows_of, cols_of = rows_ref[...], cols_ref[...]
    lines = sorted_by(jnp.where(live, rows_of, TILE), cols_of)
    lines += sorted_by(jnp.where(live, cols_of, TILE), rows_of)
    table_ref[...] = jnp.zeros_like(table_ref)
    for i, line in enumerate(lines):
        table_ref[pl.ds(i, 1), :] = line


def kernel(
    x_hbm, w_hbm, deg_hbm, tiles_hbm, idx_ref, table_ref, cot_hbm,
    out_ref, gf_ref, gw_ref,
    all_ref, tiles_ref, w_ref, wt_ref, cot_ref, deg_ref, cs_ref, rs_ref, same_ref, some_ref,
    proj_ref, seg_ref, acc_ref, part_ref,
    in_ref, merge_ref, sum_ref, z_ref, g0_ref, g1_ref, back_ref,
    core_ref, half_ref, yin_ref, ymerge_ref, ysum_ref, zin_ref, gp_ref, gft_ref, gpa_ref,
    lw_ref, px_ref, pz_ref, local_sems, send_sems, recv_sems,
):
    links = Links(send_sems, recv_sems)
    g, h = lax.axis_index("row"), lax.axis_index("col")
    y, zl, core = g // (N_ZL * N_CORE), (g // N_CORE) % N_ZL, g % N_CORE
    x, zh = h // N_ZH, h % N_ZH
    zp = 1 - zl

    def at(y_of, zl_of, core_of):
        return (y_of * N_ZL + zl_of) * N_CORE + core_of

    y_up, y_down, y_far = (y + 1) % N_Y, (y + N_Y - 1) % N_Y, (y + 2) % N_Y
    x_up, x_down, x_far = (x + 1) % N_X, (x + N_X - 1) % N_X, (x + 2) % N_X
    y_right, y_left = (at(y_up, zl, core), h), (at(y_down, zl, core), h)
    x_right, x_left = (g, x_up * N_ZH + zh), (g, x_down * N_ZH + zh)
    z_peer, c_peer = (at(y, zp, core), h), (at(y, zl, 1 - core), h)
    row_group = [((g + d) % N_ROW, h) for d in range(1, N_ROW)]
    x_group = [(g, ((x + d) % N_X) * N_ZH + zh) for d in range(1, N_X)]
    zh_group = [(g, x * N_ZH + (zh + d) % N_ZH) for d in range(1, N_ZH)]

    nodes = x_hbm.shape[1]
    hidden = w_ref.shape[1]
    wide = hidden // PARTS
    depth = x_hbm.shape[0]
    own = depth // PARTS
    blocks = nodes // TILE
    deg_rows = nodes // TILE
    sent = {}

    local = {}
    loads = (
        ("x", x_hbm, all_ref.at[g]),
        ("w", w_hbm, w_ref),
        ("dc", deg_hbm.at[pl.ds(pl.multiple_of(h * deg_rows, deg_rows), deg_rows)], deg_ref.at[0]),
        ("dr", deg_hbm.at[pl.ds(pl.multiple_of(g * deg_rows, deg_rows), deg_rows)], deg_ref.at[1]),
        ("tiles", tiles_hbm, tiles_ref),
        ("cot", cot_hbm, cot_ref),
    )
    for i, (name, src, dst) in enumerate(loads):
        local[name] = pltpu.make_async_copy(src, dst, local_sems.at[i])
        local[name].start()

    greet(row_group + x_group + zh_group)

    ag_span = nodes // AG_CHUNKS
    first, second = pl.ds(0, depth // 2), pl.ds(depth // 2, depth // 2)

    def ag_lanes(q):
        return pl.ds(q * ag_span, ag_span)

    def forward(owner, q, device, rows=slice(None)):
        block = all_ref.at[owner, rows, ag_lanes(q)]
        return links.start(block, block, device)

    def ag_own(q):
        src = x_hbm.at[:, ag_lanes(q)]
        for name, device in (("z", z_peer), ("r", y_right), ("l", y_left), ("c0", c_peer)):
            sent[name, q] = links.start(src, all_ref.at[g, :, ag_lanes(q)], device)

    def ag_z(q):
        sent["z", q].wait_recv()
        owner = at(y, zp, core)
        for name, device in (("zr", y_right), ("zl", y_left), ("c1", c_peer)):
            sent[name, q] = forward(owner, q, device)

    def ag_y(q):
        sent["r", q].wait_recv()
        sent["fr", q] = forward(at(y_down, zl, core), q, y_right, first)
        sent["l", q].wait_recv()
        sent["fl", q] = forward(at(y_up, zl, core), q, y_left, second)
        sent["c2", q] = forward(at(y_down, zl, core), q, c_peer)
        sent["c3", q] = forward(at(y_up, zl, core), q, c_peer)

    def ag_zy(q):
        sent["zr", q].wait_recv()
        sent["gr", q] = forward(at(y_down, zp, core), q, y_right, first)
        sent["zl", q].wait_recv()
        sent["gl", q] = forward(at(y_up, zp, core), q, y_left, second)
        sent["c4", q] = forward(at(y_down, zp, core), q, c_peer)
        sent["c5", q] = forward(at(y_up, zp, core), q, c_peer)

    def ag_far(q):
        sent["fr", q].wait_recv()
        sent["fl", q].wait_recv()
        sent["c6", q] = forward(at(y_far, zl, core), q, c_peer)
        sent["gr", q].wait_recv()
        sent["gl", q].wait_recv()
        sent["c7", q] = forward(at(y_far, zp, core), q, c_peer)

    def project(q):
        for i in range(8):
            sent["c%d" % i, q].wait_recv()
        if q == 0:
            local["x"].wait()
        step = min(ag_span, 256)

        @pl.loop(0, ag_span // step)
        def one(j):
            where = pl.ds(pl.multiple_of(q * ag_span + j * step, step), step)
            block = all_ref[:, :, where].reshape(-1, step)
            for p in range(PARTS):
                value = jnp.dot(
                    wt_ref[pl.ds(p * wide, wide), :], block, preferred_element_type=F32
                )
                proj_ref[p, :, where] = (value * cs_ref[:, where]).astype(BF16)

    def prepare():
        local["w"].wait()
        turned = w_ref[...].T
        for owner in range(N_COL):
            for p in range(PARTS):
                start = owner * depth + p * own
                wt_ref[pl.ds(p * wide + owner * own, own), :] = turned[start : start + own, :]
        local["dc"].wait()
        local["dr"].wait()
        for ref, i in ((cs_ref, 0), (rs_ref, 1)):
            scale = lax.rsqrt(deg_ref[i].astype(F32))
            for j in range(deg_rows):
                ref[:, pl.ds(j * TILE, TILE)] = scale[j : j + 1, :]
        for i in range(2):
            for ref, line in ((same_ref, 5 * i + 3), (some_ref, 5 * i + 4)):
                flags = table_ref[pl.ds(line, 1), :].astype(F32)
                ref[i] = jnp.broadcast_to(flags, (TILE, TILE)).T
        local["tiles"].wait()
        local["cot"].wait()

    def tiles_times(way, dense, contract, first_tile, tiles):
        @pl.loop(first_tile // GROUP, (first_tile + tiles) // GROUP)
        def step(i):
            products = []
            for j in range(GROUP):
                t = i * GROUP + j
                source = pl.ds(idx_ref[5 * way + 1, t] * TILE, TILE)
                products.append(
                    lax.dot_general(
                        dense(source),
                        tiles_ref[idx_ref[5 * way, t]],
                        contract,
                        preferred_element_type=F32,
                    )
                )
            total = acc_ref[...]
            for j in range(GROUP):
                t = i * GROUP + j
                total = total * same_ref[way, pl.ds(t, 1), :] + products[j]
                seg_ref[t] = total.astype(BF16)
            acc_ref[...] = total

    def clear():
        acc_ref[...] = jnp.zeros_like(acc_ref)

    def collect(way, ref, p):
        @pl.loop(0, blocks)
        def one(b):
            value = seg_ref[idx_ref[5 * way + 2, b]]
            where = pl.ds(pl.multiple_of(b * TILE, TILE), TILE)
            some = some_ref[way, pl.ds(b, 1), :]
            ref[p, :, where] = (value.astype(F32) * some).astype(BF16)

    by_row = (((1,), (1,)), ((), ()))
    by_col = (((1,), (0,)), ((), ()))
    grads = (g0_ref, g1_ref)

    def forward_tiles(p):
        clear()
        tiles_times(0, lambda source: proj_ref[p, :, source], by_row, 0, TILE)
        collect(0, part_ref, p)

    def backward_tiles(p, first_tile, tiles):
        if first_tile == 0:
            clear()
        tiles_times(
            1,
            lambda source: grads[p][:, :, source].reshape(wide, TILE),
            by_col,
            first_tile,
            tiles,
        )
        if first_tile + tiles == TILE:
            collect(1, back_ref, p)

    span = nodes // MID_CHUNKS
    x_rows = own * N_ZH
    x_half = x_rows // 2

    def unit(u):
        p, q = u // MID_CHUNKS, u % MID_CHUNKS
        return p, pl.ds(q * span, span)

    def part(x_of, side, u):
        p, lanes = unit(u)
        start = pl.multiple_of(x_of * x_rows + side * x_half, x_half)
        return part_ref.at[p, pl.ds(start, x_half), lanes]

    def slot(i, u):
        p, lanes = unit(u)
        return in_ref.at[i, p, :, lanes]

    def merged(i, u):
        p, lanes = unit(u)
        return merge_ref.at[i, p, :, lanes]

    def reduce_out(u):
        sent["f0", u] = links.start(part(x_far, 0, u), slot(0, u), x_right)
        sent["f1", u] = links.start(part(x_far, 1, u), slot(1, u), x_left)
        sent["d0", u] = links.start(part(x_up, 1, u), slot(2, u), x_right)
        sent["d1", u] = links.start(part(x_down, 0, u), slot(3, u), x_left)

    def reduce_merge(u):
        sent["f0", u].wait_recv()
        merged(0, u)[...] = add(slot(0, u)[...], part(x_up, 0, u)[...])
        sent["m0", u] = links.start(merged(0, u), slot(4, u), x_right)
        sent["f1", u].wait_recv()
        merged(1, u)[...] = add(slot(1, u)[...], part(x_down, 1, u)[...])
        sent["m1", u] = links.start(merged(1, u), slot(5, u), x_left)

    def reduce_z(u):
        p, lanes = unit(u)
        for name in ("d0", "d1", "m0", "m1"):
            sent[name, u].wait_recv()
        for side, (through, direct) in enumerate(((4, 3), (5, 2))):
            total = slot(through, u)[...].astype(F32) + slot(direct, u)[...].astype(F32)
            total = total + part(x, side, u)[...].astype(F32)
            sum_ref[p, pl.ds(side * x_half, x_half), lanes] = total.astype(BF16)
        for d in range(1, N_ZH):
            rows = pl.ds(pl.multiple_of(((zh + d) % N_ZH) * own, own), own)
            sent["z", d, u] = links.start(
                sum_ref.at[p, rows, lanes], z_ref.at[d - 1, p, :, lanes], zh_group[d - 1]
            )

    def activate(u):
        p, lanes = unit(u)
        value = sum_ref[p, pl.ds(pl.multiple_of(zh * own, own), own), lanes].astype(F32)
        for d in range(1, N_ZH):
            sent["z", d, u].wait_recv()
            value = value + z_ref[d - 1, p, :, lanes].astype(F32)
        scale = rs_ref[:, lanes]
        hidden_in = value * scale
        sigma = 1.0 / (1.0 + jnp.exp(-hidden_in))
        rows = pl.ds(p * own, own)
        out_ref[rows, lanes] = (hidden_in * sigma).astype(BF16)
        slope = sigma * (1.0 + hidden_in * (1.0 - sigma))
        grad = cot_ref[rows, lanes].astype(F32) * slope * scale
        grads[p][h, :, lanes] = grad.astype(BF16)
        mine = grads[p].at[h, :, lanes]
        for d in range(1, N_ZH):
            sent["g", d, u] = links.start(mine, mine, zh_group[d - 1])

    def gather_x(u):
        p, lanes = unit(u)
        for d in range(1, N_ZH):
            sent["g", d, u].wait_recv()
        mine = grads[p].at[pl.ds(x * N_ZH, N_ZH), :, lanes]
        sent["gr", u] = links.start(mine, mine, x_right)
        sent["gl", u] = links.start(mine, mine, x_left)

    def gather_far(u):
        p, lanes = unit(u)
        sent["gr", u].wait_recv()
        near = grads[p].at[pl.ds(x_down * N_ZH, N_ZH // 2), :, lanes]
        sent["hr", u] = links.start(near, near, x_right)
        sent["gl", u].wait_recv()
        near = grads[p].at[pl.ds(x_up * N_ZH + N_ZH // 2, N_ZH // 2), :, lanes]
        sent["hl", u] = links.start(near, near, x_left)

    def gather_end(u):
        sent["hr", u].wait_recv()
        sent["hl", u].wait_recv()

    end_rows = wide // END_CHUNKS
    end_half = end_rows // 2
    side_nodes = nodes // N_CORE
    mine_nodes = nodes // N_ROW
    y_nodes = mine_nodes * N_ZL

    def rows_of_unit(v, start=0, size=end_rows):
        return pl.ds(v * end_rows + start, size)

    def core_out(v):
        p, r = v // END_CHUNKS, v % END_CHUNKS
        there = pl.ds(pl.multiple_of((1 - core) * side_nodes, side_nodes), side_nodes)
        src = back_ref.at[p, pl.ds(r * end_rows, end_rows), there]
        sent["c", v] = links.start(src, core_ref.at[rows_of_unit(v), :], c_peer)

    def y_part(y_of, side, v):
        lanes = pl.ds(pl.multiple_of(y_of * y_nodes, y_nodes), y_nodes)
        return half_ref.at[rows_of_unit(v, side * end_half, end_half), lanes]

    def yslot(i, v):
        return yin_ref.at[i, pl.ds(v * end_half, end_half), :]

    def ymerged(i, v):
        return ymerge_ref.at[i, pl.ds(v * end_half, end_half), :]

    def y_out(v):
        p, r = v // END_CHUNKS, v % END_CHUNKS
        sent["c", v].wait_recv()
        step = min(side_nodes, 512)

        @pl.loop(0, side_nodes // step)
        def one(j):
            here = pl.ds(pl.multiple_of(j * step, step), step)
            there = pl.ds(pl.multiple_of(core * side_nodes + j * step, step), step)
            half_ref[rows_of_unit(v), here] = add(
                back_ref[p, pl.ds(r * end_rows, end_rows), there], core_ref[rows_of_unit(v), here]
            )

        sent["yf0", v] = links.start(y_part(y_far, 0, v), yslot(0, v), y_right)
        sent["yf1", v] = links.start(y_part(y_far, 1, v), yslot(1, v), y_left)
        sent["yd0", v] = links.start(y_part(y_up, 1, v), yslot(2, v), y_right)
        sent["yd1", v] = links.start(y_part(y_down, 0, v), yslot(3, v), y_left)

    def y_merge(v):
        sent["yf0", v].wait_recv()
        ymerged(0, v)[...] = add(yslot(0, v)[...], y_part(y_up, 0, v)[...])
        sent["ym0", v] = links.start(ymerged(0, v), yslot(4, v), y_right)
        sent["yf1", v].wait_recv()
        ymerged(1, v)[...] = add(yslot(1, v)[...], y_part(y_down, 1, v)[...])
        sent["ym1", v] = links.start(ymerged(1, v), yslot(5, v), y_left)

    def z_out(v):
        for name in ("yd0", "yd1", "ym0", "ym1"):
            sent[name, v].wait_recv()
        for side, (through, direct) in enumerate(((4, 3), (5, 2))):
            total = yslot(through, v)[...].astype(F32) + yslot(direct, v)[...].astype(F32)
            total = total + y_part(y, side, v)[...].astype(F32)
            ysum_ref[rows_of_unit(v, side * end_half, end_half), :] = total.astype(BF16)
        there = pl.ds(pl.multiple_of(zp * mine_nodes, mine_nodes), mine_nodes)
        sent["yz", v] = links.start(
            ysum_ref.at[rows_of_unit(v), there], zin_ref.at[rows_of_unit(v), :], z_peer
        )

    place = pl.ds(
        pl.multiple_of(core * side_nodes + (y * N_ZL + zl) * mine_nodes, mine_nodes), mine_nodes
    )

    def scaled(v):
        sent["yz", v].wait_recv()
        here = pl.ds(pl.multiple_of(zl * mine_nodes, mine_nodes), mine_nodes)
        value = ysum_ref[rows_of_unit(v), here].astype(F32) + zin_ref[rows_of_unit(v), :].astype(F32)
        gp_ref[rows_of_unit(v), :] = (value * cs_ref[:, place]).astype(BF16)

    def spread(name, src_of, dst):
        for d in range(1, N_ROW):
            sent[name, d] = links.start(src_of((g + d) % N_ROW), dst, row_group[d - 1])
        return src_of(g)

    def arrived(name):
        for d in range(1, N_ROW):
            sent[name, d].wait_recv()

    def spread_grad(p):
        def piece(owner):
            return gp_ref.at[pl.ds(pl.multiple_of(p * wide + owner * own, own), own), :]

        mine = spread(("gp", p), piece, gpa_ref.at[p, :, place])
        gpa_ref[p, :, place] = mine[...]

    def spread_features():
        gft_ref[...] = lax.dot_general(
            wt_ref[...], gp_ref[...], (((0,), (0,)), ((), ())), preferred_element_type=F32
        ).astype(BF16)

        def piece(owner):
            return gft_ref.at[pl.ds(pl.multiple_of(owner * depth, depth), depth), :]

        mine = spread("gf", piece, gf_ref.at[:, place])
        gf_ref[:, place] = mine[...]

    feats = w_hbm.shape[0]
    weight_total = {}

    def weight_part(p):
        arrived(("gp", p))
        total = jnp.zeros((own, feats), F32)
        step = min(nodes, 512)
        for j in range(nodes // step):
            where = pl.ds(j * step, step)
            total = total + lax.dot_general(
                gpa_ref[p, :, where],
                all_ref[:, :, where].reshape(feats, step),
                (((1,), (1,)), ((), ())),
                preferred_element_type=F32,
            )
        weight_total[p] = total
        share_out("px", p, 0, px_ref, x_group)

    def share_out(name, p, index, buffer, group):
        lw_ref[index, p] = weight_total[p].astype(BF16)
        for i, peer in enumerate(group):
            sent[name, p, i] = links.start(lw_ref.at[index, p], buffer.at[i, p], peer)

    def share_in(name, p, buffer, group):
        for i in range(len(group)):
            sent[name, p, i].wait_recv()
            weight_total[p] = weight_total[p] + buffer[i, p].astype(F32)

    def weight_x(p):
        share_in("px", p, px_ref, x_group)
        share_out("pz", p, 1, pz_ref, zh_group)

    def weight_end(p):
        share_in("pz", p, pz_ref, zh_group)
        gw_ref[pl.ds(p * own, own), :] = weight_total[p]

    ag_stages = (ag_own, ag_z, ag_y, ag_zy, ag_far, project)
    for step in range(AG_CHUNKS + len(ag_stages) - 1):
        for stage, act in enumerate(ag_stages):
            if 0 <= step - stage < AG_CHUNKS:
                act(step - stage)
        if step == 1:
            prepare()

    units = PARTS * MID_CHUNKS
    forward_tiles(0)
    for u in range(MID_CHUNKS):
        reduce_out(u)
    forward_tiles(1)
    mid_stages = (
        reduce_out, reduce_merge, reduce_z, activate, gather_x, gather_far, gather_end,
    )
    steps = units + len(mid_stages) - 1
    ready = MID_CHUNKS - 1 + len(mid_stages) - 1
    pieces = steps - 1 - ready
    for step in range(1, steps):
        for stage, act in enumerate(mid_stages):
            if 0 <= step - stage < units and not (stage == 0 and step < MID_CHUNKS):
                act(step - stage)
        if ready <= step < ready + pieces:
            share = TILE // pieces
            backward_tiles(0, (step - ready) * share, share)

    core_out(0)
    core_out(1)
    y_out(0)
    y_out(1)
    share = TILE // 4
    backward_tiles(1, 0, share)
    y_merge(0)
    backward_tiles(1, share, share)
    y_merge(1)
    backward_tiles(1, 2 * share, share)
    z_out(0)
    backward_tiles(1, 3 * share, share)
    core_out(2)
    core_out(3)
    z_out(1)
    scaled(0)
    y_out(2)
    y_out(3)
    scaled(1)
    spread_grad(0)
    y_merge(2)
    weight_part(0)
    y_merge(3)
    weight_x(0)
    z_out(2)
    weight_end(0)
    z_out(3)
    scaled(2)
    scaled(3)
    spread_grad(1)
    spread_features()
    weight_part(1)
    weight_x(1)
    weight_end(1)
    arrived("gf")
    links.drain()


def shards(features, weight, degrees, tile_values, tile_row, tile_col, tile_count, cotangent):
    nodes, depth = features.shape
    feats, hidden = weight.shape
    wide, own = hidden // PARTS, depth // PARTS
    mine = nodes // N_ROW
    x_half = own * N_ZH // 2
    end_half = wide // 2
    side, y_nodes = nodes // N_CORE, mine * N_ZL
    tiles = tile_values[0, 0]
    vmem = pl.BlockSpec(memory_space=pltpu.VMEM)
    smem = pl.BlockSpec(memory_space=pltpu.SMEM)
    anywhere = pl.BlockSpec(memory_space=pl.ANY)

    def buffer(*shape, dtype=BF16):
        return pltpu.VMEM(shape, dtype)

    table = pl.pallas_call(
        plan_kernel,
        out_shape=jax.ShapeDtypeStruct((16, TILE), I32),
        in_specs=[vmem, vmem, smem],
        out_specs=vmem,
        name="plan",
    )(tile_row[0], tile_col[0], tile_count)
    output, grad_features, grad_weight = pl.pallas_call(
        kernel,
        out_shape=(
            jax.ShapeDtypeStruct((depth, nodes), BF16),
            jax.ShapeDtypeStruct((depth, nodes), BF16),
            jax.ShapeDtypeStruct((depth, feats), F32),
        ),
        in_specs=[anywhere, anywhere, anywhere, anywhere, smem, vmem, anywhere],
        out_specs=(vmem, vmem, vmem),
        scratch_shapes=[
            buffer(N_ROW, depth, nodes),
            buffer(*tiles.shape),
            buffer(feats, hidden),
            buffer(hidden, feats),
            buffer(depth, nodes),
            buffer(2, nodes // TILE, TILE, dtype=I32),
            buffer(1, nodes, dtype=F32),
            buffer(1, nodes, dtype=F32),
            buffer(2, TILE, TILE, dtype=F32),
            buffer(2, TILE, TILE, dtype=F32),
            buffer(PARTS, wide, nodes),
            buffer(TILE, wide, TILE),
            buffer(wide, TILE, dtype=F32),
            buffer(PARTS, wide, nodes),
            buffer(6, PARTS, x_half, nodes),
            buffer(2, PARTS, x_half, nodes),
            buffer(PARTS, 2 * x_half, nodes),
            buffer(N_ZH - 1, PARTS, own, nodes),
            buffer(N_COL, own, nodes),
            buffer(N_COL, own, nodes),
            buffer(PARTS, wide, nodes),
            buffer(hidden, side),
            buffer(hidden, side),
            buffer(6, hidden // 2, y_nodes),
            buffer(2, hidden // 2, y_nodes),
            buffer(hidden, y_nodes),
            buffer(hidden, mine),
            buffer(hidden, mine),
            buffer(feats, mine),
            buffer(PARTS, own, nodes),
            buffer(2, PARTS, own, feats),
            buffer(N_X - 1, PARTS, own, feats),
            buffer(N_ZH - 1, PARTS, own, feats),
            pltpu.SemaphoreType.DMA((8,)),
            pltpu.SemaphoreType.DMA((SENDS,)),
            pltpu.SemaphoreType.DMA((SENDS,)),
        ],
        compiler_params=pltpu.CompilerParams(
            collective_id=0, has_side_effects=True, vmem_limit_bytes=VMEM_BYTES
        ),
        name="layer",
    )(
        features.T,
        weight,
        degrees.reshape(-1, TILE),
        tiles,
        table,
        table,
        cotangent.T,
    )
    return (output.T, grad_features.T, grad_weight.T)


def solution(mesh):
    in_specs = (
        P("col", "row"),
        P(),
        P(),
        P("row", "col", None, None, None),
        P("row", "col", None),
        P("row", "col", None),
        P("row", "col"),
        P("row", "col"),
    )
    out_specs = (P("row", "col"), P("col", "row"), P(None, "row"))
    return jax.shard_map(shards, mesh=mesh, in_specs=in_specs, out_specs=out_specs, check_vma=False)
```

```python
import jax
import jax.numpy as jnp
from jax import lax
from jax.experimental import pallas as pl
from jax.experimental.pallas import tpu as pltpu
from jax.sharding import PartitionSpec as P

TILE = 128
PARTS = 2
N_Y, N_ZL, N_CORE = 4, 2, 2
N_X, N_ZH = 4, 4
N_ROW, N_COL = N_Y * N_ZL * N_CORE, N_X * N_ZH
AG_CHUNKS = 4
MID_CHUNKS = 4
END_CHUNKS = 2
GROUP = 16
VMEM_BYTES = 60 * 1024 * 1024
BF16, F32, I32 = jnp.bfloat16, jnp.float32, jnp.int32
MESH = pl.DeviceIdType.MESH
SENDS = (
    AG_CHUNKS * 20
    + PARTS * MID_CHUNKS * 20
    + PARTS * END_CHUNKS * 8
    + (PARTS + 1) * (N_ROW - 1)
    + N_X - 1
    + N_ZH - 1
)


class Links:
    def __init__(self, send_sems, recv_sems):
        self.send_sems, self.recv_sems, self.used, self.open = send_sems, recv_sems, 0, []

    def start(self, src, dst, device):
        copy = pltpu.make_async_remote_copy(
            src_ref=src,
            dst_ref=dst,
            send_sem=self.send_sems.at[self.used],
            recv_sem=self.recv_sems.at[self.used],
            device_id=device,
            device_id_type=MESH,
        )
        self.used += 1
        copy.start()
        self.open.append(copy)
        return copy

    def drain(self):
        for copy in self.open:
            copy.wait_send()


def greet(peers):
    barrier = pltpu.get_barrier_semaphore()
    for peer in peers:
        pl.semaphore_signal(barrier, inc=1, device_id=peer, device_id_type=MESH)
    pl.semaphore_wait(barrier, len(peers))


def add(left, right):
    return (left.astype(F32) + right.astype(F32)).astype(BF16)


def sorted_by(key, gather):
    shape = (TILE, TILE)
    i = lax.broadcasted_iota(I32, shape, 0)
    j = lax.broadcasted_iota(I32, shape, 1)
    across = jnp.broadcast_to(key, shape)
    down = across.T
    before = (down < across) | ((down == across) & (i < j))
    rank = jnp.broadcast_to(jnp.sum(before.astype(I32), axis=0, keepdims=True), shape).T

    def total(where, value):
        return jnp.sum(jnp.where(where, value, 0), axis=0, keepdims=True)

    order = total(rank == j, i)
    source = total(rank == j, jnp.broadcast_to(gather, shape).T)
    same = (total(rank == j, down) == total(rank == j - 1, down)).astype(I32)
    last = jnp.maximum(total(down <= j, 1) - 1, 0)
    some = jnp.minimum(total(down == j, 1), 1)
    return [order, source, last, same, some]


def plan_kernel(rows_ref, cols_ref, count_ref, table_ref):
    live = lax.broadcasted_iota(I32, (1, TILE), 1) < count_ref[0, 0]
    rows_of, cols_of = rows_ref[...], cols_ref[...]
    lines = sorted_by(jnp.where(live, rows_of, TILE), cols_of)
    lines += sorted_by(jnp.where(live, cols_of, TILE), rows_of)
    table_ref[...] = jnp.zeros_like(table_ref)
    for i, line in enumerate(lines):
        table_ref[pl.ds(i, 1), :] = line


def kernel(
    x_hbm, w_hbm, deg_hbm, tiles_hbm, idx_ref, table_ref, cot_hbm,
    out_ref, gf_ref, gw_ref,
    all_ref, tiles_ref, w_ref, wt_ref, cot_ref, deg_ref, cs_ref, rs_ref, same_ref, some_ref,
    proj_ref, seg_ref, acc_ref, part_ref,
    in_ref, merge_ref, sum_ref, z_ref, zmerge_ref, g0_ref, g1_ref, back_ref,
    core_ref, half_ref, yin_ref, ymerge_ref, ysum_ref, zin_ref, gp_ref, gft_ref, gwt_ref, gwl_ref,
    lw_ref, px_ref, pz_ref, local_sems, send_sems, recv_sems,
):
    links = Links(send_sems, recv_sems)
    g, h = lax.axis_index("row"), lax.axis_index("col")
    y, zl, core = g // (N_ZL * N_CORE), (g // N_CORE) % N_ZL, g % N_CORE
    x, zh = h // N_ZH, h % N_ZH
    zp = 1 - zl

    def at(y_of, zl_of, core_of):
        return (y_of * N_ZL + zl_of) * N_CORE + core_of

    y_up, y_down, y_far = (y + 1) % N_Y, (y + N_Y - 1) % N_Y, (y + 2) % N_Y
    x_up, x_down, x_far = (x + 1) % N_X, (x + N_X - 1) % N_X, (x + 2) % N_X
    y_right, y_left = (at(y_up, zl, core), h), (at(y_down, zl, core), h)
    x_right, x_left = (g, x_up * N_ZH + zh), (g, x_down * N_ZH + zh)
    z_peer, c_peer = (at(y, zp, core), h), (at(y, zl, 1 - core), h)
    row_group = [((g + d) % N_ROW, h) for d in range(1, N_ROW)]
    x_group = [(g, ((x + d) % N_X) * N_ZH + zh) for d in range(1, N_X)]
    z_up, z_down, z_far = (zh + 1) % N_ZH, (zh + N_ZH - 1) % N_ZH, (zh + 2) % N_ZH
    z_right, z_left = (g, x * N_ZH + z_up), (g, x * N_ZH + z_down)
    zh_group = [(g, x * N_ZH + (zh + d) % N_ZH) for d in range(1, N_ZH)]

    nodes = x_hbm.shape[1]
    hidden = w_ref.shape[1]
    wide = hidden // PARTS
    depth = x_hbm.shape[0]
    own = depth // PARTS
    feats = w_hbm.shape[0]
    blocks = nodes // TILE
    deg_rows = nodes // TILE
    sent = {}

    local = {}
    loads = (
        ("x", x_hbm, all_ref.at[g]),
        ("w", w_hbm, w_ref),
        ("dc", deg_hbm.at[pl.ds(pl.multiple_of(h * deg_rows, deg_rows), deg_rows)], deg_ref.at[0]),
        ("dr", deg_hbm.at[pl.ds(pl.multiple_of(g * deg_rows, deg_rows), deg_rows)], deg_ref.at[1]),
        ("tiles", tiles_hbm, tiles_ref),
        ("cot", cot_hbm, cot_ref),
    )
    for i, (name, src, dst) in enumerate(loads):
        local[name] = pltpu.make_async_copy(src, dst, local_sems.at[i])
        local[name].start()

    greet(row_group + x_group + zh_group)

    ag_span = nodes // AG_CHUNKS
    first, second = pl.ds(0, depth // 2), pl.ds(depth // 2, depth // 2)

    def ag_lanes(q):
        return pl.ds(q * ag_span, ag_span)

    def forward(owner, q, device, rows=slice(None)):
        block = all_ref.at[owner, rows, ag_lanes(q)]
        return links.start(block, block, device)

    def ag_own(q):
        src = x_hbm.at[:, ag_lanes(q)]
        for name, device in (("z", z_peer), ("r", y_right), ("l", y_left), ("c0", c_peer)):
            sent[name, q] = links.start(src, all_ref.at[g, :, ag_lanes(q)], device)

    def ag_z(q):
        sent["z", q].wait_recv()
        owner = at(y, zp, core)
        sent["zr", q] = forward(owner, q, y_right, first)
        sent["zl", q] = forward(owner, q, y_left, first)
        sent["c1", q] = forward(owner, q, c_peer)

    def ag_y(q):
        sent["r", q].wait_recv()
        sent["fr", q] = forward(at(y_down, zl, core), q, y_right, first)
        sent["rz", q] = forward(at(y_down, zl, core), q, z_peer, second)
        sent["l", q].wait_recv()
        sent["fl", q] = forward(at(y_up, zl, core), q, y_left, second)
        sent["lz", q] = forward(at(y_up, zl, core), q, z_peer, second)
        sent["c2", q] = forward(at(y_down, zl, core), q, c_peer)
        sent["c3", q] = forward(at(y_up, zl, core), q, c_peer)

    def ag_far(q):
        sent["fl", q].wait_recv()
        sent["fz", q] = forward(at(y_far, zl, core), q, z_peer, second)
        sent["zr", q].wait_recv()
        lanes = pl.ds(q * ag_span, ag_span // 2)
        block = all_ref.at[at(y_down, zp, core), first, lanes]
        sent["gr", q] = links.start(block, block, y_right)
        sent["zl", q].wait_recv()
        lanes = pl.ds(q * ag_span + ag_span // 2, ag_span // 2)
        block = all_ref.at[at(y_up, zp, core), first, lanes]
        sent["gl", q] = links.start(block, block, y_left)
        sent["fr", q].wait_recv()
        sent["c4", q] = forward(at(y_far, zl, core), q, c_peer)

    def ag_last(q):
        sent["rz", q].wait_recv()
        sent["c5", q] = forward(at(y_down, zp, core), q, c_peer)
        sent["lz", q].wait_recv()
        sent["c6", q] = forward(at(y_up, zp, core), q, c_peer)
        for name in ("gr", "gl", "fz"):
            sent[name, q].wait_recv()
        sent["c7", q] = forward(at(y_far, zp, core), q, c_peer)

    def project(q):
        for i in range(8):
            sent["c%d" % i, q].wait_recv()
        if q == 0:
            local["x"].wait()
        step = min(ag_span, 256)

        @pl.loop(0, ag_span // step)
        def one(j):
            where = pl.ds(pl.multiple_of(q * ag_span + j * step, step), step)
            block = all_ref[:, :, where].reshape(-1, step)
            for p in range(PARTS):
                value = jnp.dot(
                    wt_ref[pl.ds(p * wide, wide), :], block, preferred_element_type=F32
                )
                proj_ref[p, :, where] = (value * cs_ref[:, where]).astype(BF16)

    def prepare():
        local["w"].wait()
        turned = w_ref[...].T
        for owner in range(N_COL):
            for p in range(PARTS):
                start = owner * depth + p * own
                wt_ref[pl.ds(p * wide + owner * own, own), :] = turned[start : start + own, :]
        local["dc"].wait()
        local["dr"].wait()
        for ref, i in ((cs_ref, 0), (rs_ref, 1)):
            scale = lax.rsqrt(deg_ref[i].astype(F32))
            for j in range(deg_rows):
                ref[:, pl.ds(j * TILE, TILE)] = scale[j : j + 1, :]
        for i in range(2):
            for ref, line in ((same_ref, 5 * i + 3), (some_ref, 5 * i + 4)):
                flags = table_ref[pl.ds(line, 1), :].astype(F32)
                ref[i] = jnp.broadcast_to(flags, (TILE, TILE)).T
        local["tiles"].wait()
        local["cot"].wait()

    def tiles_times(way, dense, contract, first_tile, tiles):
        @pl.loop(first_tile // GROUP, (first_tile + tiles) // GROUP)
        def step(i):
            products = []
            for j in range(GROUP):
                t = i * GROUP + j
                source = pl.ds(idx_ref[5 * way + 1, t] * TILE, TILE)
                products.append(
                    lax.dot_general(
                        dense(source),
                        tiles_ref[idx_ref[5 * way, t]],
                        contract,
                        preferred_element_type=F32,
                    )
                )
            total = acc_ref[...]
            for j in range(GROUP):
                t = i * GROUP + j
                total = total * same_ref[way, pl.ds(t, 1), :] + products[j]
                seg_ref[t] = total.astype(BF16)
            acc_ref[...] = total

    def clear():
        acc_ref[...] = jnp.zeros_like(acc_ref)

    def collect(way, ref, p):
        @pl.loop(0, blocks)
        def one(b):
            value = seg_ref[idx_ref[5 * way + 2, b]]
            where = pl.ds(pl.multiple_of(b * TILE, TILE), TILE)
            some = some_ref[way, pl.ds(b, 1), :]
            ref[p, :, where] = (value.astype(F32) * some).astype(BF16)

    by_row = (((1,), (1,)), ((), ()))
    by_col = (((1,), (0,)), ((), ()))
    grads = (g0_ref, g1_ref)

    def forward_tiles(p):
        clear()
        tiles_times(0, lambda source: proj_ref[p, :, source], by_row, 0, TILE)
        collect(0, part_ref, p)

    def backward_tiles(p, first_tile, tiles):
        if first_tile == 0:
            clear()
        tiles_times(
            1,
            lambda source: grads[p][:, :, source].reshape(wide, TILE),
            by_col,
            first_tile,
            tiles,
        )
        if first_tile + tiles == TILE:
            collect(1, back_ref, p)

    span = nodes // MID_CHUNKS
    x_rows = own * N_ZH
    x_half = x_rows // 2

    def unit(u):
        p, q = u // MID_CHUNKS, u % MID_CHUNKS
        return p, pl.ds(q * span, span)

    def part(x_of, side, u):
        p, lanes = unit(u)
        start = pl.multiple_of(x_of * x_rows + side * x_half, x_half)
        return part_ref.at[p, pl.ds(start, x_half), lanes]

    def slot(i, u):
        p, lanes = unit(u)
        return in_ref.at[i, p, :, lanes]

    def merged(i, u):
        p, lanes = unit(u)
        return merge_ref.at[i, p, :, lanes]

    def reduce_out(u):
        sent["f0", u] = links.start(part(x_far, 0, u), slot(0, u), x_right)
        sent["f1", u] = links.start(part(x_far, 1, u), slot(1, u), x_left)
        sent["d0", u] = links.start(part(x_up, 1, u), slot(2, u), x_right)
        sent["d1", u] = links.start(part(x_down, 0, u), slot(3, u), x_left)

    def reduce_merge(u):
        sent["f0", u].wait_recv()
        merged(0, u)[...] = add(slot(0, u)[...], part(x_up, 0, u)[...])
        sent["m0", u] = links.start(merged(0, u), slot(4, u), x_right)
        sent["f1", u].wait_recv()
        merged(1, u)[...] = add(slot(1, u)[...], part(x_down, 1, u)[...])
        sent["m1", u] = links.start(merged(1, u), slot(5, u), x_left)

    def reduce_z(u):
        p, lanes = unit(u)
        for name in ("d0", "d1", "m0", "m1"):
            sent[name, u].wait_recv()
        for side, (through, direct) in enumerate(((4, 3), (5, 2))):
            total = slot(through, u)[...].astype(F32) + slot(direct, u)[...].astype(F32)
            total = total + part(x, side, u)[...].astype(F32)
            sum_ref[p, pl.ds(side * x_half, x_half), lanes] = total.astype(BF16)
        sent["zf0", u] = links.start(z_part(z_far, 0, u), z_slot(0, u), z_right)
        sent["zf1", u] = links.start(z_part(z_far, 1, u), z_slot(1, u), z_left)
        sent["zd0", u] = links.start(z_part(z_up, 1, u), z_slot(2, u), z_right)
        sent["zd1", u] = links.start(z_part(z_down, 0, u), z_slot(3, u), z_left)

    def half_lanes(u, side):
        return pl.ds((u % MID_CHUNKS) * span + side * (span // 2), span // 2)

    def z_part(zh_of, side, u):
        rows = pl.ds(pl.multiple_of(zh_of * own, own), own)
        return sum_ref.at[u // MID_CHUNKS, rows, half_lanes(u, side)]

    def z_slot(i, u):
        return z_ref.at[i, u // MID_CHUNKS, :, pl.ds((u % MID_CHUNKS) * (span // 2), span // 2)]

    def z_merged(i, u):
        lanes = pl.ds((u % MID_CHUNKS) * (span // 2), span // 2)
        return zmerge_ref.at[i, u // MID_CHUNKS, :, lanes]

    def merge_z(u):
        sent["zf0", u].wait_recv()
        z_merged(0, u)[...] = add(z_slot(0, u)[...], z_part(z_up, 0, u)[...])
        sent["zm0", u] = links.start(z_merged(0, u), z_slot(4, u), z_right)
        sent["zf1", u].wait_recv()
        z_merged(1, u)[...] = add(z_slot(1, u)[...], z_part(z_down, 1, u)[...])
        sent["zm1", u] = links.start(z_merged(1, u), z_slot(5, u), z_left)

    def activate(u):
        p, lanes = unit(u)
        for name in ("zd0", "zd1", "zm0", "zm1"):
            sent[name, u].wait_recv()
        rows = pl.ds(p * own, own)
        for side, (through, direct) in enumerate(((4, 3), (5, 2))):
            here = half_lanes(u, side)
            value = z_slot(through, u)[...].astype(F32) + z_slot(direct, u)[...].astype(F32)
            value = value + z_part(zh, side, u)[...].astype(F32)
            scale = rs_ref[:, here]
            hidden_in = value * scale
            sigma = 1.0 / (1.0 + jnp.exp(-hidden_in))
            out_ref[rows, here] = (hidden_in * sigma).astype(BF16)
            slope = sigma * (1.0 + hidden_in * (1.0 - sigma))
            grad = cot_ref[rows, here].astype(F32) * slope * scale
            grads[p][h, :, here] = grad.astype(BF16)
        mine = grads[p].at[h, :, lanes]
        sent["ar", u] = links.start(mine, mine, z_right)
        sent["al", u] = links.start(mine, mine, z_left)

    def gather_z(u):
        p = u // MID_CHUNKS
        sent["ar", u].wait_recv()
        near = grads[p].at[x * N_ZH + z_down, :, half_lanes(u, 0)]
        sent["br", u] = links.start(near, near, z_right)
        sent["al", u].wait_recv()
        near = grads[p].at[x * N_ZH + z_up, :, half_lanes(u, 1)]
        sent["bl", u] = links.start(near, near, z_left)

    def gather_x(u):
        p, lanes = unit(u)
        sent["br", u].wait_recv()
        sent["bl", u].wait_recv()
        mine = grads[p].at[pl.ds(x * N_ZH, N_ZH), :, lanes]
        sent["gr", u] = links.start(mine, mine, x_right)
        sent["gl", u] = links.start(mine, mine, x_left)

    def gather_far(u):
        p, lanes = unit(u)
        sent["gr", u].wait_recv()
        near = grads[p].at[pl.ds(x_down * N_ZH, N_ZH // 2), :, lanes]
        sent["hr", u] = links.start(near, near, x_right)
        sent["gl", u].wait_recv()
        near = grads[p].at[pl.ds(x_up * N_ZH + N_ZH // 2, N_ZH // 2), :, lanes]
        sent["hl", u] = links.start(near, near, x_left)

    def gather_end(u):
        sent["hr", u].wait_recv()
        sent["hl", u].wait_recv()

    end_rows = wide // END_CHUNKS
    end_half = end_rows // 2
    side_nodes = nodes // N_CORE
    mine_nodes = nodes // N_ROW
    y_nodes = mine_nodes * N_ZL

    def rows_of_unit(v, start=0, size=end_rows):
        return pl.ds(v * end_rows + start, size)

    def core_out(v):
        p, r = v // END_CHUNKS, v % END_CHUNKS
        there = pl.ds(pl.multiple_of((1 - core) * side_nodes, side_nodes), side_nodes)
        src = back_ref.at[p, pl.ds(r * end_rows, end_rows), there]
        sent["c", v] = links.start(src, core_ref.at[rows_of_unit(v), :], c_peer)

    def y_part(y_of, side, v):
        lanes = pl.ds(pl.multiple_of(y_of * y_nodes, y_nodes), y_nodes)
        return half_ref.at[rows_of_unit(v, side * end_half, end_half), lanes]

    def yslot(i, v):
        return yin_ref.at[i, pl.ds(v * end_half, end_half), :]

    def ymerged(i, v):
        return ymerge_ref.at[i, pl.ds(v * end_half, end_half), :]

    def y_out(v):
        p, r = v // END_CHUNKS, v % END_CHUNKS
        sent["c", v].wait_recv()
        step = min(side_nodes, 512)

        @pl.loop(0, side_nodes // step)
        def one(j):
            here = pl.ds(pl.multiple_of(j * step, step), step)
            there = pl.ds(pl.multiple_of(core * side_nodes + j * step, step), step)
            half_ref[rows_of_unit(v), here] = add(
                back_ref[p, pl.ds(r * end_rows, end_rows), there], core_ref[rows_of_unit(v), here]
            )

        sent["yf0", v] = links.start(y_part(y_far, 0, v), yslot(0, v), y_right)
        sent["yf1", v] = links.start(y_part(y_far, 1, v), yslot(1, v), y_left)
        sent["yd0", v] = links.start(y_part(y_up, 1, v), yslot(2, v), y_right)
        sent["yd1", v] = links.start(y_part(y_down, 0, v), yslot(3, v), y_left)

    def y_merge(v):
        sent["yf0", v].wait_recv()
        ymerged(0, v)[...] = add(yslot(0, v)[...], y_part(y_up, 0, v)[...])
        sent["ym0", v] = links.start(ymerged(0, v), yslot(4, v), y_right)
        sent["yf1", v].wait_recv()
        ymerged(1, v)[...] = add(yslot(1, v)[...], y_part(y_down, 1, v)[...])
        sent["ym1", v] = links.start(ymerged(1, v), yslot(5, v), y_left)

    def z_out(v):
        for name in ("yd0", "yd1", "ym0", "ym1"):
            sent[name, v].wait_recv()
        for side, (through, direct) in enumerate(((4, 3), (5, 2))):
            total = yslot(through, v)[...].astype(F32) + yslot(direct, v)[...].astype(F32)
            total = total + y_part(y, side, v)[...].astype(F32)
            ysum_ref[rows_of_unit(v, side * end_half, end_half), :] = total.astype(BF16)
        there = pl.ds(pl.multiple_of(zp * mine_nodes, mine_nodes), mine_nodes)
        sent["yz", v] = links.start(
            ysum_ref.at[rows_of_unit(v), there], zin_ref.at[rows_of_unit(v), :], z_peer
        )

    place = pl.ds(
        pl.multiple_of(core * side_nodes + (y * N_ZL + zl) * mine_nodes, mine_nodes), mine_nodes
    )

    def scaled(v):
        sent["yz", v].wait_recv()
        here = pl.ds(pl.multiple_of(zl * mine_nodes, mine_nodes), mine_nodes)
        value = ysum_ref[rows_of_unit(v), here].astype(F32) + zin_ref[rows_of_unit(v), :].astype(F32)
        gp_ref[rows_of_unit(v), :] = (value * cs_ref[:, place]).astype(BF16)

    def spread(name, src_of, dst):
        for d in range(1, N_ROW):
            sent[name, d] = links.start(src_of((g + d) % N_ROW), dst, row_group[d - 1])
        return src_of(g)

    def arrived(name):
        for d in range(1, N_ROW):
            sent[name, d].wait_recv()

    def spread_weight(p):
        gwt_ref[p] = lax.dot_general(
            gp_ref[pl.ds(p * wide, wide), :],
            all_ref[:, :, place].reshape(feats, mine_nodes),
            (((1,), (1,)), ((), ())),
            preferred_element_type=F32,
        ).astype(BF16)

        def piece(owner):
            return gwt_ref.at[p, pl.ds(pl.multiple_of(owner * own, own), own), :]

        spread(("gw", p), piece, gwl_ref.at[p, g])

    def sum_weight(p):
        arrived(("gw", p))
        total = gwt_ref[p, pl.ds(pl.multiple_of(g * own, own), own), :].astype(F32)
        for d in range(1, N_ROW):
            total = total + gwl_ref[p, (g + d) % N_ROW].astype(F32)
        gw_ref[pl.ds(p * own, own), :] = total

    def feature_product():
        gft_ref[...] = lax.dot_general(
            wt_ref[...], gp_ref[...], (((0,), (0,)), ((), ())), preferred_element_type=F32
        ).astype(BF16)

    def spread_features():
        def piece(owner):
            return gft_ref.at[pl.ds(pl.multiple_of(owner * depth, depth), depth), :]

        mine = spread("gf", piece, gf_ref.at[:, place])
        gf_ref[:, place] = mine[...]

    def share_out(name, index, buffer, group):
        lw_ref[index] = gw_ref[...].astype(BF16)
        for i, peer in enumerate(group):
            sent[name, i] = links.start(lw_ref.at[index], buffer.at[i], peer)

    def share_in(name, buffer, group):
        total = gw_ref[...]
        for i in range(len(group)):
            sent[name, i].wait_recv()
            total = total + buffer[i].astype(F32)
        gw_ref[...] = total

    for q in range(AG_CHUNKS):
        ag_own(q)
    prepare()
    for q in range(AG_CHUNKS):
        ag_z(q)
        ag_y(q)
    ag_far(0)
    ag_far(1)
    ag_last(0)
    ag_far(2)
    ag_last(1)
    project(0)
    ag_far(3)
    ag_last(2)
    project(1)
    ag_last(3)
    project(2)
    project(3)

    units = PARTS * MID_CHUNKS
    share = TILE // 4
    forward_tiles(0)
    reduce_out(0)
    reduce_out(1)
    forward_tiles(1)
    mid_stages = (
        (0, reduce_merge), (-2, reduce_out), (1, reduce_z), (2, merge_z), (3, activate),
        (4, gather_z), (5, gather_x), (6, gather_far),
    )
    for step in range(units + 6):
        for lag, act in mid_stages:
            u = step - lag
            if 0 <= u < units and not (act is reduce_out and u < 2):
                act(u)
        if step == units + 2:
            for u in range(MID_CHUNKS):
                gather_end(u)
            backward_tiles(0, 0, share)
            backward_tiles(0, share, share)
        if step == units + 3:
            backward_tiles(0, 2 * share, share)
            backward_tiles(0, 3 * share, share)
            core_out(0)
            core_out(1)
        if step == units + 4:
            y_out(0)
            y_out(1)
    y_merge(0)
    for u in range(MID_CHUNKS, units):
        gather_end(u)
    backward_tiles(1, 0, share)
    y_merge(1)
    backward_tiles(1, share, share)
    z_out(0)
    backward_tiles(1, 2 * share, share)
    z_out(1)
    backward_tiles(1, 3 * share, share)
    core_out(2)
    core_out(3)
    scaled(0)
    scaled(1)
    y_out(2)
    y_out(3)
    y_merge(2)
    y_merge(3)
    spread_weight(0)
    z_out(2)
    z_out(3)
    scaled(2)
    scaled(3)
    spread_weight(1)
    sum_weight(0)
    feature_product()
    sum_weight(1)
    share_out("px", 0, px_ref, x_group)
    spread_features()
    share_in("px", px_ref, x_group)
    share_out("pz", 1, pz_ref, zh_group)
    share_in("pz", pz_ref, zh_group)
    arrived("gf")
    links.drain()


def write_kernel(*refs):
    count = len(refs) // 2
    for i in range(count):
        refs[count + i][...] = refs[i][...]


def shards(features, weight, degrees, tile_values, tile_row, tile_col, tile_count, cotangent):
    nodes, depth = features.shape
    feats, hidden = weight.shape
    wide, own = hidden // PARTS, depth // PARTS
    mine = nodes // N_ROW
    x_half = own * N_ZH // 2
    end_half = wide // 2
    side, y_nodes = nodes // N_CORE, mine * N_ZL
    tiles = tile_values[0, 0]
    vmem = pl.BlockSpec(memory_space=pltpu.VMEM)
    smem = pl.BlockSpec(memory_space=pltpu.SMEM)
    anywhere = pl.BlockSpec(memory_space=pl.ANY)

    def buffer(*shape, dtype=BF16):
        return pltpu.VMEM(shape, dtype)

    table = pl.pallas_call(
        plan_kernel,
        out_shape=jax.ShapeDtypeStruct((16, TILE), I32),
        in_specs=[vmem, vmem, smem],
        out_specs=vmem,
        name="plan",
    )(tile_row[0], tile_col[0], tile_count)
    results = pl.pallas_call(
        kernel,
        out_shape=(
            jax.ShapeDtypeStruct((depth, nodes), BF16),
            jax.ShapeDtypeStruct((depth, nodes), BF16),
            jax.ShapeDtypeStruct((depth, feats), F32),
        ),
        in_specs=[anywhere, anywhere, anywhere, anywhere, smem, vmem, anywhere],
        out_specs=(vmem, vmem, vmem),
        scratch_shapes=[
            buffer(N_ROW, depth, nodes),
            buffer(*tiles.shape),
            buffer(feats, hidden),
            buffer(hidden, feats),
            buffer(depth, nodes),
            buffer(2, nodes // TILE, TILE, dtype=I32),
            buffer(1, nodes, dtype=F32),
            buffer(1, nodes, dtype=F32),
            buffer(2, TILE, TILE, dtype=F32),
            buffer(2, TILE, TILE, dtype=F32),
            buffer(PARTS, wide, nodes),
            buffer(TILE, wide, TILE),
            buffer(wide, TILE, dtype=F32),
            buffer(PARTS, wide, nodes),
            buffer(6, PARTS, x_half, nodes),
            buffer(2, PARTS, x_half, nodes),
            buffer(PARTS, 2 * x_half, nodes),
            buffer(6, PARTS, own, nodes // 2),
            buffer(2, PARTS, own, nodes // 2),
            buffer(N_COL, own, nodes),
            buffer(N_COL, own, nodes),
            buffer(PARTS, wide, nodes),
            buffer(hidden, side),
            buffer(hidden, side),
            buffer(6, hidden // 2, y_nodes),
            buffer(2, hidden // 2, y_nodes),
            buffer(hidden, y_nodes),
            buffer(hidden, mine),
            buffer(hidden, mine),
            buffer(feats, mine),
            buffer(PARTS, wide, feats),
            buffer(PARTS, N_ROW, own, feats),
            buffer(2, depth, feats),
            buffer(N_X - 1, depth, feats),
            buffer(N_ZH - 1, depth, feats),
            pltpu.SemaphoreType.DMA((8,)),
            pltpu.SemaphoreType.DMA((SENDS,)),
            pltpu.SemaphoreType.DMA((SENDS,)),
        ],
        compiler_params=pltpu.CompilerParams(
            collective_id=0, has_side_effects=True, vmem_limit_bytes=VMEM_BYTES
        ),
        name="layer",
    )(
        features.T,
        weight,
        degrees.reshape(-1, TILE),
        tiles,
        table,
        table,
        cotangent.T,
    )
    output, grad_features, grad_weight = pl.pallas_call(
        write_kernel,
        out_shape=tuple(jax.ShapeDtypeStruct(r.shape, r.dtype) for r in results),
        in_specs=[vmem] * len(results),
        out_specs=(vmem,) * len(results),
        name="write",
    )(*results)
    return (output.T, grad_features.T, grad_weight.T)


def solution(mesh):
    in_specs = (
        P("col", "row"),
        P(),
        P(),
        P("row", "col", None, None, None),
        P("row", "col", None),
        P("row", "col", None),
        P("row", "col"),
        P("row", "col"),
    )
    out_specs = (P("row", "col"), P("col", "row"), P(None, "row"))
    return jax.shard_map(shards, mesh=mesh, in_specs=in_specs, out_specs=out_specs, check_vma=False)
```

```python
import jax
import jax.numpy as jnp
from jax import lax
from jax.experimental import pallas as pl
from jax.experimental.pallas import tpu as pltpu
from jax.sharding import PartitionSpec as P

TILE = 128
PARTS = 2
N_Y, N_ZL, N_CORE = 4, 2, 2
N_X, N_ZH = 4, 4
N_ROW, N_COL = N_Y * N_ZL * N_CORE, N_X * N_ZH
AG_CHUNKS = 4
MID_CHUNKS = 4
END_CHUNKS = 2
Z_FIRST = (4,)
GROUP = 16
VMEM_BYTES = 60 * 1024 * 1024
BF16, F32, I32 = jnp.bfloat16, jnp.float32, jnp.int32
MESH = pl.DeviceIdType.MESH
SENDS = (
    AG_CHUNKS * 20
    + PARTS * MID_CHUNKS * 20
    + PARTS * END_CHUNKS * 8
    + (PARTS + 1) * (N_ROW - 1)
    + PARTS * (N_X - 1 + N_ZH - 1)
)


class Links:
    def __init__(self, send_sems, recv_sems):
        self.send_sems, self.recv_sems, self.used, self.open = send_sems, recv_sems, 0, []

    def start(self, src, dst, device):
        copy = pltpu.make_async_remote_copy(
            src_ref=src,
            dst_ref=dst,
            send_sem=self.send_sems.at[self.used],
            recv_sem=self.recv_sems.at[self.used],
            device_id=device,
            device_id_type=MESH,
        )
        self.used += 1
        copy.start()
        self.open.append(copy)
        return copy

    def drain(self):
        for copy in self.open:
            copy.wait_send()


def greet(peers):
    barrier = pltpu.get_barrier_semaphore()
    for peer in peers:
        pl.semaphore_signal(barrier, inc=1, device_id=peer, device_id_type=MESH)
    pl.semaphore_wait(barrier, len(peers))


def add(left, right):
    return (left.astype(F32) + right.astype(F32)).astype(BF16)


def sorted_by(key, gather):
    shape = (TILE, TILE)
    i = lax.broadcasted_iota(I32, shape, 0)
    j = lax.broadcasted_iota(I32, shape, 1)
    across = jnp.broadcast_to(key, shape)
    down = across.T
    before = (down < across) | ((down == across) & (i < j))
    rank = jnp.broadcast_to(jnp.sum(before.astype(I32), axis=0, keepdims=True), shape).T

    def total(where, value):
        return jnp.sum(jnp.where(where, value, 0), axis=0, keepdims=True)

    order = total(rank == j, i)
    source = total(rank == j, jnp.broadcast_to(gather, shape).T)
    same = (total(rank == j, down) == total(rank == j - 1, down)).astype(I32)
    last = jnp.maximum(total(down <= j, 1) - 1, 0)
    some = jnp.minimum(total(down == j, 1), 1)
    return [order, source, last, same, some]


def plan_kernel(rows_ref, cols_ref, count_ref, table_ref):
    live = lax.broadcasted_iota(I32, (1, TILE), 1) < count_ref[0, 0]
    rows_of, cols_of = rows_ref[...], cols_ref[...]
    lines = sorted_by(jnp.where(live, rows_of, TILE), cols_of)
    lines += sorted_by(jnp.where(live, cols_of, TILE), rows_of)
    table_ref[...] = jnp.zeros_like(table_ref)
    for i, line in enumerate(lines):
        table_ref[pl.ds(i, 1), :] = line


def kernel(
    x_hbm, w_hbm, deg_hbm, tiles_hbm, idx_ref, table_ref, cot_hbm,
    out_ref, gf_ref, gw_ref,
    all_ref, tiles_ref, w_ref, wt_ref, cot_ref, deg_ref, cs_ref, rs_ref, same_ref, some_ref,
    proj_ref, seg_ref, acc_ref, part_ref,
    in_ref, merge_ref, sum_ref, z_ref, zmerge_ref, g0_ref, g1_ref, back_ref,
    core_ref, half_ref, yin_ref, ymerge_ref, ysum_ref, zin_ref, gp_ref, gft_ref, gwt_ref, gwl_ref,
    lw_ref, px_ref, pz_ref, local_sems, send_sems, recv_sems,
):
    links = Links(send_sems, recv_sems)
    g, h = lax.axis_index("row"), lax.axis_index("col")
    y, zl, core = g // (N_ZL * N_CORE), (g // N_CORE) % N_ZL, g % N_CORE
    x, zh = h // N_ZH, h % N_ZH
    zp = 1 - zl

    def at(y_of, zl_of, core_of):
        return (y_of * N_ZL + zl_of) * N_CORE + core_of

    y_up, y_down, y_far = (y + 1) % N_Y, (y + N_Y - 1) % N_Y, (y + 2) % N_Y
    x_up, x_down, x_far = (x + 1) % N_X, (x + N_X - 1) % N_X, (x + 2) % N_X
    y_right, y_left = (at(y_up, zl, core), h), (at(y_down, zl, core), h)
    x_right, x_left = (g, x_up * N_ZH + zh), (g, x_down * N_ZH + zh)
    z_peer, c_peer = (at(y, zp, core), h), (at(y, zl, 1 - core), h)
    row_group = [((g + d) % N_ROW, h) for d in range(1, N_ROW)]
    x_group = [(g, ((x + d) % N_X) * N_ZH + zh) for d in range(1, N_X)]
    z_up, z_down, z_far = (zh + 1) % N_ZH, (zh + N_ZH - 1) % N_ZH, (zh + 2) % N_ZH
    z_right, z_left = (g, x * N_ZH + z_up), (g, x * N_ZH + z_down)
    zh_group = [(g, x * N_ZH + (zh + d) % N_ZH) for d in range(1, N_ZH)]

    nodes = x_hbm.shape[1]
    hidden = w_ref.shape[1]
    wide = hidden // PARTS
    depth = x_hbm.shape[0]
    own = depth // PARTS
    feats = w_hbm.shape[0]
    blocks = nodes // TILE
    deg_rows = nodes // TILE
    sent = {}

    local = {}
    loads = (
        ("x", x_hbm, all_ref.at[g]),
        ("w", w_hbm, w_ref),
        ("dc", deg_hbm.at[pl.ds(pl.multiple_of(h * deg_rows, deg_rows), deg_rows)], deg_ref.at[0]),
        ("dr", deg_hbm.at[pl.ds(pl.multiple_of(g * deg_rows, deg_rows), deg_rows)], deg_ref.at[1]),
        ("tiles", tiles_hbm, tiles_ref),
        ("cot", cot_hbm, cot_ref),
    )
    for i, (name, src, dst) in enumerate(loads):
        local[name] = pltpu.make_async_copy(src, dst, local_sems.at[i])
        local[name].start()

    greet(row_group + x_group + zh_group)

    ag_span = nodes // AG_CHUNKS
    first, second = pl.ds(0, depth // 2), pl.ds(depth // 2, depth // 2)

    def ag_lanes(q):
        return pl.ds(q * ag_span, ag_span)

    def forward(owner, q, device, rows=slice(None)):
        block = all_ref.at[owner, rows, ag_lanes(q)]
        return links.start(block, block, device)

    def ag_own(q):
        src = x_hbm.at[:, ag_lanes(q)]
        for name, device in (("z", z_peer), ("r", y_right), ("l", y_left), ("c0", c_peer)):
            sent[name, q] = links.start(src, all_ref.at[g, :, ag_lanes(q)], device)

    def ag_z(q):
        sent["z", q].wait_recv()
        owner = at(y, zp, core)
        sent["zr", q] = forward(owner, q, y_right, first)
        sent["zl", q] = forward(owner, q, y_left, first)
        sent["c1", q] = forward(owner, q, c_peer)

    def ag_y(q):
        sent["r", q].wait_recv()
        sent["fr", q] = forward(at(y_down, zl, core), q, y_right, first)
        sent["rz", q] = forward(at(y_down, zl, core), q, z_peer, second)
        sent["l", q].wait_recv()
        sent["fl", q] = forward(at(y_up, zl, core), q, y_left, second)
        sent["lz", q] = forward(at(y_up, zl, core), q, z_peer, second)
        sent["c2", q] = forward(at(y_down, zl, core), q, c_peer)
        sent["c3", q] = forward(at(y_up, zl, core), q, c_peer)

    def ag_far(q):
        sent["fl", q].wait_recv()
        sent["fz", q] = forward(at(y_far, zl, core), q, z_peer, second)
        sent["zr", q].wait_recv()
        lanes = pl.ds(q * ag_span, ag_span // 2)
        block = all_ref.at[at(y_down, zp, core), first, lanes]
        sent["gr", q] = links.start(block, block, y_right)
        sent["zl", q].wait_recv()
        lanes = pl.ds(q * ag_span + ag_span // 2, ag_span // 2)
        block = all_ref.at[at(y_up, zp, core), first, lanes]
        sent["gl", q] = links.start(block, block, y_left)
        sent["fr", q].wait_recv()
        sent["c4", q] = forward(at(y_far, zl, core), q, c_peer)

    def ag_last(q):
        sent["rz", q].wait_recv()
        sent["c5", q] = forward(at(y_down, zp, core), q, c_peer)
        sent["lz", q].wait_recv()
        sent["c6", q] = forward(at(y_up, zp, core), q, c_peer)
        for name in ("gr", "gl", "fz"):
            sent[name, q].wait_recv()
        sent["c7", q] = forward(at(y_far, zp, core), q, c_peer)

    def project(q):
        for i in range(8):
            sent["c%d" % i, q].wait_recv()
        if q == 0:
            local["x"].wait()
        step = min(ag_span, 512)

        @pl.loop(0, ag_span // step)
        def one(j):
            where = pl.ds(pl.multiple_of(q * ag_span + j * step, step), step)
            block = all_ref[:, :, where].reshape(-1, step)
            value = jnp.dot(wt_ref[...], block, preferred_element_type=F32)
            value = (value * cs_ref[:, where]).astype(BF16)
            for p in range(PARTS):
                proj_ref[p, :, where] = value[p * wide : (p + 1) * wide, :]

    def prepare():
        local["w"].wait()
        turned = w_ref[...].T
        for owner in range(N_COL):
            for p in range(PARTS):
                start = owner * depth + p * own
                wt_ref[pl.ds(p * wide + owner * own, own), :] = turned[start : start + own, :]
        local["dc"].wait()
        local["dr"].wait()
        for ref, i in ((cs_ref, 0), (rs_ref, 1)):
            scale = lax.rsqrt(deg_ref[i].astype(F32))
            for j in range(deg_rows):
                ref[:, pl.ds(j * TILE, TILE)] = scale[j : j + 1, :]
        for i in range(2):
            for ref, line in ((same_ref, 5 * i + 3), (some_ref, 5 * i + 4)):
                flags = table_ref[pl.ds(line, 1), :].astype(F32)
                ref[i] = jnp.broadcast_to(flags, (TILE, TILE)).T
        local["tiles"].wait()
        local["cot"].wait()

    def tiles_times(way, dense, contract, first_tile, tiles):
        @pl.loop(first_tile // GROUP, (first_tile + tiles) // GROUP)
        def step(i):
            products = []
            for j in range(GROUP):
                t = i * GROUP + j
                source = pl.ds(idx_ref[5 * way + 1, t] * TILE, TILE)
                products.append(
                    lax.dot_general(
                        dense(source),
                        tiles_ref[idx_ref[5 * way, t]],
                        contract,
                        preferred_element_type=F32,
                    )
                )
            total = acc_ref[...]
            for j in range(GROUP):
                t = i * GROUP + j
                total = total * same_ref[way, pl.ds(t, 1), :] + products[j]
                seg_ref[t] = total.astype(BF16)
            acc_ref[...] = total

    def clear():
        acc_ref[...] = jnp.zeros_like(acc_ref)

    def collect(way, ref, p):
        @pl.loop(0, blocks)
        def one(b):
            value = seg_ref[idx_ref[5 * way + 2, b]]
            where = pl.ds(pl.multiple_of(b * TILE, TILE), TILE)
            some = some_ref[way, pl.ds(b, 1), :]
            value = (value.astype(F32) * some).astype(BF16)
            if len(ref.shape) == 3:
                ref[p, :, where] = value
            else:
                ref[p, :, :, :, where] = value.reshape(N_X, N_ZH, own, TILE)

    by_row = (((1,), (1,)), ((), ()))
    by_col = (((1,), (0,)), ((), ()))
    grads = (g0_ref, g1_ref)

    def forward_tiles(p):
        clear()
        tiles_times(0, lambda source: proj_ref[p, :, source], by_row, 0, TILE)
        collect(0, part_ref, p)

    def backward_tiles(p, first_tile, tiles):
        if first_tile == 0:
            clear()
        tiles_times(
            1,
            lambda source: grads[p][:, :, :, source].reshape(wide, TILE),
            by_col,
            first_tile,
            tiles,
        )
        if first_tile + tiles == TILE:
            collect(1, back_ref, p)

    span = nodes // MID_CHUNKS
    pair = N_X // 2
    ring = {
        "x": (x, x_up, x_down, x_far, x_right, x_left),
        "z": (zh, z_up, z_down, z_far, z_right, z_left),
    }

    def axes(u):
        return ("z", "x") if u in Z_FIRST else ("x", "z")

    def unit(u):
        p, q = u // MID_CHUNKS, u % MID_CHUNKS
        return p, pl.ds(q * span, span)

    def half_lanes(u, side):
        return pl.ds((u % MID_CHUNKS) * span + side * (span // 2), span // 2)

    def grid(ref, axis, along, across, lanes):
        if axis == "x":
            return ref.at[along, across, :, lanes]
        return ref.at[across, along, :, lanes]

    def part(coord, side, u):
        p, lanes = unit(u)
        return grid(part_ref.at[p], axes(u)[0], coord, pl.ds(side * pair, pair), lanes)

    def slot(i, u):
        p, lanes = unit(u)
        return in_ref.at[i, p, :, :, lanes]

    def merged(i, u):
        p, lanes = unit(u)
        return merge_ref.at[i, p, :, :, lanes]

    def reduce_out(u):
        me, up, down, far, right, left = ring[axes(u)[0]]
        sent["f0", u] = links.start(part(far, 0, u), slot(0, u), right)
        sent["f1", u] = links.start(part(far, 1, u), slot(1, u), left)
        sent["d0", u] = links.start(part(up, 1, u), slot(2, u), right)
        sent["d1", u] = links.start(part(down, 0, u), slot(3, u), left)

    def reduce_merge(u):
        me, up, down, far, right, left = ring[axes(u)[0]]
        sent["f0", u].wait_recv()
        merged(0, u)[...] = add(slot(0, u)[...], part(up, 0, u)[...])
        sent["m0", u] = links.start(merged(0, u), slot(4, u), right)
        sent["f1", u].wait_recv()
        merged(1, u)[...] = add(slot(1, u)[...], part(down, 1, u)[...])
        sent["m1", u] = links.start(merged(1, u), slot(5, u), left)

    def second_part(coord, side, u):
        return sum_ref.at[u // MID_CHUNKS, coord, :, half_lanes(u, side)]

    def second_slot(i, u):
        return z_ref.at[i, u // MID_CHUNKS, :, pl.ds((u % MID_CHUNKS) * (span // 2), span // 2)]

    def second_merged(i, u):
        lanes = pl.ds((u % MID_CHUNKS) * (span // 2), span // 2)
        return zmerge_ref.at[i, u // MID_CHUNKS, :, lanes]

    def reduce_second(u):
        p, lanes = unit(u)
        me = ring[axes(u)[0]][0]
        for name in ("d0", "d1", "m0", "m1"):
            sent[name, u].wait_recv()
        for side, (through, direct) in enumerate(((4, 3), (5, 2))):
            total = slot(through, u)[...].astype(F32) + slot(direct, u)[...].astype(F32)
            total = total + part(me, side, u)[...].astype(F32)
            sum_ref[p, pl.ds(side * pair, pair), :, lanes] = total.astype(BF16)
        me, up, down, far, right, left = ring[axes(u)[1]]
        sent["zf0", u] = links.start(second_part(far, 0, u), second_slot(0, u), right)
        sent["zf1", u] = links.start(second_part(far, 1, u), second_slot(1, u), left)
        sent["zd0", u] = links.start(second_part(up, 1, u), second_slot(2, u), right)
        sent["zd1", u] = links.start(second_part(down, 0, u), second_slot(3, u), left)

    def merge_second(u):
        me, up, down, far, right, left = ring[axes(u)[1]]
        sent["zf0", u].wait_recv()
        second_merged(0, u)[...] = add(second_slot(0, u)[...], second_part(up, 0, u)[...])
        sent["zm0", u] = links.start(second_merged(0, u), second_slot(4, u), right)
        sent["zf1", u].wait_recv()
        second_merged(1, u)[...] = add(second_slot(1, u)[...], second_part(down, 1, u)[...])
        sent["zm1", u] = links.start(second_merged(1, u), second_slot(5, u), left)

    def activate(u):
        p, lanes = unit(u)
        me, up, down, far, right, left = ring[axes(u)[1]]
        for name in ("zd0", "zd1", "zm0", "zm1"):
            sent[name, u].wait_recv()
        rows = pl.ds(p * own, own)
        for side, (through, direct) in enumerate(((4, 3), (5, 2))):
            here = half_lanes(u, side)
            value = second_slot(through, u)[...].astype(F32)
            value = value + second_slot(direct, u)[...].astype(F32)
            value = value + second_part(me, side, u)[...].astype(F32)
            scale = rs_ref[:, here]
            hidden_in = value * scale
            sigma = 1.0 / (1.0 + jnp.exp(-hidden_in))
            out_ref[rows, here] = (hidden_in * sigma).astype(BF16)
            slope = sigma * (1.0 + hidden_in * (1.0 - sigma))
            grad = cot_ref[rows, here].astype(F32) * slope * scale
            grads[p][x, zh, :, here] = grad.astype(BF16)
        mine = grads[p].at[x, zh, :, lanes]
        sent["ar", u] = links.start(mine, mine, right)
        sent["al", u] = links.start(mine, mine, left)

    def gather_second(u):
        first_axis, axis = axes(u)
        me, up, down, far, right, left = ring[axis]
        across, ref = ring[first_axis][0], grads[u // MID_CHUNKS]
        sent["ar", u].wait_recv()
        near = grid(ref, axis, down, across, half_lanes(u, 0))
        sent["br", u] = links.start(near, near, right)
        sent["al", u].wait_recv()
        near = grid(ref, axis, up, across, half_lanes(u, 1))
        sent["bl", u] = links.start(near, near, left)

    def gather_first(u):
        p, lanes = unit(u)
        axis = axes(u)[0]
        me, up, down, far, right, left = ring[axis]
        sent["br", u].wait_recv()
        sent["bl", u].wait_recv()
        mine = grid(grads[p], axis, me, slice(None), lanes)
        sent["gr", u] = links.start(mine, mine, right)
        sent["gl", u] = links.start(mine, mine, left)

    def gather_far(u):
        p, lanes = unit(u)
        axis = axes(u)[0]
        me, up, down, far, right, left = ring[axis]
        sent["gr", u].wait_recv()
        near = grid(grads[p], axis, down, pl.ds(0, pair), lanes)
        sent["hr", u] = links.start(near, near, right)
        sent["gl", u].wait_recv()
        near = grid(grads[p], axis, up, pl.ds(pair, pair), lanes)
        sent["hl", u] = links.start(near, near, left)

    def gather_end(u):
        sent["hr", u].wait_recv()
        sent["hl", u].wait_recv()

    end_rows = wide // END_CHUNKS
    end_half = end_rows // 2
    side_nodes = nodes // N_CORE
    mine_nodes = nodes // N_ROW
    y_nodes = mine_nodes * N_ZL

    def rows_of_unit(v, start=0, size=end_rows):
        return pl.ds(v * end_rows + start, size)

    def core_out(v):
        p, r = v // END_CHUNKS, v % END_CHUNKS
        there = pl.ds(pl.multiple_of((1 - core) * side_nodes, side_nodes), side_nodes)
        src = back_ref.at[p, pl.ds(r * end_rows, end_rows), there]
        sent["c", v] = links.start(src, core_ref.at[rows_of_unit(v), :], c_peer)

    def y_part(y_of, side, v):
        lanes = pl.ds(pl.multiple_of(y_of * y_nodes, y_nodes), y_nodes)
        return half_ref.at[rows_of_unit(v, side * end_half, end_half), lanes]

    def yslot(i, v):
        return yin_ref.at[i, pl.ds(v * end_half, end_half), :]

    def ymerged(i, v):
        return ymerge_ref.at[i, pl.ds(v * end_half, end_half), :]

    def y_out(v):
        p, r = v // END_CHUNKS, v % END_CHUNKS
        sent["c", v].wait_recv()
        step = min(side_nodes, 512)

        @pl.loop(0, side_nodes // step)
        def one(j):
            here = pl.ds(pl.multiple_of(j * step, step), step)
            there = pl.ds(pl.multiple_of(core * side_nodes + j * step, step), step)
            half_ref[rows_of_unit(v), here] = add(
                back_ref[p, pl.ds(r * end_rows, end_rows), there], core_ref[rows_of_unit(v), here]
            )

        sent["yf0", v] = links.start(y_part(y_far, 0, v), yslot(0, v), y_right)
        sent["yf1", v] = links.start(y_part(y_far, 1, v), yslot(1, v), y_left)
        sent["yd0", v] = links.start(y_part(y_up, 1, v), yslot(2, v), y_right)
        sent["yd1", v] = links.start(y_part(y_down, 0, v), yslot(3, v), y_left)

    def y_merge(v):
        sent["yf0", v].wait_recv()
        ymerged(0, v)[...] = add(yslot(0, v)[...], y_part(y_up, 0, v)[...])
        sent["ym0", v] = links.start(ymerged(0, v), yslot(4, v), y_right)
        sent["yf1", v].wait_recv()
        ymerged(1, v)[...] = add(yslot(1, v)[...], y_part(y_down, 1, v)[...])
        sent["ym1", v] = links.start(ymerged(1, v), yslot(5, v), y_left)

    def z_out(v):
        for name in ("yd0", "yd1", "ym0", "ym1"):
            sent[name, v].wait_recv()
        for side, (through, direct) in enumerate(((4, 3), (5, 2))):
            total = yslot(through, v)[...].astype(F32) + yslot(direct, v)[...].astype(F32)
            total = total + y_part(y, side, v)[...].astype(F32)
            ysum_ref[rows_of_unit(v, side * end_half, end_half), :] = total.astype(BF16)
        there = pl.ds(pl.multiple_of(zp * mine_nodes, mine_nodes), mine_nodes)
        sent["yz", v] = links.start(
            ysum_ref.at[rows_of_unit(v), there], zin_ref.at[rows_of_unit(v), :], z_peer
        )

    place = pl.ds(
        pl.multiple_of(core * side_nodes + (y * N_ZL + zl) * mine_nodes, mine_nodes), mine_nodes
    )

    def scaled(v):
        sent["yz", v].wait_recv()
        here = pl.ds(pl.multiple_of(zl * mine_nodes, mine_nodes), mine_nodes)
        value = ysum_ref[rows_of_unit(v), here].astype(F32) + zin_ref[rows_of_unit(v), :].astype(F32)
        gp_ref[rows_of_unit(v), :] = (value * cs_ref[:, place]).astype(BF16)

    def spread(name, src_of, dst):
        for d in range(1, N_ROW):
            sent[name, d] = links.start(src_of((g + d) % N_ROW), dst, row_group[d - 1])
        return src_of(g)

    def arrived(name):
        for d in range(1, N_ROW):
            sent[name, d].wait_recv()

    def spread_weight(p):
        gwt_ref[p] = lax.dot_general(
            gp_ref[pl.ds(p * wide, wide), :],
            all_ref[:, :, place].reshape(feats, mine_nodes),
            (((1,), (1,)), ((), ())),
            preferred_element_type=F32,
        ).astype(BF16)

        def piece(owner):
            return gwt_ref.at[p, pl.ds(pl.multiple_of(owner * own, own), own), :]

        spread(("gw", p), piece, gwl_ref.at[p, g])

    def sum_weight(p):
        arrived(("gw", p))
        total = gwt_ref[p, pl.ds(pl.multiple_of(g * own, own), own), :].astype(F32)
        for d in range(1, N_ROW):
            total = total + gwl_ref[p, (g + d) % N_ROW].astype(F32)
        gw_ref[pl.ds(p * own, own), :] = total

    def feature_product():
        gft_ref[...] = lax.dot_general(
            wt_ref[...], gp_ref[...], (((0,), (0,)), ((), ())), preferred_element_type=F32
        ).astype(BF16)

    def spread_features():
        def piece(owner):
            return gft_ref.at[pl.ds(pl.multiple_of(owner * depth, depth), depth), :]

        mine = spread("gf", piece, gf_ref.at[:, place])
        gf_ref[:, place] = mine[...]

    def share_out(name, p, buffer, group):
        sums = lw_ref.at[0 if name == "px" else 1, p]
        sums[...] = gw_ref[pl.ds(p * own, own), :].astype(BF16)
        for i, peer in enumerate(group):
            sent[name, p, i] = links.start(sums, buffer.at[i, p], peer)

    def share_in(name, p, buffer, group):
        total = gw_ref[pl.ds(p * own, own), :]
        for i in range(len(group)):
            sent[name, p, i].wait_recv()
            total = total + buffer[i, p].astype(F32)
        gw_ref[pl.ds(p * own, own), :] = total

    for q in range(AG_CHUNKS):
        ag_own(q)
    prepare()
    for q in range(AG_CHUNKS):
        ag_z(q)
        ag_y(q)
    ag_far(0)
    ag_far(1)
    ag_last(0)
    ag_far(2)
    ag_far(3)
    ag_last(1)
    project(0)
    ag_last(2)
    project(1)
    ag_last(3)
    project(2)
    project(3)

    units = PARTS * MID_CHUNKS
    share = TILE // 4
    forward_tiles(0)
    reduce_out(0)
    reduce_out(1)
    forward_tiles(1)
    x_lags = (
        (0, reduce_merge), (-2, reduce_out), (1, reduce_second), (2, merge_second),
        (3, activate), (4, gather_second), (5, gather_first), (6, gather_far),
    )
    z_lags = (
        (0, reduce_out), (2, reduce_merge), (3, reduce_second), (4, merge_second),
        (6, activate), (7, gather_second), (8, gather_first), (10, gather_far),
    )
    x_first = [u for u in range(units) if u not in Z_FIRST]
    steps = len(x_first) + 6
    for step in range(steps):
        for lag, act in x_lags:
            if max(0, -lag) <= step - lag < len(x_first):
                act(x_first[step - lag])
        for lag, act in z_lags:
            for u in Z_FIRST:
                if step == lag:
                    act(u)
        if step == steps - 4:
            for u in range(MID_CHUNKS):
                gather_end(u)
            backward_tiles(0, 0, 2 * share)
        if step == steps - 3:
            backward_tiles(0, 2 * share, 2 * share)
            core_out(0)
            core_out(1)
        if step == steps - 2:
            y_out(0)
            y_out(1)
    for u in range(MID_CHUNKS, units):
        gather_end(u)
    backward_tiles(1, 0, share)
    y_merge(0)
    backward_tiles(1, share, share)
    y_merge(1)
    backward_tiles(1, 2 * share, 2 * share)
    core_out(2)
    core_out(3)
    z_out(0)
    z_out(1)
    y_out(2)
    y_out(3)
    scaled(0)
    scaled(1)
    y_merge(2)
    y_merge(3)
    spread_weight(0)
    z_out(2)
    z_out(3)
    sum_weight(0)
    share_out("px", 0, px_ref, x_group)
    scaled(2)
    scaled(3)
    spread_weight(1)
    share_in("px", 0, px_ref, x_group)
    share_out("pz", 0, pz_ref, zh_group)
    feature_product()
    sum_weight(1)
    share_out("px", 1, px_ref, x_group)
    spread_features()
    share_in("pz", 0, pz_ref, zh_group)
    share_in("px", 1, px_ref, x_group)
    share_out("pz", 1, pz_ref, zh_group)
    share_in("pz", 1, pz_ref, zh_group)
    arrived("gf")
    links.drain()


def write_kernel(*refs):
    count = len(refs) // 2
    for i in range(count):
        refs[count + i][...] = refs[i][...]


def shards(features, weight, degrees, tile_values, tile_row, tile_col, tile_count, cotangent):
    nodes, depth = features.shape
    feats, hidden = weight.shape
    wide, own = hidden // PARTS, depth // PARTS
    mine = nodes // N_ROW
    side, y_nodes = nodes // N_CORE, mine * N_ZL
    tiles = tile_values[0, 0]
    vmem = pl.BlockSpec(memory_space=pltpu.VMEM)
    smem = pl.BlockSpec(memory_space=pltpu.SMEM)
    anywhere = pl.BlockSpec(memory_space=pl.ANY)

    def buffer(*shape, dtype=BF16):
        return pltpu.VMEM(shape, dtype)

    table = pl.pallas_call(
        plan_kernel,
        out_shape=jax.ShapeDtypeStruct((16, TILE), I32),
        in_specs=[vmem, vmem, smem],
        out_specs=vmem,
        name="plan",
    )(tile_row[0], tile_col[0], tile_count)
    results = pl.pallas_call(
        kernel,
        out_shape=(
            jax.ShapeDtypeStruct((depth, nodes), BF16),
            jax.ShapeDtypeStruct((depth, nodes), BF16),
            jax.ShapeDtypeStruct((depth, feats), F32),
        ),
        in_specs=[anywhere, anywhere, anywhere, anywhere, smem, vmem, anywhere],
        out_specs=(vmem, vmem, vmem),
        scratch_shapes=[
            buffer(N_ROW, depth, nodes),
            buffer(*tiles.shape),
            buffer(feats, hidden),
            buffer(hidden, feats),
            buffer(depth, nodes),
            buffer(2, nodes // TILE, TILE, dtype=I32),
            buffer(1, nodes, dtype=F32),
            buffer(1, nodes, dtype=F32),
            buffer(2, TILE, TILE, dtype=F32),
            buffer(2, TILE, TILE, dtype=F32),
            buffer(PARTS, wide, nodes),
            buffer(TILE, wide, TILE),
            buffer(wide, TILE, dtype=F32),
            buffer(PARTS, N_X, N_ZH, own, nodes),
            buffer(6, PARTS, N_X // 2, own, nodes),
            buffer(2, PARTS, N_X // 2, own, nodes),
            buffer(PARTS, N_X, own, nodes),
            buffer(6, PARTS, own, nodes // 2),
            buffer(2, PARTS, own, nodes // 2),
            buffer(N_X, N_ZH, own, nodes),
            buffer(N_X, N_ZH, own, nodes),
            buffer(PARTS, wide, nodes),
            buffer(hidden, side),
            buffer(hidden, side),
            buffer(6, hidden // 2, y_nodes),
            buffer(2, hidden // 2, y_nodes),
            buffer(hidden, y_nodes),
            buffer(hidden, mine),
            buffer(hidden, mine),
            buffer(feats, mine),
            buffer(PARTS, wide, feats),
            buffer(PARTS, N_ROW, own, feats),
            buffer(2, PARTS, own, feats),
            buffer(N_X - 1, PARTS, own, feats),
            buffer(N_ZH - 1, PARTS, own, feats),
            pltpu.SemaphoreType.DMA((8,)),
            pltpu.SemaphoreType.DMA((SENDS,)),
            pltpu.SemaphoreType.DMA((SENDS,)),
        ],
        compiler_params=pltpu.CompilerParams(
            collective_id=0, has_side_effects=True, vmem_limit_bytes=VMEM_BYTES
        ),
        name="layer",
    )(
        features.T,
        weight,
        degrees.reshape(-1, TILE),
        tiles,
        table,
        table,
        cotangent.T,
    )
    output, grad_features, grad_weight = pl.pallas_call(
        write_kernel,
        out_shape=tuple(jax.ShapeDtypeStruct(r.shape, r.dtype) for r in results),
        in_specs=[vmem] * len(results),
        out_specs=(vmem,) * len(results),
        name="write",
    )(*results)
    return (output.T, grad_features.T, grad_weight.T)


def solution(mesh):
    in_specs = (
        P("col", "row"),
        P(),
        P(),
        P("row", "col", None, None, None),
        P("row", "col", None),
        P("row", "col", None),
        P("row", "col"),
        P("row", "col"),
    )
    out_specs = (P("row", "col"), P("col", "row"), P(None, "row"))
    return jax.shard_map(shards, mesh=mesh, in_specs=in_specs, out_specs=out_specs, check_vma=False)
```

```python
import jax
import jax.numpy as jnp
from jax import lax
from jax.experimental import pallas as pl
from jax.experimental.pallas import tpu as pltpu
from jax.sharding import PartitionSpec as P

TILE = 128
PARTS = 2
N_Y, N_ZL, N_CORE = 4, 2, 2
N_X, N_ZH = 4, 4
N_ROW, N_COL = N_Y * N_ZL * N_CORE, N_X * N_ZH
AG_CHUNKS = 4
MID_CHUNKS = 4
END_CHUNKS = 2
Z_FIRST = (4,)
GROUP = 32
VMEM_BYTES = 60 * 1024 * 1024
BF16, F32, I32 = jnp.bfloat16, jnp.float32, jnp.int32
MESH = pl.DeviceIdType.MESH
SENDS = 64
RECEIVES = AG_CHUNKS * 13 + PARTS * MID_CHUNKS * 8 + PARTS * END_CHUNKS * 4 + PARTS * 3 + 1


class Links:
    def __init__(self, send_sems, recv_sems):
        self.send_sems, self.recv_sems, self.copies, self.groups, self.used = (
            send_sems, recv_sems, [], {}, 0
        )

    def start(self, src, dst, device, group=None):
        count = len(self.copies)
        if count >= SENDS:
            self.copies[count - SENDS].wait_send()
        place = self.groups.get(group)
        if place is None:
            place, self.used = self.used, self.used + 1
            if group is not None:
                self.groups[group] = place
        copy = pltpu.make_async_remote_copy(
            src_ref=src,
            dst_ref=dst,
            send_sem=self.send_sems.at[count % SENDS],
            recv_sem=self.recv_sems.at[place],
            device_id=device,
            device_id_type=MESH,
        )
        copy.start()
        self.copies.append(copy)
        return copy

    def wait(self, group, like):
        pltpu.make_async_copy(like, like, self.recv_sems.at[self.groups[group]]).wait()

    def drain(self):
        for copy in self.copies[-SENDS:]:
            copy.wait_send()


def greet(peers):
    barrier = pltpu.get_barrier_semaphore()
    for peer in peers:
        pl.semaphore_signal(barrier, inc=1, device_id=peer, device_id_type=MESH)
    pl.semaphore_wait(barrier, len(peers))


def add(left, right):
    return (left.astype(F32) + right.astype(F32)).astype(BF16)


def sorted_by(key, gather):
    shape = (TILE, TILE)
    i = lax.broadcasted_iota(I32, shape, 0)
    j = lax.broadcasted_iota(I32, shape, 1)
    across = jnp.broadcast_to(key, shape)
    down = across.T
    before = (down < across) | ((down == across) & (i < j))
    rank = jnp.broadcast_to(jnp.sum(before.astype(I32), axis=0, keepdims=True), shape).T

    def total(where, value):
        return jnp.sum(jnp.where(where, value, 0), axis=0, keepdims=True)

    order = total(rank == j, i)
    source = total(rank == j, jnp.broadcast_to(gather, shape).T)
    same = (total(rank == j, down) == total(rank == j - 1, down)).astype(I32)
    last = jnp.maximum(total(down <= j, 1) - 1, 0)
    some = jnp.minimum(total(down == j, 1), 1)
    return [order, source, last, same, some]


def plan_kernel(rows_ref, cols_ref, count_ref, table_ref):
    live = lax.broadcasted_iota(I32, (1, TILE), 1) < count_ref[0, 0]
    rows_of, cols_of = rows_ref[...], cols_ref[...]
    lines = sorted_by(jnp.where(live, rows_of, TILE), cols_of)
    lines += sorted_by(jnp.where(live, cols_of, TILE), rows_of)
    table_ref[...] = jnp.zeros_like(table_ref)
    for i, line in enumerate(lines):
        table_ref[pl.ds(i, 1), :] = line


def kernel(
    x_hbm, w_hbm, deg_hbm, tiles_hbm, idx_ref, table_ref, cot_hbm,
    out_ref, gf_ref, gw_ref,
    all_ref, tiles_ref, w_ref, wt_ref, cot_ref, deg_ref, cs_ref, rs_ref, same_ref, some_ref,
    proj_ref, seg_ref, acc_ref, part_ref,
    in_ref, merge_ref, sum_ref, z_ref, zmerge_ref, g0_ref, g1_ref, back_ref,
    core_ref, half_ref, yin_ref, ymerge_ref, ysum_ref, zin_ref, gp_ref, gft_ref, gwt_ref, gwl_ref,
    lw_ref, px_ref, pz_ref, local_sems, send_sems, recv_sems,
):
    links = Links(send_sems, recv_sems)
    g, h = lax.axis_index("row"), lax.axis_index("col")
    y, zl, core = g // (N_ZL * N_CORE), (g // N_CORE) % N_ZL, g % N_CORE
    x, zh = h // N_ZH, h % N_ZH
    zp = 1 - zl

    def at(y_of, zl_of, core_of):
        return (y_of * N_ZL + zl_of) * N_CORE + core_of

    y_up, y_down, y_far = (y + 1) % N_Y, (y + N_Y - 1) % N_Y, (y + 2) % N_Y
    x_up, x_down, x_far = (x + 1) % N_X, (x + N_X - 1) % N_X, (x + 2) % N_X
    y_right, y_left = (at(y_up, zl, core), h), (at(y_down, zl, core), h)
    x_right, x_left = (g, x_up * N_ZH + zh), (g, x_down * N_ZH + zh)
    z_peer, c_peer = (at(y, zp, core), h), (at(y, zl, 1 - core), h)
    row_group = [((g + d) % N_ROW, h) for d in range(1, N_ROW)]
    x_group = [(g, ((x + d) % N_X) * N_ZH + zh) for d in range(1, N_X)]
    z_up, z_down, z_far = (zh + 1) % N_ZH, (zh + N_ZH - 1) % N_ZH, (zh + 2) % N_ZH
    z_right, z_left = (g, x * N_ZH + z_up), (g, x * N_ZH + z_down)
    zh_group = [(g, x * N_ZH + (zh + d) % N_ZH) for d in range(1, N_ZH)]

    nodes = x_hbm.shape[1]
    hidden = w_ref.shape[1]
    wide = hidden // PARTS
    depth = x_hbm.shape[0]
    own = depth // PARTS
    feats = w_hbm.shape[0]
    blocks = nodes // TILE
    deg_rows = nodes // TILE
    sent = {}

    local = {}
    loads = (
        ("x", x_hbm, all_ref.at[g]),
        ("w", w_hbm, w_ref),
        ("dc", deg_hbm.at[pl.ds(pl.multiple_of(h * deg_rows, deg_rows), deg_rows)], deg_ref.at[0]),
        ("dr", deg_hbm.at[pl.ds(pl.multiple_of(g * deg_rows, deg_rows), deg_rows)], deg_ref.at[1]),
        ("tiles", tiles_hbm, tiles_ref),
        ("cot", cot_hbm, cot_ref),
    )
    for i, (name, src, dst) in enumerate(loads):
        local[name] = pltpu.make_async_copy(src, dst, local_sems.at[i])
        local[name].start()

    greet(row_group + x_group + zh_group)

    ag_span = nodes // AG_CHUNKS
    first, second = pl.ds(0, depth // 2), pl.ds(depth // 2, depth // 2)

    def ag_lanes(q):
        return pl.ds(q * ag_span, ag_span)

    def forward(owner, q, device, rows=slice(None), group=None):
        block = all_ref.at[owner, rows, ag_lanes(q)]
        return links.start(block, block, device, group)

    def ag_own(q):
        src = x_hbm.at[:, ag_lanes(q)]
        for name, device in (("z", z_peer), ("r", y_right), ("l", y_left)):
            sent[name, q] = links.start(src, all_ref.at[g, :, ag_lanes(q)], device)
        links.start(src, all_ref.at[g, :, ag_lanes(q)], c_peer, ("core", q))

    def ag_z(q):
        sent["z", q].wait_recv()
        owner = at(y, zp, core)
        sent["zr", q] = forward(owner, q, y_right, first)
        sent["zl", q] = forward(owner, q, y_left, first)
        forward(owner, q, c_peer, group=("core", q))

    def ag_y(q):
        sent["r", q].wait_recv()
        sent["fr", q] = forward(at(y_down, zl, core), q, y_right, first)
        sent["rz", q] = forward(at(y_down, zl, core), q, z_peer, second)
        sent["l", q].wait_recv()
        sent["fl", q] = forward(at(y_up, zl, core), q, y_left, second)
        sent["lz", q] = forward(at(y_up, zl, core), q, z_peer, second)
        forward(at(y_down, zl, core), q, c_peer, group=("core", q))
        forward(at(y_up, zl, core), q, c_peer, group=("core", q))

    def ag_far(q):
        sent["fl", q].wait_recv()
        sent["fz", q] = forward(at(y_far, zl, core), q, z_peer, second)
        sent["zr", q].wait_recv()
        lanes = pl.ds(q * ag_span, ag_span // 2)
        block = all_ref.at[at(y_down, zp, core), first, lanes]
        sent["gr", q] = links.start(block, block, y_right)
        sent["zl", q].wait_recv()
        lanes = pl.ds(q * ag_span + ag_span // 2, ag_span // 2)
        block = all_ref.at[at(y_up, zp, core), first, lanes]
        sent["gl", q] = links.start(block, block, y_left)
        sent["fr", q].wait_recv()
        forward(at(y_far, zl, core), q, c_peer, group=("core", q))

    def ag_last(q):
        sent["rz", q].wait_recv()
        forward(at(y_down, zp, core), q, c_peer, group=("core", q))
        sent["lz", q].wait_recv()
        forward(at(y_up, zp, core), q, c_peer, group=("core", q))
        for name in ("gr", "gl", "fz"):
            sent[name, q].wait_recv()
        forward(at(y_far, zp, core), q, c_peer, group=("core", q))

    def project(q):
        links.wait(("core", q), all_ref.at[pl.ds(0, N_Y * N_ZL), :, ag_lanes(q)])
        if q == 0:
            local["x"].wait()
        step = min(ag_span, 512)

        @pl.loop(0, ag_span // step)
        def one(j):
            where = pl.ds(pl.multiple_of(q * ag_span + j * step, step), step)
            block = all_ref[:, :, where].reshape(-1, step)
            value = jnp.dot(wt_ref[...], block, preferred_element_type=F32)
            value = (value * cs_ref[:, where]).astype(BF16)
            for p in range(PARTS):
                proj_ref[p, :, where] = value[p * wide : (p + 1) * wide, :]

    def prepare():
        local["w"].wait()
        turned = w_ref[...].T
        for owner in range(N_COL):
            for p in range(PARTS):
                start = owner * depth + p * own
                wt_ref[pl.ds(p * wide + owner * own, own), :] = turned[start : start + own, :]
        local["dc"].wait()
        local["dr"].wait()
        for ref, i in ((cs_ref, 0), (rs_ref, 1)):
            scale = lax.rsqrt(deg_ref[i].astype(F32))
            for j in range(deg_rows):
                ref[:, pl.ds(j * TILE, TILE)] = scale[j : j + 1, :]
        for i in range(2):
            for ref, line in ((same_ref, 5 * i + 3), (some_ref, 5 * i + 4)):
                flags = table_ref[pl.ds(line, 1), :].astype(F32)
                ref[i] = jnp.broadcast_to(flags, (TILE, TILE)).T
        local["tiles"].wait()
        local["cot"].wait()

    def tiles_times(way, dense, contract, first_tile, tiles):
        @pl.loop(first_tile // GROUP, (first_tile + tiles) // GROUP)
        def step(i):
            products = []
            for j in range(GROUP):
                t = i * GROUP + j
                source = pl.ds(idx_ref[5 * way + 1, t] * TILE, TILE)
                products.append(
                    lax.dot_general(
                        dense(source),
                        tiles_ref[idx_ref[5 * way, t]],
                        contract,
                        preferred_element_type=F32,
                    )
                )
            total = acc_ref[...]
            for j in range(GROUP):
                t = i * GROUP + j
                total = total * same_ref[way, pl.ds(t, 1), :] + products[j]
                seg_ref[t] = total.astype(BF16)
            acc_ref[...] = total

    def clear():
        acc_ref[...] = jnp.zeros_like(acc_ref)

    def collect(way, ref, p):
        @pl.loop(0, blocks)
        def one(b):
            value = seg_ref[idx_ref[5 * way + 2, b]]
            where = pl.ds(pl.multiple_of(b * TILE, TILE), TILE)
            some = some_ref[way, pl.ds(b, 1), :]
            value = (value.astype(F32) * some).astype(BF16)
            if len(ref.shape) == 3:
                ref[p, :, where] = value
            else:
                ref[p, :, :, :, where] = value.reshape(N_X, N_ZH, own, TILE)

    by_row = (((1,), (1,)), ((), ()))
    by_col = (((1,), (0,)), ((), ()))
    grads = (g0_ref, g1_ref)

    def forward_tiles(p):
        clear()
        tiles_times(0, lambda source: proj_ref[p, :, source], by_row, 0, TILE)
        collect(0, part_ref, p)

    def backward_tiles(p, first_tile, tiles):
        if first_tile == 0:
            clear()
        tiles_times(
            1,
            lambda source: grads[p][:, :, :, source].reshape(wide, TILE),
            by_col,
            first_tile,
            tiles,
        )
        if first_tile + tiles == TILE:
            collect(1, back_ref, p)

    span = nodes // MID_CHUNKS
    pair = N_X // 2
    ring = {
        "x": (x, x_up, x_down, x_far, x_right, x_left),
        "z": (zh, z_up, z_down, z_far, z_right, z_left),
    }

    def axes(u):
        return ("z", "x") if u in Z_FIRST else ("x", "z")

    def unit(u):
        p, q = u // MID_CHUNKS, u % MID_CHUNKS
        return p, pl.ds(q * span, span)

    def half_lanes(u, side):
        return pl.ds((u % MID_CHUNKS) * span + side * (span // 2), span // 2)

    def grid(ref, axis, along, across, lanes):
        if axis == "x":
            return ref.at[along, across, :, lanes]
        return ref.at[across, along, :, lanes]

    def part(coord, side, u):
        p, lanes = unit(u)
        return grid(part_ref.at[p], axes(u)[0], coord, pl.ds(side * pair, pair), lanes)

    def slot(i, u):
        p, lanes = unit(u)
        return in_ref.at[i, p, :, :, lanes]

    def merged(i, u):
        p, lanes = unit(u)
        return merge_ref.at[i, p, :, :, lanes]

    def reduce_out(u):
        me, up, down, far, right, left = ring[axes(u)[0]]
        links.start(part(far, 0, u), slot(0, u), right, ("f", u))
        links.start(part(far, 1, u), slot(1, u), left, ("f", u))
        links.start(part(up, 1, u), slot(2, u), right, ("d", u))
        links.start(part(down, 0, u), slot(3, u), left, ("d", u))

    def reduce_merge(u):
        me, up, down, far, right, left = ring[axes(u)[0]]
        p, lanes = unit(u)
        links.wait(("f", u), in_ref.at[pl.ds(0, 2), p, :, :, lanes])
        merged(0, u)[...] = add(slot(0, u)[...], part(up, 0, u)[...])
        links.start(merged(0, u), slot(4, u), right, ("d", u))
        merged(1, u)[...] = add(slot(1, u)[...], part(down, 1, u)[...])
        links.start(merged(1, u), slot(5, u), left, ("d", u))

    def second_part(coord, side, u):
        return sum_ref.at[u // MID_CHUNKS, coord, :, half_lanes(u, side)]

    def second_slots(i, count, u):
        lanes = pl.ds((u % MID_CHUNKS) * (span // 2), span // 2)
        return z_ref.at[pl.ds(i, count), u // MID_CHUNKS, :, lanes]

    def second_slot(i, u):
        return z_ref.at[i, u // MID_CHUNKS, :, pl.ds((u % MID_CHUNKS) * (span // 2), span // 2)]

    def second_merged(i, u):
        lanes = pl.ds((u % MID_CHUNKS) * (span // 2), span // 2)
        return zmerge_ref.at[i, u // MID_CHUNKS, :, lanes]

    def reduce_second(u):
        p, lanes = unit(u)
        me = ring[axes(u)[0]][0]
        links.wait(("d", u), in_ref.at[pl.ds(0, 4), p, :, :, lanes])
        for side, (through, direct) in enumerate(((4, 3), (5, 2))):
            total = slot(through, u)[...].astype(F32) + slot(direct, u)[...].astype(F32)
            total = total + part(me, side, u)[...].astype(F32)
            sum_ref[p, pl.ds(side * pair, pair), :, lanes] = total.astype(BF16)
        me, up, down, far, right, left = ring[axes(u)[1]]
        links.start(second_part(far, 0, u), second_slot(0, u), right, ("zf", u))
        links.start(second_part(far, 1, u), second_slot(1, u), left, ("zf", u))
        links.start(second_part(up, 1, u), second_slot(2, u), right, ("zd", u))
        links.start(second_part(down, 0, u), second_slot(3, u), left, ("zd", u))

    def merge_second(u):
        me, up, down, far, right, left = ring[axes(u)[1]]
        links.wait(("zf", u), second_slots(0, 2, u))
        second_merged(0, u)[...] = add(second_slot(0, u)[...], second_part(up, 0, u)[...])
        links.start(second_merged(0, u), second_slot(4, u), right, ("zd", u))
        second_merged(1, u)[...] = add(second_slot(1, u)[...], second_part(down, 1, u)[...])
        links.start(second_merged(1, u), second_slot(5, u), left, ("zd", u))

    def activate(u):
        p, lanes = unit(u)
        me, up, down, far, right, left = ring[axes(u)[1]]
        links.wait(("zd", u), second_slots(0, 4, u))
        rows = pl.ds(p * own, own)
        for side, (through, direct) in enumerate(((4, 3), (5, 2))):
            here = half_lanes(u, side)
            value = second_slot(through, u)[...].astype(F32)
            value = value + second_slot(direct, u)[...].astype(F32)
            value = value + second_part(me, side, u)[...].astype(F32)
            scale = rs_ref[:, here]
            hidden_in = value * scale
            sigma = 1.0 / (1.0 + jnp.exp(-hidden_in))
            out_ref[rows, here] = (hidden_in * sigma).astype(BF16)
            slope = sigma * (1.0 + hidden_in * (1.0 - sigma))
            grad = cot_ref[rows, here].astype(F32) * slope * scale
            grads[p][x, zh, :, here] = grad.astype(BF16)
        mine = grads[p].at[x, zh, :, lanes]
        links.start(mine, mine, right, ("a", u))
        links.start(mine, mine, left, ("a", u))

    def gather_second(u):
        first_axis, axis = axes(u)
        me, up, down, far, right, left = ring[axis]
        across, ref = ring[first_axis][0], grads[u // MID_CHUNKS]
        lanes = unit(u)[1]
        links.wait(("a", u), ref.at[0, pl.ds(0, 2), :, lanes])
        near = grid(ref, axis, down, across, half_lanes(u, 0))
        links.start(near, near, right, ("b", u))
        near = grid(ref, axis, up, across, half_lanes(u, 1))
        links.start(near, near, left, ("b", u))

    def gather_first(u):
        p, lanes = unit(u)
        axis = axes(u)[0]
        me, up, down, far, right, left = ring[axis]
        links.wait(("b", u), grads[p].at[0, 0, :, lanes])
        mine = grid(grads[p], axis, me, slice(None), lanes)
        links.start(mine, mine, right, ("g", u))
        links.start(mine, mine, left, ("g", u))

    def gather_far(u):
        p, lanes = unit(u)
        axis = axes(u)[0]
        me, up, down, far, right, left = ring[axis]
        links.wait(("g", u), grads[p].at[pl.ds(0, 2), :, :, lanes])
        near = grid(grads[p], axis, down, pl.ds(0, pair), lanes)
        links.start(near, near, right, ("h", u))
        near = grid(grads[p], axis, up, pl.ds(pair, pair), lanes)
        links.start(near, near, left, ("h", u))

    def gather_end(u):
        p, lanes = unit(u)
        links.wait(("h", u), grads[p].at[0, :, :, lanes])

    end_rows = wide // END_CHUNKS
    end_half = end_rows // 2
    side_nodes = nodes // N_CORE
    mine_nodes = nodes // N_ROW

    def rows_of_unit(v, start=0, size=end_rows):
        return pl.ds(v * end_rows + start, size)

    def core_out(v):
        p, r = v // END_CHUNKS, v % END_CHUNKS
        there = pl.ds(pl.multiple_of((1 - core) * side_nodes, side_nodes), side_nodes)
        src = back_ref.at[p, pl.ds(r * end_rows, end_rows), there]
        sent["c", v] = links.start(src, core_ref.at[rows_of_unit(v), :], c_peer)

    def core_sum(v):
        p, r = v // END_CHUNKS, v % END_CHUNKS
        sent["c", v].wait_recv()
        for j in range(N_Y * N_ZL):
            here = pl.ds(j * mine_nodes, mine_nodes)
            there = pl.ds(
                pl.multiple_of(core * side_nodes + j * mine_nodes, mine_nodes), mine_nodes
            )
            half_ref[j // N_ZL, j % N_ZL, rows_of_unit(v), :] = add(
                back_ref[p, pl.ds(r * end_rows, end_rows), there], core_ref[rows_of_unit(v), here]
            )

    def y_part(y_of, side, v):
        rows = rows_of_unit(v, side * end_half, end_half)
        if v % 2:
            return ysum_ref.at[pl.ds(y_of, 1), rows, :]
        return half_ref.at[y_of, :, rows, :]

    def y_buffer(ref, i, v):
        rows = pl.ds(v * end_half, end_half)
        return ref.at[i, pl.ds(0, 1) if v % 2 else slice(None), rows, :]

    def yslots(count, v):
        return y_buffer(yin_ref, pl.ds(0, count), v)

    def yslot(i, v):
        return y_buffer(yin_ref, i, v)

    def ymerged(i, v):
        return y_buffer(ymerge_ref, i, v)

    def y_send(v):
        links.start(y_part(y_far, 0, v), yslot(0, v), y_right, ("yf", v))
        links.start(y_part(y_far, 1, v), yslot(1, v), y_left, ("yf", v))
        links.start(y_part(y_up, 1, v), yslot(2, v), y_right, ("yd", v))
        links.start(y_part(y_down, 0, v), yslot(3, v), y_left, ("yd", v))

    def y_out(v):
        core_sum(v)
        y_send(v)

    def z_first(v):
        core_sum(v)
        sent["yz", v] = links.start(
            half_ref.at[:, zp, rows_of_unit(v), :], zin_ref.at[:, rows_of_unit(v), :], z_peer
        )

    def z_then_y(v):
        sent["yz", v].wait_recv()
        for j in range(N_Y):
            ysum_ref[j, rows_of_unit(v), :] = add(
                half_ref[j, zl, rows_of_unit(v), :], zin_ref[j, rows_of_unit(v), :]
            )
        y_send(v)

    def y_merge(v):
        links.wait(("yf", v), yslots(2, v))
        ymerged(0, v)[...] = add(yslot(0, v)[...], y_part(y_up, 0, v)[...])
        links.start(ymerged(0, v), yslot(4, v), y_right, ("yd", v))
        ymerged(1, v)[...] = add(yslot(1, v)[...], y_part(y_down, 1, v)[...])
        links.start(ymerged(1, v), yslot(5, v), y_left, ("yd", v))

    def y_total(v, side):
        through, direct = ((4, 3), (5, 2))[side]
        total = yslot(through, v)[...].astype(F32) + yslot(direct, v)[...].astype(F32)
        return total + y_part(y, side, v)[...].astype(F32)

    def y_arrived(v):
        links.wait(("yd", v), yslots(4, v))

    def z_out(v):
        y_arrived(v)
        for side in range(2):
            rows = rows_of_unit(v, side * end_half, end_half)
            ysum_ref[pl.ds(0, N_ZL), rows, :] = y_total(v, side).astype(BF16)
        sent["yz", v] = links.start(
            ysum_ref.at[zp, rows_of_unit(v), :], zin_ref.at[0, rows_of_unit(v), :], z_peer
        )

    place = pl.ds(
        pl.multiple_of(core * side_nodes + (y * N_ZL + zl) * mine_nodes, mine_nodes), mine_nodes
    )

    def scaled(v):
        if v % 2:
            y_arrived(v)
            for side in range(2):
                rows = rows_of_unit(v, side * end_half, end_half)
                gp_ref[rows, :] = (y_total(v, side)[0] * cs_ref[:, place]).astype(BF16)
            return
        sent["yz", v].wait_recv()
        rows = rows_of_unit(v)
        value = ysum_ref[zl, rows, :].astype(F32) + zin_ref[0, rows, :].astype(F32)
        gp_ref[rows, :] = (value * cs_ref[:, place]).astype(BF16)

    def spread(name, src_of, dst):
        for d in range(1, N_ROW):
            links.start(src_of((g + d) % N_ROW), dst, row_group[d - 1], name)
        return src_of(g)

    def spread_weight(p):
        gwt_ref[p] = lax.dot_general(
            gp_ref[pl.ds(p * wide, wide), :],
            all_ref[:, :, place].reshape(feats, mine_nodes),
            (((1,), (1,)), ((), ())),
            preferred_element_type=F32,
        ).astype(BF16)

        def piece(owner):
            return gwt_ref.at[p, pl.ds(pl.multiple_of(owner * own, own), own), :]

        spread(("gw", p), piece, gwl_ref.at[p, g])

    def sum_weight(p):
        links.wait(("gw", p), gwl_ref.at[p, pl.ds(0, N_ROW - 1)])
        total = gwt_ref[p, pl.ds(pl.multiple_of(g * own, own), own), :].astype(F32)
        for d in range(1, N_ROW):
            total = total + gwl_ref[p, (g + d) % N_ROW].astype(F32)
        gw_ref[pl.ds(p * own, own), :] = total

    def feature_product():
        gft_ref[...] = lax.dot_general(
            wt_ref[...], gp_ref[...], (((0,), (0,)), ((), ())), preferred_element_type=F32
        ).astype(BF16)

    def spread_features():
        def piece(owner):
            return gft_ref.at[pl.ds(pl.multiple_of(owner * depth, depth), depth), :]

        mine = spread("gf", piece, gf_ref.at[:, place])
        gf_ref[:, place] = mine[...]

    def share_out(name, p, buffer, group):
        sums = lw_ref.at[0 if name == "px" else 1, p]
        sums[...] = gw_ref[pl.ds(p * own, own), :].astype(BF16)
        for i, peer in enumerate(group):
            links.start(sums, buffer.at[i, p], peer, (name, p))

    def share_in(name, p, buffer, group):
        total = gw_ref[pl.ds(p * own, own), :]
        links.wait((name, p), buffer.at[:, p])
        for i in range(len(group)):
            total = total + buffer[i, p].astype(F32)
        gw_ref[pl.ds(p * own, own), :] = total

    ag_own(0)
    ag_own(1)
    ag_own(2)
    prepare()
    ag_z(0)
    ag_y(0)
    ag_own(3)
    ag_z(1)
    ag_y(1)
    ag_far(0)
    ag_z(2)
    ag_y(2)
    ag_far(1)
    ag_last(0)
    ag_z(3)
    ag_y(3)
    ag_far(2)
    ag_last(1)
    project(0)
    ag_far(3)
    ag_last(2)
    project(1)
    ag_last(3)
    project(2)
    project(3)

    units = PARTS * MID_CHUNKS
    share = TILE // 4
    forward_tiles(0)
    reduce_out(0)
    reduce_out(1)
    forward_tiles(1)
    x_lags = (
        (0, reduce_merge), (-2, reduce_out), (1, reduce_second), (2, merge_second),
        (3, activate), (4, gather_second), (5, gather_first), (6, gather_far),
    )
    z_lags = (
        (0, reduce_out), (2, reduce_merge), (3, reduce_second), (4, merge_second),
        (6, activate), (7, gather_second), (9, gather_first), (11, gather_far),
    )
    x_first = [u for u in range(units) if u not in Z_FIRST]
    steps = len(x_first) + 6
    for step in range(steps):
        for lag, act in x_lags:
            if max(0, -lag) <= step - lag < len(x_first):
                act(x_first[step - lag])
        for lag, act in z_lags:
            for u in Z_FIRST:
                if step == lag:
                    act(u)
        if step == steps - 3:
            for u in range(MID_CHUNKS):
                gather_end(u)
            backward_tiles(0, 0, TILE)
            core_out(1)
            core_out(0)
        if step == steps - 2:
            z_first(1)
            y_out(0)
    for u in range(MID_CHUNKS, units):
        gather_end(u)
    backward_tiles(1, 0, share)
    y_merge(0)
    backward_tiles(1, share, share)
    z_then_y(1)
    backward_tiles(1, 2 * share, 2 * share)
    core_out(3)
    core_out(2)
    y_merge(1)
    z_out(0)
    z_first(3)
    y_out(2)
    scaled(1)
    scaled(0)
    spread_weight(0)
    y_merge(2)
    z_then_y(3)
    z_out(2)
    y_merge(3)
    scaled(2)
    scaled(3)
    spread_weight(1)
    sum_weight(0)
    share_out("px", 0, px_ref, x_group)
    feature_product()
    share_in("px", 0, px_ref, x_group)
    share_out("pz", 0, pz_ref, zh_group)
    sum_weight(1)
    share_out("px", 1, px_ref, x_group)
    spread_features()
    share_in("px", 1, px_ref, x_group)
    share_out("pz", 1, pz_ref, zh_group)
    share_in("pz", 0, pz_ref, zh_group)
    share_in("pz", 1, pz_ref, zh_group)
    links.wait("gf", gft_ref.at[pl.ds(0, (N_ROW - 1) * depth), :])
    links.drain()


def write_kernel(*refs):
    count = len(refs) // 2
    for i in range(count):
        refs[count + i][...] = refs[i][...]


def shards(features, weight, degrees, tile_values, tile_row, tile_col, tile_count, cotangent):
    nodes, depth = features.shape
    feats, hidden = weight.shape
    wide, own = hidden // PARTS, depth // PARTS
    mine = nodes // N_ROW
    side = nodes // N_CORE
    tiles = tile_values[0, 0]
    vmem = pl.BlockSpec(memory_space=pltpu.VMEM)
    smem = pl.BlockSpec(memory_space=pltpu.SMEM)
    anywhere = pl.BlockSpec(memory_space=pl.ANY)

    def buffer(*shape, dtype=BF16):
        return pltpu.VMEM(shape, dtype)

    table = pl.pallas_call(
        plan_kernel,
        out_shape=jax.ShapeDtypeStruct((16, TILE), I32),
        in_specs=[vmem, vmem, smem],
        out_specs=vmem,
        name="plan",
    )(tile_row[0], tile_col[0], tile_count)
    results = pl.pallas_call(
        kernel,
        out_shape=(
            jax.ShapeDtypeStruct((depth, nodes), BF16),
            jax.ShapeDtypeStruct((depth, nodes), BF16),
            jax.ShapeDtypeStruct((depth, feats), F32),
        ),
        in_specs=[anywhere, anywhere, anywhere, anywhere, smem, vmem, anywhere],
        out_specs=(vmem, vmem, vmem),
        scratch_shapes=[
            buffer(N_ROW, depth, nodes),
            buffer(*tiles.shape),
            buffer(feats, hidden),
            buffer(hidden, feats),
            buffer(depth, nodes),
            buffer(2, nodes // TILE, TILE, dtype=I32),
            buffer(1, nodes, dtype=F32),
            buffer(1, nodes, dtype=F32),
            buffer(2, TILE, TILE, dtype=F32),
            buffer(2, TILE, TILE, dtype=F32),
            buffer(PARTS, wide, nodes),
            buffer(TILE, wide, TILE),
            buffer(wide, TILE, dtype=F32),
            buffer(PARTS, N_X, N_ZH, own, nodes),
            buffer(6, PARTS, N_X // 2, own, nodes),
            buffer(2, PARTS, N_X // 2, own, nodes),
            buffer(PARTS, N_X, own, nodes),
            buffer(6, PARTS, own, nodes // 2),
            buffer(2, PARTS, own, nodes // 2),
            buffer(N_X, N_ZH, own, nodes),
            buffer(N_X, N_ZH, own, nodes),
            buffer(PARTS, wide, nodes),
            buffer(hidden, side),
            buffer(N_Y, N_ZL, hidden, mine),
            buffer(6, N_ZL, hidden // 2, mine),
            buffer(2, N_ZL, hidden // 2, mine),
            buffer(N_Y, hidden, mine),
            buffer(N_Y, hidden, mine),
            buffer(hidden, mine),
            buffer(feats, mine),
            buffer(PARTS, wide, feats),
            buffer(PARTS, N_ROW, own, feats),
            buffer(2, PARTS, own, feats),
            buffer(N_X - 1, PARTS, own, feats),
            buffer(N_ZH - 1, PARTS, own, feats),
            pltpu.SemaphoreType.DMA((8,)),
            pltpu.SemaphoreType.DMA((SENDS,)),
            pltpu.SemaphoreType.DMA((RECEIVES,)),
        ],
        compiler_params=pltpu.CompilerParams(
            collective_id=0, has_side_effects=True, vmem_limit_bytes=VMEM_BYTES
        ),
        name="layer",
    )(
        features.T,
        weight,
        degrees.reshape(-1, TILE),
        tiles,
        table,
        table,
        cotangent.T,
    )
    output, grad_features, grad_weight = pl.pallas_call(
        write_kernel,
        out_shape=tuple(jax.ShapeDtypeStruct(r.shape, r.dtype) for r in results),
        in_specs=[vmem] * len(results),
        out_specs=(vmem,) * len(results),
        name="write",
    )(*results)
    return (output.T, grad_features.T, grad_weight.T)


def solution(mesh):
    in_specs = (
        P("col", "row"),
        P(),
        P(),
        P("row", "col", None, None, None),
        P("row", "col", None),
        P("row", "col", None),
        P("row", "col"),
        P("row", "col"),
    )
    out_specs = (P("row", "col"), P("col", "row"), P(None, "row"))
    return jax.shard_map(shards, mesh=mesh, in_specs=in_specs, out_specs=out_specs, check_vma=False)
```

```python
import jax
import jax.numpy as jnp
from jax import lax
from jax.experimental import pallas as pl
from jax.experimental.pallas import tpu as pltpu
from jax.sharding import PartitionSpec as P

TILE = 128
PARTS = 2
N_Y, N_ZL, N_CORE = 4, 2, 2
N_X, N_ZH = 4, 4
N_ROW, N_COL = N_Y * N_ZL * N_CORE, N_X * N_ZH
AG_CHUNKS = 4
MID_CHUNKS = 4
END_CHUNKS = 2
Z_FIRST = (4,)
GROUP = 32
VMEM_BYTES = 60 * 1024 * 1024
BF16, F32, I32 = jnp.bfloat16, jnp.float32, jnp.int32
MESH = pl.DeviceIdType.MESH
SENDS = 40
RECEIVES = AG_CHUNKS * 13 + PARTS * MID_CHUNKS * 8 + PARTS * END_CHUNKS * 4 + PARTS * 3 + 1


class Links:
    def __init__(self, send_sems, recv_sems):
        self.send_sems, self.recv_sems, self.copies, self.groups, self.used = (
            send_sems, recv_sems, [], {}, 0
        )

    def start(self, src, dst, device, group=None):
        count = len(self.copies)
        if count >= SENDS:
            self.copies[count - SENDS].wait_send()
        place = self.groups.get(group)
        if place is None:
            place, self.used = self.used, self.used + 1
            if group is not None:
                self.groups[group] = place
        copy = pltpu.make_async_remote_copy(
            src_ref=src,
            dst_ref=dst,
            send_sem=self.send_sems.at[count % SENDS],
            recv_sem=self.recv_sems.at[place],
            device_id=device,
            device_id_type=MESH,
        )
        copy.start()
        self.copies.append(copy)
        return copy

    def wait(self, group, like):
        pltpu.make_async_copy(like, like, self.recv_sems.at[self.groups[group]]).wait()

    def drain(self):
        for copy in self.copies[-SENDS:]:
            copy.wait_send()


def greet(peers):
    barrier = pltpu.get_barrier_semaphore()
    for peer in peers:
        pl.semaphore_signal(barrier, inc=1, device_id=peer, device_id_type=MESH)
    pl.semaphore_wait(barrier, len(peers))


def add(left, right):
    return (left.astype(F32) + right.astype(F32)).astype(BF16)


def sorted_by(key, gather):
    shape = (TILE, TILE)
    i = lax.broadcasted_iota(I32, shape, 0)
    j = lax.broadcasted_iota(I32, shape, 1)
    across = jnp.broadcast_to(key, shape)
    down = across.T
    before = (down < across).astype(I32) + (down == across).astype(I32) * (i < j).astype(I32)
    rank = jnp.broadcast_to(jnp.sum(before, axis=0, keepdims=True), shape).T

    def total(where, value):
        return jnp.sum(where.astype(I32) * value, axis=0, keepdims=True)

    order = total(rank == j, i)
    source = total(rank == j, jnp.broadcast_to(gather, shape).T)
    same = (total(rank == j, down) == total(rank == j - 1, down)).astype(I32)
    last = jnp.maximum(total(down <= j, 1) - 1, 0)
    some = jnp.minimum(total(down == j, 1), 1)
    return [order, source, last, same, some]


def kernel(
    x_hbm, w_hbm, deg_hbm, tiles_hbm, rows_ref, cols_ref, count_ref, cot_hbm,
    out_ref, gf_ref, gw_ref,
    all_ref, tiles_ref, w_ref, wt_ref, cot_ref, deg_ref, cs_ref, rs_ref, table_ref, idx_ref, same_ref, some_ref,
    proj_ref, seg_ref, acc_ref, part_ref,
    in_ref, merge_ref, sum_ref, z_ref, zmerge_ref, g0_ref, g1_ref, back_ref,
    core_ref, half_ref, yin_ref, ymerge_ref, ysum_ref, zin_ref, gp_ref, gft_ref, gwt_ref, gwl_ref,
    lw_ref, px_ref, pz_ref, local_sems, send_sems, recv_sems,
):
    links = Links(send_sems, recv_sems)
    g, h = lax.axis_index("row"), lax.axis_index("col")
    y, zl, core = g // (N_ZL * N_CORE), (g // N_CORE) % N_ZL, g % N_CORE
    x, zh = h // N_ZH, h % N_ZH
    zp = 1 - zl

    def at(y_of, zl_of, core_of):
        return (y_of * N_ZL + zl_of) * N_CORE + core_of

    y_up, y_down, y_far = (y + 1) % N_Y, (y + N_Y - 1) % N_Y, (y + 2) % N_Y
    x_up, x_down, x_far = (x + 1) % N_X, (x + N_X - 1) % N_X, (x + 2) % N_X
    y_right, y_left = (at(y_up, zl, core), h), (at(y_down, zl, core), h)
    x_right, x_left = (g, x_up * N_ZH + zh), (g, x_down * N_ZH + zh)
    z_peer, c_peer = (at(y, zp, core), h), (at(y, zl, 1 - core), h)
    row_group = [((g + d) % N_ROW, h) for d in range(1, N_ROW)]
    x_group = [(g, ((x + d) % N_X) * N_ZH + zh) for d in range(1, N_X)]
    z_up, z_down, z_far = (zh + 1) % N_ZH, (zh + N_ZH - 1) % N_ZH, (zh + 2) % N_ZH
    z_right, z_left = (g, x * N_ZH + z_up), (g, x * N_ZH + z_down)
    zh_group = [(g, x * N_ZH + (zh + d) % N_ZH) for d in range(1, N_ZH)]

    nodes = x_hbm.shape[1]
    hidden = w_ref.shape[1]
    wide = hidden // PARTS
    depth = x_hbm.shape[0]
    own = depth // PARTS
    feats = w_hbm.shape[0]
    blocks = nodes // TILE
    deg_rows = nodes // TILE
    sent = {}

    local = {}
    loads = (
        ("x", x_hbm, all_ref.at[g]),
        ("w", w_hbm, w_ref),
        ("dc", deg_hbm.at[pl.ds(pl.multiple_of(h * deg_rows, deg_rows), deg_rows)], deg_ref.at[0]),
        ("dr", deg_hbm.at[pl.ds(pl.multiple_of(g * deg_rows, deg_rows), deg_rows)], deg_ref.at[1]),
        ("tiles", tiles_hbm, tiles_ref),
        ("cot", cot_hbm, cot_ref),
    )
    for i, (name, src, dst) in enumerate(loads):
        local[name] = pltpu.make_async_copy(src, dst, local_sems.at[i])
        local[name].start()

    greet(row_group + x_group + zh_group)

    ag_span = nodes // AG_CHUNKS
    first, second = pl.ds(0, depth // 2), pl.ds(depth // 2, depth // 2)

    def ag_lanes(q):
        return pl.ds(q * ag_span, ag_span)

    def forward(owner, q, device, rows=slice(None), group=None):
        block = all_ref.at[owner, rows, ag_lanes(q)]
        return links.start(block, block, device, group)

    def ag_own(q):
        src = x_hbm.at[:, ag_lanes(q)]
        for name, device in (("z", z_peer), ("r", y_right), ("l", y_left)):
            sent[name, q] = links.start(src, all_ref.at[g, :, ag_lanes(q)], device)
        links.start(src, all_ref.at[g, :, ag_lanes(q)], c_peer, ("core", q))

    def ag_z(q):
        sent["z", q].wait_recv()
        owner = at(y, zp, core)
        sent["zr", q] = forward(owner, q, y_right, first)
        sent["zl", q] = forward(owner, q, y_left, first)
        forward(owner, q, c_peer, group=("core", q))

    def ag_y(q):
        sent["r", q].wait_recv()
        sent["fr", q] = forward(at(y_down, zl, core), q, y_right, first)
        sent["rz", q] = forward(at(y_down, zl, core), q, z_peer, second)
        sent["l", q].wait_recv()
        sent["fl", q] = forward(at(y_up, zl, core), q, y_left, second)
        sent["lz", q] = forward(at(y_up, zl, core), q, z_peer, second)
        forward(at(y_down, zl, core), q, c_peer, group=("core", q))
        forward(at(y_up, zl, core), q, c_peer, group=("core", q))

    def ag_far(q):
        sent["fl", q].wait_recv()
        sent["fz", q] = forward(at(y_far, zl, core), q, z_peer, second)
        sent["zr", q].wait_recv()
        lanes = pl.ds(q * ag_span, ag_span // 2)
        block = all_ref.at[at(y_down, zp, core), first, lanes]
        sent["gr", q] = links.start(block, block, y_right)
        sent["zl", q].wait_recv()
        lanes = pl.ds(q * ag_span + ag_span // 2, ag_span // 2)
        block = all_ref.at[at(y_up, zp, core), first, lanes]
        sent["gl", q] = links.start(block, block, y_left)
        sent["fr", q].wait_recv()
        forward(at(y_far, zl, core), q, c_peer, group=("core", q))

    def ag_last(q):
        sent["rz", q].wait_recv()
        forward(at(y_down, zp, core), q, c_peer, group=("core", q))
        sent["lz", q].wait_recv()
        forward(at(y_up, zp, core), q, c_peer, group=("core", q))
        for name in ("gr", "gl", "fz"):
            sent[name, q].wait_recv()
        forward(at(y_far, zp, core), q, c_peer, group=("core", q))

    def project(q):
        links.wait(("core", q), all_ref.at[pl.ds(0, N_Y * N_ZL), :, ag_lanes(q)])
        if q == 0:
            local["x"].wait()
        step = min(ag_span, 512)

        @pl.loop(0, ag_span // step)
        def one(j):
            where = pl.ds(pl.multiple_of(q * ag_span + j * step, step), step)
            block = all_ref[:, :, where].reshape(-1, step)
            value = jnp.dot(wt_ref[...], block, preferred_element_type=F32)
            value = (value * cs_ref[:, where]).astype(BF16)
            for p in range(PARTS):
                proj_ref[p, :, where] = value[p * wide : (p + 1) * wide, :]

    def prepare():
        local["w"].wait()
        turned = w_ref[...].T
        for owner in range(N_COL):
            for p in range(PARTS):
                start = owner * depth + p * own
                wt_ref[pl.ds(p * wide + owner * own, own), :] = turned[start : start + own, :]
        local["dc"].wait()
        local["dr"].wait()
        for ref, i in ((cs_ref, 0), (rs_ref, 1)):
            scale = lax.rsqrt(deg_ref[i].astype(F32))
            for j in range(deg_rows):
                ref[:, pl.ds(j * TILE, TILE)] = scale[j : j + 1, :]
        live = lax.broadcasted_iota(I32, (1, TILE), 1) < jnp.broadcast_to(count_ref[...], (1, TILE))
        live = live.astype(I32)
        rows_of, cols_of = rows_ref[...], cols_ref[...]
        dead = (1 - live) * TILE
        ways = (
            sorted_by(live * rows_of + dead, cols_of),
            sorted_by(live * cols_of + dead, rows_of),
        )
        table_ref[...] = jnp.zeros_like(table_ref)
        for way, lines in enumerate(ways):
            for i, line in enumerate(lines[:3]):
                table_ref[pl.ds(3 * way + i, 1), :] = line
            for ref, line in zip((same_ref, some_ref), lines[3:]):
                ref[way] = jnp.broadcast_to(line.astype(F32), (TILE, TILE)).T
        local["idx"] = pltpu.make_async_copy(table_ref, idx_ref, local_sems.at[len(loads)])
        local["idx"].start()
        local["tiles"].wait()
        local["cot"].wait()

    def tiles_times(way, dense, contract, first_tile, tiles):
        @pl.loop(first_tile // GROUP, (first_tile + tiles) // GROUP)
        def step(i):
            products = []
            for j in range(GROUP):
                t = i * GROUP + j
                source = pl.ds(idx_ref[3 * way + 1, t] * TILE, TILE)
                products.append(
                    lax.dot_general(
                        dense(source),
                        tiles_ref[idx_ref[3 * way, t]],
                        contract,
                        preferred_element_type=F32,
                    )
                )
            total = acc_ref[...]
            for j in range(GROUP):
                t = i * GROUP + j
                total = total * same_ref[way, pl.ds(t, 1), :] + products[j]
                seg_ref[t] = total.astype(BF16)
            acc_ref[...] = total

    def clear():
        acc_ref[...] = jnp.zeros_like(acc_ref)

    def collect(way, ref, p):
        @pl.loop(0, blocks)
        def one(b):
            value = seg_ref[idx_ref[3 * way + 2, b]]
            where = pl.ds(pl.multiple_of(b * TILE, TILE), TILE)
            some = some_ref[way, pl.ds(b, 1), :]
            value = (value.astype(F32) * some).astype(BF16)
            if len(ref.shape) == 3:
                ref[p, :, where] = value
            else:
                ref[p, :, :, :, where] = value.reshape(N_X, N_ZH, own, TILE)

    by_row = (((1,), (1,)), ((), ()))
    by_col = (((1,), (0,)), ((), ()))
    grads = (g0_ref, g1_ref)

    def forward_tiles(p):
        clear()
        tiles_times(0, lambda source: proj_ref[p, :, source], by_row, 0, TILE)
        collect(0, part_ref, p)

    def backward_tiles(p, first_tile, tiles):
        if first_tile == 0:
            clear()
        tiles_times(
            1,
            lambda source: grads[p][:, :, :, source].reshape(wide, TILE),
            by_col,
            first_tile,
            tiles,
        )
        if first_tile + tiles == TILE:
            collect(1, back_ref, p)

    span = nodes // MID_CHUNKS
    pair = N_X // 2
    ring = {
        "x": (x, x_up, x_down, x_far, x_right, x_left),
        "z": (zh, z_up, z_down, z_far, z_right, z_left),
    }

    def axes(u):
        return ("z", "x") if u in Z_FIRST else ("x", "z")

    def unit(u):
        p, q = u // MID_CHUNKS, u % MID_CHUNKS
        return p, pl.ds(q * span, span)

    def half_lanes(u, side):
        return pl.ds((u % MID_CHUNKS) * span + side * (span // 2), span // 2)

    def grid(ref, axis, along, across, lanes):
        if axis == "x":
            return ref.at[along, across, :, lanes]
        return ref.at[across, along, :, lanes]

    def part(coord, side, u):
        p, lanes = unit(u)
        return grid(part_ref.at[p], axes(u)[0], coord, pl.ds(side * pair, pair), lanes)

    def slot(i, u):
        p, lanes = unit(u)
        return in_ref.at[i, p, :, :, lanes]

    def merged(i, u):
        p, lanes = unit(u)
        return merge_ref.at[i, p, :, :, lanes]

    def reduce_out(u):
        me, up, down, far, right, left = ring[axes(u)[0]]
        links.start(part(far, 0, u), slot(0, u), right, ("f", u))
        links.start(part(far, 1, u), slot(1, u), left, ("f", u))
        links.start(part(up, 1, u), slot(2, u), right, ("d", u))
        links.start(part(down, 0, u), slot(3, u), left, ("d", u))

    def reduce_merge(u):
        me, up, down, far, right, left = ring[axes(u)[0]]
        p, lanes = unit(u)
        links.wait(("f", u), in_ref.at[pl.ds(0, 2), p, :, :, lanes])
        merged(0, u)[...] = add(slot(0, u)[...], part(up, 0, u)[...])
        links.start(merged(0, u), slot(4, u), right, ("d", u))
        merged(1, u)[...] = add(slot(1, u)[...], part(down, 1, u)[...])
        links.start(merged(1, u), slot(5, u), left, ("d", u))

    def second_part(coord, side, u):
        return sum_ref.at[u // MID_CHUNKS, coord, :, half_lanes(u, side)]

    def second_slots(i, count, u):
        lanes = pl.ds((u % MID_CHUNKS) * (span // 2), span // 2)
        return z_ref.at[pl.ds(i, count), u // MID_CHUNKS, :, lanes]

    def second_slot(i, u):
        return z_ref.at[i, u // MID_CHUNKS, :, pl.ds((u % MID_CHUNKS) * (span // 2), span // 2)]

    def second_merged(i, u):
        lanes = pl.ds((u % MID_CHUNKS) * (span // 2), span // 2)
        return zmerge_ref.at[i, u // MID_CHUNKS, :, lanes]

    def reduce_second(u):
        p, lanes = unit(u)
        me = ring[axes(u)[0]][0]
        links.wait(("d", u), in_ref.at[pl.ds(0, 4), p, :, :, lanes])
        for side, (through, direct) in enumerate(((4, 3), (5, 2))):
            total = slot(through, u)[...].astype(F32) + slot(direct, u)[...].astype(F32)
            total = total + part(me, side, u)[...].astype(F32)
            sum_ref[p, pl.ds(side * pair, pair), :, lanes] = total.astype(BF16)
        me, up, down, far, right, left = ring[axes(u)[1]]
        links.start(second_part(far, 0, u), second_slot(0, u), right, ("zf", u))
        links.start(second_part(far, 1, u), second_slot(1, u), left, ("zf", u))
        links.start(second_part(up, 1, u), second_slot(2, u), right, ("zd", u))
        links.start(second_part(down, 0, u), second_slot(3, u), left, ("zd", u))

    def merge_second(u):
        me, up, down, far, right, left = ring[axes(u)[1]]
        links.wait(("zf", u), second_slots(0, 2, u))
        second_merged(0, u)[...] = add(second_slot(0, u)[...], second_part(up, 0, u)[...])
        links.start(second_merged(0, u), second_slot(4, u), right, ("zd", u))
        second_merged(1, u)[...] = add(second_slot(1, u)[...], second_part(down, 1, u)[...])
        links.start(second_merged(1, u), second_slot(5, u), left, ("zd", u))

    def activate(u):
        p, lanes = unit(u)
        me, up, down, far, right, left = ring[axes(u)[1]]
        links.wait(("zd", u), second_slots(0, 4, u))
        rows = pl.ds(p * own, own)
        for side, (through, direct) in enumerate(((4, 3), (5, 2))):
            here = half_lanes(u, side)
            value = second_slot(through, u)[...].astype(F32)
            value = value + second_slot(direct, u)[...].astype(F32)
            value = value + second_part(me, side, u)[...].astype(F32)
            scale = rs_ref[:, here]
            hidden_in = value * scale
            sigma = 1.0 / (1.0 + jnp.exp(-hidden_in))
            out_ref[rows, here] = (hidden_in * sigma).astype(BF16)
            slope = sigma * (1.0 + hidden_in * (1.0 - sigma))
            grad = cot_ref[rows, here].astype(F32) * slope * scale
            grads[p][x, zh, :, here] = grad.astype(BF16)
        mine = grads[p].at[x, zh, :, lanes]
        links.start(mine, mine, right, ("a", u))
        links.start(mine, mine, left, ("a", u))

    def gather_second(u):
        first_axis, axis = axes(u)
        me, up, down, far, right, left = ring[axis]
        across, ref = ring[first_axis][0], grads[u // MID_CHUNKS]
        lanes = unit(u)[1]
        links.wait(("a", u), ref.at[0, pl.ds(0, 2), :, lanes])
        near = grid(ref, axis, down, across, half_lanes(u, 0))
        links.start(near, near, right, ("b", u))
        near = grid(ref, axis, up, across, half_lanes(u, 1))
        links.start(near, near, left, ("b", u))

    def gather_first(u):
        p, lanes = unit(u)
        axis = axes(u)[0]
        me, up, down, far, right, left = ring[axis]
        links.wait(("b", u), grads[p].at[0, 0, :, lanes])
        mine = grid(grads[p], axis, me, slice(None), lanes)
        links.start(mine, mine, right, ("g", u))
        links.start(mine, mine, left, ("g", u))

    def gather_far(u):
        p, lanes = unit(u)
        axis = axes(u)[0]
        me, up, down, far, right, left = ring[axis]
        links.wait(("g", u), grads[p].at[pl.ds(0, 2), :, :, lanes])
        near = grid(grads[p], axis, down, pl.ds(0, pair), lanes)
        links.start(near, near, right, ("h", u))
        near = grid(grads[p], axis, up, pl.ds(pair, pair), lanes)
        links.start(near, near, left, ("h", u))

    def gather_end(u):
        p, lanes = unit(u)
        links.wait(("h", u), grads[p].at[0, :, :, lanes])

    end_rows = wide // END_CHUNKS
    end_half = end_rows // 2
    side_nodes = nodes // N_CORE
    mine_nodes = nodes // N_ROW

    def rows_of_unit(v, start=0, size=end_rows):
        return pl.ds(v * end_rows + start, size)

    def core_out(v):
        p, r = v // END_CHUNKS, v % END_CHUNKS
        there = pl.ds(pl.multiple_of((1 - core) * side_nodes, side_nodes), side_nodes)
        src = back_ref.at[p, pl.ds(r * end_rows, end_rows), there]
        sent["c", v] = links.start(src, core_ref.at[rows_of_unit(v), :], c_peer)

    def core_sum(v):
        p, r = v // END_CHUNKS, v % END_CHUNKS
        sent["c", v].wait_recv()
        for j in range(N_Y * N_ZL):
            here = pl.ds(j * mine_nodes, mine_nodes)
            there = pl.ds(
                pl.multiple_of(core * side_nodes + j * mine_nodes, mine_nodes), mine_nodes
            )
            half_ref[j // N_ZL, j % N_ZL, rows_of_unit(v), :] = add(
                back_ref[p, pl.ds(r * end_rows, end_rows), there], core_ref[rows_of_unit(v), here]
            )

    def y_part(y_of, side, v):
        rows = rows_of_unit(v, side * end_half, end_half)
        if v % 2:
            return ysum_ref.at[pl.ds(y_of, 1), rows, :]
        return half_ref.at[y_of, :, rows, :]

    def y_buffer(ref, i, v):
        rows = pl.ds(v * end_half, end_half)
        return ref.at[i, pl.ds(0, 1) if v % 2 else slice(None), rows, :]

    def yslots(count, v):
        return y_buffer(yin_ref, pl.ds(0, count), v)

    def yslot(i, v):
        return y_buffer(yin_ref, i, v)

    def ymerged(i, v):
        return y_buffer(ymerge_ref, i, v)

    def y_send(v):
        links.start(y_part(y_far, 0, v), yslot(0, v), y_right, ("yf", v))
        links.start(y_part(y_far, 1, v), yslot(1, v), y_left, ("yf", v))
        links.start(y_part(y_up, 1, v), yslot(2, v), y_right, ("yd", v))
        links.start(y_part(y_down, 0, v), yslot(3, v), y_left, ("yd", v))

    def y_out(v):
        core_sum(v)
        y_send(v)

    def z_first(v):
        core_sum(v)
        sent["yz", v] = links.start(
            half_ref.at[:, zp, rows_of_unit(v), :], zin_ref.at[:, rows_of_unit(v), :], z_peer
        )

    def z_then_y(v):
        sent["yz", v].wait_recv()
        for j in range(N_Y):
            ysum_ref[j, rows_of_unit(v), :] = add(
                half_ref[j, zl, rows_of_unit(v), :], zin_ref[j, rows_of_unit(v), :]
            )
        y_send(v)

    def y_merge(v):
        links.wait(("yf", v), yslots(2, v))
        ymerged(0, v)[...] = add(yslot(0, v)[...], y_part(y_up, 0, v)[...])
        links.start(ymerged(0, v), yslot(4, v), y_right, ("yd", v))
        ymerged(1, v)[...] = add(yslot(1, v)[...], y_part(y_down, 1, v)[...])
        links.start(ymerged(1, v), yslot(5, v), y_left, ("yd", v))

    def y_total(v, side):
        through, direct = ((4, 3), (5, 2))[side]
        total = yslot(through, v)[...].astype(F32) + yslot(direct, v)[...].astype(F32)
        return total + y_part(y, side, v)[...].astype(F32)

    def y_arrived(v):
        links.wait(("yd", v), yslots(4, v))

    def z_out(v):
        y_arrived(v)
        for side in range(2):
            rows = rows_of_unit(v, side * end_half, end_half)
            ysum_ref[pl.ds(0, N_ZL), rows, :] = y_total(v, side).astype(BF16)
        sent["yz", v] = links.start(
            ysum_ref.at[zp, rows_of_unit(v), :], zin_ref.at[0, rows_of_unit(v), :], z_peer
        )

    place = pl.ds(
        pl.multiple_of(core * side_nodes + (y * N_ZL + zl) * mine_nodes, mine_nodes), mine_nodes
    )

    def scaled(v):
        if v % 2:
            y_arrived(v)
            for side in range(2):
                rows = rows_of_unit(v, side * end_half, end_half)
                gp_ref[rows, :] = (y_total(v, side)[0] * cs_ref[:, place]).astype(BF16)
            return
        sent["yz", v].wait_recv()
        rows = rows_of_unit(v)
        value = ysum_ref[zl, rows, :].astype(F32) + zin_ref[0, rows, :].astype(F32)
        gp_ref[rows, :] = (value * cs_ref[:, place]).astype(BF16)

    def spread(name, src_of, dst):
        for d in range(1, N_ROW):
            links.start(src_of((g + d) % N_ROW), dst, row_group[d - 1], name)
        return src_of(g)

    def spread_weight(p):
        gwt_ref[p] = lax.dot_general(
            gp_ref[pl.ds(p * wide, wide), :],
            all_ref[:, :, place].reshape(feats, mine_nodes),
            (((1,), (1,)), ((), ())),
            preferred_element_type=F32,
        ).astype(BF16)

        def piece(owner):
            return gwt_ref.at[p, pl.ds(pl.multiple_of(owner * own, own), own), :]

        spread(("gw", p), piece, gwl_ref.at[p, g])

    def sum_weight(p):
        links.wait(("gw", p), gwl_ref.at[p, pl.ds(0, N_ROW - 1)])
        total = gwt_ref[p, pl.ds(pl.multiple_of(g * own, own), own), :].astype(F32)
        for d in range(1, N_ROW):
            total = total + gwl_ref[p, (g + d) % N_ROW].astype(F32)
        gw_ref[pl.ds(p * own, own), :] = total

    def feature_product():
        gft_ref[...] = lax.dot_general(
            wt_ref[...], gp_ref[...], (((0,), (0,)), ((), ())), preferred_element_type=F32
        ).astype(BF16)

    def spread_features():
        def piece(owner):
            return gft_ref.at[pl.ds(pl.multiple_of(owner * depth, depth), depth), :]

        mine = spread("gf", piece, gf_ref.at[:, place])
        gf_ref[:, place] = mine[...]

    def share_out(name, p, buffer, group):
        sums = lw_ref.at[0 if name == "px" else 1, p]
        sums[...] = gw_ref[pl.ds(p * own, own), :].astype(BF16)
        for i, peer in enumerate(group):
            links.start(sums, buffer.at[i, p], peer, (name, p))

    def share_in(name, p, buffer, group):
        total = gw_ref[pl.ds(p * own, own), :]
        links.wait((name, p), buffer.at[:, p])
        for i in range(len(group)):
            total = total + buffer[i, p].astype(F32)
        gw_ref[pl.ds(p * own, own), :] = total

    ag_own(0)
    ag_own(1)
    ag_own(2)
    prepare()
    ag_z(0)
    ag_y(0)
    ag_own(3)
    ag_z(1)
    ag_y(1)
    ag_far(0)
    ag_z(2)
    ag_y(2)
    ag_far(1)
    ag_last(0)
    ag_z(3)
    ag_y(3)
    ag_far(2)
    ag_last(1)
    project(0)
    ag_far(3)
    ag_last(2)
    project(1)
    ag_last(3)
    project(2)
    project(3)

    units = PARTS * MID_CHUNKS
    share = TILE // 4
    local["idx"].wait()
    forward_tiles(0)
    reduce_out(0)
    reduce_out(1)
    forward_tiles(1)
    x_lags = (
        (0, reduce_merge), (-2, reduce_out), (1, reduce_second), (2, merge_second),
        (3, activate), (4, gather_second), (5, gather_first), (6, gather_far),
    )
    z_lags = (
        (0, reduce_out), (2, reduce_merge), (3, reduce_second), (4, merge_second),
        (6, activate), (7, gather_second), (9, gather_first), (11, gather_far),
    )
    x_first = [u for u in range(units) if u not in Z_FIRST]
    steps = len(x_first) + 6
    for step in range(steps):
        for lag, act in x_lags:
            if max(0, -lag) <= step - lag < len(x_first):
                act(x_first[step - lag])
        for lag, act in z_lags:
            for u in Z_FIRST:
                if step == lag:
                    act(u)
        if step == steps - 3:
            for u in range(MID_CHUNKS):
                gather_end(u)
            backward_tiles(0, 0, TILE)
            core_out(1)
            core_out(0)
        if step == steps - 2:
            z_first(1)
            y_out(0)
    for u in range(MID_CHUNKS, units):
        gather_end(u)
    backward_tiles(1, 0, share)
    y_merge(0)
    backward_tiles(1, share, share)
    z_then_y(1)
    backward_tiles(1, 2 * share, 2 * share)
    core_out(3)
    core_out(2)
    y_merge(1)
    z_out(0)
    z_first(3)
    y_out(2)
    scaled(1)
    scaled(0)
    spread_weight(0)
    y_merge(2)
    z_then_y(3)
    z_out(2)
    y_merge(3)
    scaled(2)
    scaled(3)
    spread_weight(1)
    sum_weight(0)
    share_out("px", 0, px_ref, x_group)
    feature_product()
    share_in("px", 0, px_ref, x_group)
    share_out("pz", 0, pz_ref, zh_group)
    sum_weight(1)
    share_out("px", 1, px_ref, x_group)
    spread_features()
    share_in("px", 1, px_ref, x_group)
    share_out("pz", 1, pz_ref, zh_group)
    share_in("pz", 0, pz_ref, zh_group)
    share_in("pz", 1, pz_ref, zh_group)
    links.wait("gf", gft_ref.at[pl.ds(0, (N_ROW - 1) * depth), :])
    links.drain()


def write_kernel(*refs):
    count = len(refs) // 2
    for i in range(count):
        refs[count + i][...] = refs[i][...]


def shards(features, weight, degrees, tile_values, tile_row, tile_col, tile_count, cotangent):
    nodes, depth = features.shape
    feats, hidden = weight.shape
    wide, own = hidden // PARTS, depth // PARTS
    mine = nodes // N_ROW
    side = nodes // N_CORE
    tiles = tile_values[0, 0]
    vmem = pl.BlockSpec(memory_space=pltpu.VMEM)
    anywhere = pl.BlockSpec(memory_space=pl.ANY)

    def buffer(*shape, dtype=BF16):
        return pltpu.VMEM(shape, dtype)

    results = pl.pallas_call(
        kernel,
        out_shape=(
            jax.ShapeDtypeStruct((depth, nodes), BF16),
            jax.ShapeDtypeStruct((depth, nodes), BF16),
            jax.ShapeDtypeStruct((depth, feats), F32),
        ),
        in_specs=[anywhere, anywhere, anywhere, anywhere, vmem, vmem, vmem, anywhere],
        out_specs=(vmem, vmem, vmem),
        scratch_shapes=[
            buffer(N_ROW, depth, nodes),
            buffer(*tiles.shape),
            buffer(feats, hidden),
            buffer(hidden, feats),
            buffer(depth, nodes),
            buffer(2, nodes // TILE, TILE, dtype=I32),
            buffer(1, nodes, dtype=F32),
            buffer(1, nodes, dtype=F32),
            buffer(8, TILE, dtype=I32),
            pltpu.SMEM((8, TILE), I32),
            buffer(2, TILE, TILE, dtype=F32),
            buffer(2, TILE, TILE, dtype=F32),
            buffer(PARTS, wide, nodes),
            buffer(TILE, wide, TILE),
            buffer(wide, TILE, dtype=F32),
            buffer(PARTS, N_X, N_ZH, own, nodes),
            buffer(6, PARTS, N_X // 2, own, nodes),
            buffer(2, PARTS, N_X // 2, own, nodes),
            buffer(PARTS, N_X, own, nodes),
            buffer(6, PARTS, own, nodes // 2),
            buffer(2, PARTS, own, nodes // 2),
            buffer(N_X, N_ZH, own, nodes),
            buffer(N_X, N_ZH, own, nodes),
            buffer(PARTS, wide, nodes),
            buffer(hidden, side),
            buffer(N_Y, N_ZL, hidden, mine),
            buffer(6, N_ZL, hidden // 2, mine),
            buffer(2, N_ZL, hidden // 2, mine),
            buffer(N_Y, hidden, mine),
            buffer(N_Y, hidden, mine),
            buffer(hidden, mine),
            buffer(feats, mine),
            buffer(PARTS, wide, feats),
            buffer(PARTS, N_ROW, own, feats),
            buffer(2, PARTS, own, feats),
            buffer(N_X - 1, PARTS, own, feats),
            buffer(N_ZH - 1, PARTS, own, feats),
            pltpu.SemaphoreType.DMA((7,)),
            pltpu.SemaphoreType.DMA((SENDS,)),
            pltpu.SemaphoreType.DMA((RECEIVES,)),
        ],
        compiler_params=pltpu.CompilerParams(
            collective_id=0, has_side_effects=True, vmem_limit_bytes=VMEM_BYTES
        ),
        name="layer",
    )(
        features.T,
        weight,
        degrees.reshape(-1, TILE),
        tiles,
        tile_row[0],
        tile_col[0],
        tile_count,
        cotangent.T,
    )
    output, grad_features, grad_weight = pl.pallas_call(
        write_kernel,
        out_shape=tuple(jax.ShapeDtypeStruct(r.shape, r.dtype) for r in results),
        in_specs=[vmem] * len(results),
        out_specs=(vmem,) * len(results),
        name="write",
    )(*results)
    return (output.T, grad_features.T, grad_weight.T)


def solution(mesh):
    in_specs = (
        P("col", "row"),
        P(),
        P(),
        P("row", "col", None, None, None),
        P("row", "col", None),
        P("row", "col", None),
        P("row", "col"),
        P("row", "col"),
    )
    out_specs = (P("row", "col"), P("col", "row"), P(None, "row"))
    return jax.shard_map(shards, mesh=mesh, in_specs=in_specs, out_specs=out_specs, check_vma=False)
```

```python
import jax
import jax.numpy as jnp
from jax import lax
from jax.experimental import pallas as pl
from jax.experimental.pallas import tpu as pltpu
from jax.sharding import PartitionSpec as P

TILE = 128
PARTS = 2
N_Y, N_ZL, N_CORE = 4, 2, 2
N_X, N_ZH = 4, 4
N_ROW, N_COL = N_Y * N_ZL * N_CORE, N_X * N_ZH
AG_CHUNKS = 4
MID_CHUNKS = 4
END_CHUNKS = 2
Z_FIRST = (4,)
GROUP = 32
VMEM_BYTES = 60 * 1024 * 1024
BF16, F32, I32 = jnp.bfloat16, jnp.float32, jnp.int32
MESH = pl.DeviceIdType.MESH
SENDS = 40
RECEIVES = AG_CHUNKS * 13 + PARTS * MID_CHUNKS * 8 + PARTS * END_CHUNKS * 4 + PARTS * 3 + 1


class Links:
    def __init__(self, send_sems, recv_sems):
        self.send_sems, self.recv_sems, self.copies, self.groups, self.used = (
            send_sems, recv_sems, [], {}, 0
        )

    def start(self, src, dst, device, group=None):
        count = len(self.copies)
        if count >= SENDS:
            self.copies[count - SENDS].wait_send()
        place = self.groups.get(group)
        if place is None:
            place, self.used = self.used, self.used + 1
            if group is not None:
                self.groups[group] = place
        copy = pltpu.make_async_remote_copy(
            src_ref=src,
            dst_ref=dst,
            send_sem=self.send_sems.at[count % SENDS],
            recv_sem=self.recv_sems.at[place],
            device_id=device,
            device_id_type=MESH,
        )
        copy.start()
        self.copies.append(copy)
        return copy

    def wait(self, group, like):
        pltpu.make_async_copy(like, like, self.recv_sems.at[self.groups[group]]).wait()

    def drain(self):
        for copy in self.copies[-SENDS:]:
            copy.wait_send()


def greet(peers):
    barrier = pltpu.get_barrier_semaphore()
    for peer in peers:
        pl.semaphore_signal(barrier, inc=1, device_id=peer, device_id_type=MESH)
    pl.semaphore_wait(barrier, len(peers))


def add(left, right):
    return (left.astype(F32) + right.astype(F32)).astype(BF16)


def sorted_by(key, gather):
    shape = (TILE, TILE)
    i = lax.broadcasted_iota(I32, shape, 0)
    j = lax.broadcasted_iota(I32, shape, 1)
    across = jnp.broadcast_to(key, shape)
    down = across.T
    before = (down < across).astype(I32) + (down == across).astype(I32) * (i < j).astype(I32)
    rank = jnp.broadcast_to(jnp.sum(before, axis=0, keepdims=True), shape).T

    def total(where, value):
        return jnp.sum(where.astype(I32) * value, axis=0, keepdims=True)

    order = total(rank == j, i)
    source = total(rank == j, jnp.broadcast_to(gather, shape).T)
    same = (total(rank == j, down) == total(rank == j - 1, down)).astype(I32)
    last = jnp.maximum(total(down <= j, 1) - 1, 0)
    some = jnp.minimum(total(down == j, 1), 1)
    return [order, source, last, same, some]


def kernel(
    x_hbm, w_hbm, deg_hbm, tiles_hbm, rows_ref, cols_ref, count_ref, cot_hbm,
    out_ref, gf_ref, gw_ref,
    all_ref, tiles_ref, w_ref, wt_ref, cot_ref, deg_ref, cs_ref, rs_ref, table_ref, idx_ref, same_ref, some_ref,
    proj_ref, seg_ref, acc_ref, part_ref,
    in_ref, merge_ref, sum_ref, z_ref, zmerge_ref, g0_ref, g1_ref, back_ref,
    core_ref, half_ref, yin_ref, ymerge_ref, ysum_ref, zin_ref, gp_ref, gft_ref, gwt_ref, gwl_ref,
    lw_ref, px_ref, pz_ref, local_sems, send_sems, recv_sems,
):
    links = Links(send_sems, recv_sems)
    g, h = lax.axis_index("row"), lax.axis_index("col")
    y, zl, core = g // (N_ZL * N_CORE), (g // N_CORE) % N_ZL, g % N_CORE
    x, zh = h // N_ZH, h % N_ZH
    zp = 1 - zl

    def at(y_of, zl_of, core_of):
        return (y_of * N_ZL + zl_of) * N_CORE + core_of

    y_up, y_down, y_far = (y + 1) % N_Y, (y + N_Y - 1) % N_Y, (y + 2) % N_Y
    x_up, x_down, x_far = (x + 1) % N_X, (x + N_X - 1) % N_X, (x + 2) % N_X
    y_right, y_left = (at(y_up, zl, core), h), (at(y_down, zl, core), h)
    x_right, x_left = (g, x_up * N_ZH + zh), (g, x_down * N_ZH + zh)
    z_peer, c_peer = (at(y, zp, core), h), (at(y, zl, 1 - core), h)
    row_group = [((g + d) % N_ROW, h) for d in range(1, N_ROW)]
    x_group = [(g, ((x + d) % N_X) * N_ZH + zh) for d in range(1, N_X)]
    z_up, z_down, z_far = (zh + 1) % N_ZH, (zh + N_ZH - 1) % N_ZH, (zh + 2) % N_ZH
    z_right, z_left = (g, x * N_ZH + z_up), (g, x * N_ZH + z_down)
    zh_group = [(g, x * N_ZH + (zh + d) % N_ZH) for d in range(1, N_ZH)]

    nodes = x_hbm.shape[1]
    hidden = w_ref.shape[1]
    wide = hidden // PARTS
    depth = x_hbm.shape[0]
    own = depth // PARTS
    feats = w_hbm.shape[0]
    blocks = nodes // TILE
    deg_rows = nodes // TILE
    sent = {}

    local = {}
    loads = (
        ("x", x_hbm, all_ref.at[g]),
        ("w", w_hbm, w_ref),
        ("dc", deg_hbm.at[pl.ds(pl.multiple_of(h * deg_rows, deg_rows), deg_rows)], deg_ref.at[0]),
        ("dr", deg_hbm.at[pl.ds(pl.multiple_of(g * deg_rows, deg_rows), deg_rows)], deg_ref.at[1]),
        ("tiles", tiles_hbm, tiles_ref),
        ("cot", cot_hbm, cot_ref),
    )
    for i, (name, src, dst) in enumerate(loads):
        local[name] = pltpu.make_async_copy(src, dst, local_sems.at[i])
        local[name].start()

    greet(row_group + x_group + zh_group)

    ag_span = nodes // AG_CHUNKS
    first, second = pl.ds(0, depth // 2), pl.ds(depth // 2, depth // 2)

    def ag_lanes(q):
        return pl.ds(q * ag_span, ag_span)

    def forward(owner, q, device, rows=slice(None), group=None):
        block = all_ref.at[owner, rows, ag_lanes(q)]
        return links.start(block, block, device, group)

    def ag_own(q):
        src = x_hbm.at[:, ag_lanes(q)]
        for name, device in (("z", z_peer), ("r", y_right), ("l", y_left)):
            sent[name, q] = links.start(src, all_ref.at[g, :, ag_lanes(q)], device)
        links.start(src, all_ref.at[g, :, ag_lanes(q)], c_peer, ("core", q))

    def ag_z(q):
        sent["z", q].wait_recv()
        owner = at(y, zp, core)
        sent["zr", q] = forward(owner, q, y_right, first)
        sent["zl", q] = forward(owner, q, y_left, first)
        forward(owner, q, c_peer, group=("core", q))

    def ag_y(q):
        sent["r", q].wait_recv()
        sent["fr", q] = forward(at(y_down, zl, core), q, y_right, first)
        sent["rz", q] = forward(at(y_down, zl, core), q, z_peer, second)
        sent["l", q].wait_recv()
        sent["fl", q] = forward(at(y_up, zl, core), q, y_left, second)
        sent["lz", q] = forward(at(y_up, zl, core), q, z_peer, second)
        forward(at(y_down, zl, core), q, c_peer, group=("core", q))
        forward(at(y_up, zl, core), q, c_peer, group=("core", q))

    def ag_far(q):
        sent["fl", q].wait_recv()
        sent["fz", q] = forward(at(y_far, zl, core), q, z_peer, second)
        sent["zr", q].wait_recv()
        lanes = pl.ds(q * ag_span, ag_span // 2)
        block = all_ref.at[at(y_down, zp, core), first, lanes]
        sent["gr", q] = links.start(block, block, y_right)
        sent["zl", q].wait_recv()
        lanes = pl.ds(q * ag_span + ag_span // 2, ag_span // 2)
        block = all_ref.at[at(y_up, zp, core), first, lanes]
        sent["gl", q] = links.start(block, block, y_left)
        sent["fr", q].wait_recv()
        forward(at(y_far, zl, core), q, c_peer, group=("core", q))

    def ag_last(q):
        sent["rz", q].wait_recv()
        forward(at(y_down, zp, core), q, c_peer, group=("core", q))
        sent["lz", q].wait_recv()
        forward(at(y_up, zp, core), q, c_peer, group=("core", q))
        for name in ("gr", "gl", "fz"):
            sent[name, q].wait_recv()
        forward(at(y_far, zp, core), q, c_peer, group=("core", q))

    def project(q):
        links.wait(("core", q), all_ref.at[pl.ds(0, N_Y * N_ZL), :, ag_lanes(q)])
        if q == 0:
            local["x"].wait()
        step = min(ag_span, 512)

        @pl.loop(0, ag_span // step)
        def one(j):
            where = pl.ds(pl.multiple_of(q * ag_span + j * step, step), step)
            block = all_ref[:, :, where].reshape(-1, step)
            value = jnp.dot(wt_ref[...], block, preferred_element_type=F32)
            value = (value * cs_ref[:, where]).astype(BF16)
            for p in range(PARTS):
                proj_ref[p, :, where] = value[p * wide : (p + 1) * wide, :]

    def prepare():
        local["w"].wait()
        turned = w_ref[...].T
        for owner in range(N_COL):
            for p in range(PARTS):
                start = owner * depth + p * own
                wt_ref[pl.ds(p * wide + owner * own, own), :] = turned[start : start + own, :]
        local["dc"].wait()
        local["dr"].wait()
        for ref, i in ((cs_ref, 0), (rs_ref, 1)):
            scale = lax.rsqrt(deg_ref[i].astype(F32))
            for j in range(deg_rows):
                ref[:, pl.ds(j * TILE, TILE)] = scale[j : j + 1, :]
        live = lax.broadcasted_iota(I32, (1, TILE), 1) < jnp.broadcast_to(count_ref[...], (1, TILE))
        live = live.astype(I32)
        rows_of, cols_of = rows_ref[...], cols_ref[...]
        dead = (1 - live) * TILE
        ways = (
            sorted_by(live * rows_of + dead, cols_of),
            sorted_by(live * cols_of + dead, rows_of),
        )
        table_ref[...] = jnp.zeros_like(table_ref)
        for way, lines in enumerate(ways):
            for i, line in enumerate(lines[:3]):
                table_ref[pl.ds(3 * way + i, 1), :] = line
            for ref, line in zip((same_ref, some_ref), lines[3:]):
                ref[way] = jnp.broadcast_to(line.astype(F32), (TILE, TILE)).T
        local["idx"] = pltpu.make_async_copy(table_ref, idx_ref, local_sems.at[len(loads)])
        local["idx"].start()
        local["tiles"].wait()
        local["cot"].wait()

    def tiles_times(way, dense, contract, first_tile, tiles):
        @pl.loop(first_tile // GROUP, (first_tile + tiles) // GROUP)
        def step(i):
            products = []
            for j in range(GROUP):
                t = i * GROUP + j
                source = pl.ds(idx_ref[3 * way + 1, t] * TILE, TILE)
                products.append(
                    lax.dot_general(
                        dense(source),
                        tiles_ref[idx_ref[3 * way, t]],
                        contract,
                        preferred_element_type=F32,
                    )
                )
            total = acc_ref[...]
            for j in range(GROUP):
                t = i * GROUP + j
                total = total * same_ref[way, pl.ds(t, 1), :] + products[j]
                seg_ref[t] = total.astype(BF16)
            acc_ref[...] = total

    def clear():
        acc_ref[...] = jnp.zeros_like(acc_ref)

    def collect(way, ref, p):
        @pl.loop(0, blocks)
        def one(b):
            value = seg_ref[idx_ref[3 * way + 2, b]]
            where = pl.ds(pl.multiple_of(b * TILE, TILE), TILE)
            some = some_ref[way, pl.ds(b, 1), :]
            value = (value.astype(F32) * some).astype(BF16)
            if len(ref.shape) == 3:
                ref[p, :, where] = value
            else:
                ref[p, :, :, :, where] = value.reshape(N_X, N_ZH, own, TILE)

    by_row = (((1,), (1,)), ((), ()))
    by_col = (((1,), (0,)), ((), ()))
    grads = (g0_ref, g1_ref)

    def forward_tiles(p):
        clear()
        tiles_times(0, lambda source: proj_ref[p, :, source], by_row, 0, TILE)
        collect(0, part_ref, p)

    def backward_tiles(p, first_tile, tiles):
        if first_tile == 0:
            clear()
        tiles_times(
            1,
            lambda source: grads[p][:, :, :, source].reshape(wide, TILE),
            by_col,
            first_tile,
            tiles,
        )
        if first_tile + tiles == TILE:
            collect(1, back_ref, p)

    span = nodes // MID_CHUNKS
    pair = N_X // 2
    ring = {
        "x": (x, x_up, x_down, x_far, x_right, x_left),
        "z": (zh, z_up, z_down, z_far, z_right, z_left),
    }

    def axes(u):
        return ("z", "x") if u in Z_FIRST else ("x", "z")

    def unit(u):
        p, q = u // MID_CHUNKS, u % MID_CHUNKS
        return p, pl.ds(q * span, span)

    def half_lanes(u, side):
        return pl.ds((u % MID_CHUNKS) * span + side * (span // 2), span // 2)

    def grid(ref, axis, along, across, lanes):
        if axis == "x":
            return ref.at[along, across, :, lanes]
        return ref.at[across, along, :, lanes]

    def part(coord, side, u):
        p, lanes = unit(u)
        return grid(part_ref.at[p], axes(u)[0], coord, pl.ds(side * pair, pair), lanes)

    def slot(i, u):
        p, lanes = unit(u)
        return in_ref.at[i, p, :, :, lanes]

    def merged(i, u):
        p, lanes = unit(u)
        return merge_ref.at[i, p, :, :, lanes]

    def reduce_out(u):
        me, up, down, far, right, left = ring[axes(u)[0]]
        links.start(part(far, 0, u), slot(0, u), right, ("f", u))
        links.start(part(far, 1, u), slot(1, u), left, ("f", u))
        links.start(part(up, 1, u), slot(2, u), right, ("d", u))
        links.start(part(down, 0, u), slot(3, u), left, ("d", u))

    def reduce_merge(u):
        me, up, down, far, right, left = ring[axes(u)[0]]
        p, lanes = unit(u)
        links.wait(("f", u), in_ref.at[pl.ds(0, 2), p, :, :, lanes])
        merged(0, u)[...] = add(slot(0, u)[...], part(up, 0, u)[...])
        links.start(merged(0, u), slot(4, u), right, ("d", u))
        merged(1, u)[...] = add(slot(1, u)[...], part(down, 1, u)[...])
        links.start(merged(1, u), slot(5, u), left, ("d", u))

    def second_part(coord, side, u):
        return sum_ref.at[u // MID_CHUNKS, coord, :, half_lanes(u, side)]

    def second_slots(i, count, u):
        lanes = pl.ds((u % MID_CHUNKS) * (span // 2), span // 2)
        return z_ref.at[pl.ds(i, count), u // MID_CHUNKS, :, lanes]

    def second_slot(i, u):
        return z_ref.at[i, u // MID_CHUNKS, :, pl.ds((u % MID_CHUNKS) * (span // 2), span // 2)]

    def second_merged(i, u):
        lanes = pl.ds((u % MID_CHUNKS) * (span // 2), span // 2)
        return zmerge_ref.at[i, u // MID_CHUNKS, :, lanes]

    def reduce_second(u):
        p, lanes = unit(u)
        me = ring[axes(u)[0]][0]
        links.wait(("d", u), in_ref.at[pl.ds(0, 4), p, :, :, lanes])
        for side, (through, direct) in enumerate(((4, 3), (5, 2))):
            total = slot(through, u)[...].astype(F32) + slot(direct, u)[...].astype(F32)
            total = total + part(me, side, u)[...].astype(F32)
            sum_ref[p, pl.ds(side * pair, pair), :, lanes] = total.astype(BF16)
        me, up, down, far, right, left = ring[axes(u)[1]]
        links.start(second_part(far, 0, u), second_slot(0, u), right, ("zf", u))
        links.start(second_part(far, 1, u), second_slot(1, u), left, ("zf", u))
        links.start(second_part(up, 1, u), second_slot(2, u), right, ("zd", u))
        links.start(second_part(down, 0, u), second_slot(3, u), left, ("zd", u))

    def merge_second(u):
        me, up, down, far, right, left = ring[axes(u)[1]]
        links.wait(("zf", u), second_slots(0, 2, u))
        second_merged(0, u)[...] = add(second_slot(0, u)[...], second_part(up, 0, u)[...])
        links.start(second_merged(0, u), second_slot(4, u), right, ("zd", u))
        second_merged(1, u)[...] = add(second_slot(1, u)[...], second_part(down, 1, u)[...])
        links.start(second_merged(1, u), second_slot(5, u), left, ("zd", u))

    def activate(u):
        p, lanes = unit(u)
        me, up, down, far, right, left = ring[axes(u)[1]]
        links.wait(("zd", u), second_slots(0, 4, u))
        rows = pl.ds(p * own, own)
        for side, (through, direct) in enumerate(((4, 3), (5, 2))):
            here = half_lanes(u, side)
            value = second_slot(through, u)[...].astype(F32)
            value = value + second_slot(direct, u)[...].astype(F32)
            value = value + second_part(me, side, u)[...].astype(F32)
            scale = rs_ref[:, here]
            hidden_in = value * scale
            sigma = 1.0 / (1.0 + jnp.exp(-hidden_in))
            out_ref[rows, here] = (hidden_in * sigma).astype(BF16)
            slope = sigma * (1.0 + hidden_in * (1.0 - sigma))
            grad = cot_ref[rows, here].astype(F32) * slope * scale
            grads[p][x, zh, :, here] = grad.astype(BF16)
        mine = grads[p].at[x, zh, :, lanes]
        links.start(mine, mine, right, ("a", u))
        links.start(mine, mine, left, ("a", u))

    def gather_second(u):
        first_axis, axis = axes(u)
        me, up, down, far, right, left = ring[axis]
        across, ref = ring[first_axis][0], grads[u // MID_CHUNKS]
        lanes = unit(u)[1]
        links.wait(("a", u), ref.at[0, pl.ds(0, 2), :, lanes])
        near = grid(ref, axis, down, across, half_lanes(u, 0))
        links.start(near, near, right, ("b", u))
        near = grid(ref, axis, up, across, half_lanes(u, 1))
        links.start(near, near, left, ("b", u))

    def gather_first(u):
        p, lanes = unit(u)
        axis = axes(u)[0]
        me, up, down, far, right, left = ring[axis]
        links.wait(("b", u), grads[p].at[0, 0, :, lanes])
        mine = grid(grads[p], axis, me, slice(None), lanes)
        links.start(mine, mine, right, ("g", u))
        links.start(mine, mine, left, ("g", u))

    def gather_far(u):
        p, lanes = unit(u)
        axis = axes(u)[0]
        me, up, down, far, right, left = ring[axis]
        links.wait(("g", u), grads[p].at[pl.ds(0, 2), :, :, lanes])
        near = grid(grads[p], axis, down, pl.ds(0, pair), lanes)
        links.start(near, near, right, ("h", u))
        near = grid(grads[p], axis, up, pl.ds(pair, pair), lanes)
        links.start(near, near, left, ("h", u))

    def gather_end(u):
        p, lanes = unit(u)
        links.wait(("h", u), grads[p].at[0, :, :, lanes])

    end_rows = wide // END_CHUNKS
    end_half = end_rows // 2
    side_nodes = nodes // N_CORE
    mine_nodes = nodes // N_ROW

    def rows_of_unit(v, start=0, size=end_rows):
        return pl.ds(v * end_rows + start, size)

    def core_out(v):
        p, r = v // END_CHUNKS, v % END_CHUNKS
        there = pl.ds(pl.multiple_of((1 - core) * side_nodes, side_nodes), side_nodes)
        src = back_ref.at[p, pl.ds(r * end_rows, end_rows), there]
        sent["c", v] = links.start(src, core_ref.at[rows_of_unit(v), :], c_peer)

    def core_sum(v):
        p, r = v // END_CHUNKS, v % END_CHUNKS
        sent["c", v].wait_recv()
        for j in range(N_Y * N_ZL):
            here = pl.ds(j * mine_nodes, mine_nodes)
            there = pl.ds(
                pl.multiple_of(core * side_nodes + j * mine_nodes, mine_nodes), mine_nodes
            )
            half_ref[j // N_ZL, j % N_ZL, rows_of_unit(v), :] = add(
                back_ref[p, pl.ds(r * end_rows, end_rows), there], core_ref[rows_of_unit(v), here]
            )

    def y_part(y_of, side, v):
        rows = rows_of_unit(v, side * end_half, end_half)
        if v % 2:
            return ysum_ref.at[pl.ds(y_of, 1), rows, :]
        return half_ref.at[y_of, :, rows, :]

    def y_buffer(ref, i, v):
        rows = pl.ds(v * end_half, end_half)
        return ref.at[i, pl.ds(0, 1) if v % 2 else slice(None), rows, :]

    def yslots(count, v):
        return y_buffer(yin_ref, pl.ds(0, count), v)

    def yslot(i, v):
        return y_buffer(yin_ref, i, v)

    def ymerged(i, v):
        return y_buffer(ymerge_ref, i, v)

    def y_send(v):
        links.start(y_part(y_far, 0, v), yslot(0, v), y_right, ("yf", v))
        links.start(y_part(y_far, 1, v), yslot(1, v), y_left, ("yf", v))
        links.start(y_part(y_up, 1, v), yslot(2, v), y_right, ("yd", v))
        links.start(y_part(y_down, 0, v), yslot(3, v), y_left, ("yd", v))

    def y_out(v):
        core_sum(v)
        y_send(v)

    def z_first(v):
        core_sum(v)
        sent["yz", v] = links.start(
            half_ref.at[:, zp, rows_of_unit(v), :], zin_ref.at[:, rows_of_unit(v), :], z_peer
        )

    def z_then_y(v):
        sent["yz", v].wait_recv()
        for j in range(N_Y):
            ysum_ref[j, rows_of_unit(v), :] = add(
                half_ref[j, zl, rows_of_unit(v), :], zin_ref[j, rows_of_unit(v), :]
            )
        y_send(v)

    def y_merge(v):
        links.wait(("yf", v), yslots(2, v))
        ymerged(0, v)[...] = add(yslot(0, v)[...], y_part(y_up, 0, v)[...])
        links.start(ymerged(0, v), yslot(4, v), y_right, ("yd", v))
        ymerged(1, v)[...] = add(yslot(1, v)[...], y_part(y_down, 1, v)[...])
        links.start(ymerged(1, v), yslot(5, v), y_left, ("yd", v))

    def y_total(v, side):
        through, direct = ((4, 3), (5, 2))[side]
        total = yslot(through, v)[...].astype(F32) + yslot(direct, v)[...].astype(F32)
        return total + y_part(y, side, v)[...].astype(F32)

    def y_arrived(v):
        links.wait(("yd", v), yslots(4, v))

    def z_out(v):
        y_arrived(v)
        for side in range(2):
            rows = rows_of_unit(v, side * end_half, end_half)
            ysum_ref[pl.ds(0, N_ZL), rows, :] = y_total(v, side).astype(BF16)
        sent["yz", v] = links.start(
            ysum_ref.at[zp, rows_of_unit(v), :], zin_ref.at[0, rows_of_unit(v), :], z_peer
        )

    place = pl.ds(
        pl.multiple_of(core * side_nodes + (y * N_ZL + zl) * mine_nodes, mine_nodes), mine_nodes
    )

    def scaled(v):
        if v % 2:
            y_arrived(v)
            for side in range(2):
                rows = rows_of_unit(v, side * end_half, end_half)
                gp_ref[rows, :] = (y_total(v, side)[0] * cs_ref[:, place]).astype(BF16)
            return
        sent["yz", v].wait_recv()
        rows = rows_of_unit(v)
        value = ysum_ref[zl, rows, :].astype(F32) + zin_ref[0, rows, :].astype(F32)
        gp_ref[rows, :] = (value * cs_ref[:, place]).astype(BF16)

    def spread(name, src_of, dst):
        for d in range(1, N_ROW):
            links.start(src_of((g + d) % N_ROW), dst, row_group[d - 1], name)
        return src_of(g)

    def spread_weight(p):
        gwt_ref[p] = lax.dot_general(
            gp_ref[pl.ds(p * wide, wide), :],
            all_ref[:, :, place].reshape(feats, mine_nodes),
            (((1,), (1,)), ((), ())),
            preferred_element_type=F32,
        ).astype(BF16)

        def piece(owner):
            return gwt_ref.at[p, pl.ds(pl.multiple_of(owner * own, own), own), :]

        spread(("gw", p), piece, gwl_ref.at[p, g])

    def sum_weight(p):
        links.wait(("gw", p), gwl_ref.at[p, pl.ds(0, N_ROW - 1)])
        total = gwt_ref[p, pl.ds(pl.multiple_of(g * own, own), own), :].astype(F32)
        for d in range(1, N_ROW):
            total = total + gwl_ref[p, (g + d) % N_ROW].astype(F32)
        gw_ref[pl.ds(p * own, own), :] = total

    def feature_product():
        gft_ref[...] = lax.dot_general(
            wt_ref[...], gp_ref[...], (((0,), (0,)), ((), ())), preferred_element_type=F32
        ).astype(BF16)

    def spread_features():
        def piece(owner):
            return gft_ref.at[pl.ds(pl.multiple_of(owner * depth, depth), depth), :]

        mine = spread("gf", piece, gf_ref.at[:, place])
        gf_ref[:, place] = mine[...]

    def share_out(name, p, buffer, group):
        sums = lw_ref.at[0 if name == "px" else 1, p]
        sums[...] = gw_ref[pl.ds(p * own, own), :].astype(BF16)
        for i, peer in enumerate(group):
            links.start(sums, buffer.at[i, p], peer, (name, p))

    def share_in(name, p, buffer, group):
        total = gw_ref[pl.ds(p * own, own), :]
        links.wait((name, p), buffer.at[:, p])
        for i in range(len(group)):
            total = total + buffer[i, p].astype(F32)
        gw_ref[pl.ds(p * own, own), :] = total

    ag_own(0)
    ag_own(1)
    ag_own(2)
    prepare()
    ag_z(0)
    ag_y(0)
    ag_own(3)
    ag_z(1)
    ag_y(1)
    ag_far(0)
    ag_z(2)
    ag_y(2)
    ag_far(1)
    ag_last(0)
    ag_z(3)
    ag_y(3)
    ag_far(2)
    ag_last(1)
    project(0)
    ag_far(3)
    ag_last(2)
    project(1)
    ag_last(3)
    project(2)
    project(3)

    units = PARTS * MID_CHUNKS
    share = TILE // 4
    local["idx"].wait()
    forward_tiles(0)
    reduce_out(0)
    reduce_out(1)
    forward_tiles(1)
    x_lags = (
        (0, reduce_merge), (-2, reduce_out), (1, reduce_second), (2, merge_second),
        (3, activate), (4, gather_second), (5, gather_first), (6, gather_far),
    )
    z_lags = (
        (0, reduce_out), (2, reduce_merge), (3, reduce_second), (4, merge_second),
        (6, activate), (7, gather_second), (9, gather_first),
    )
    x_first = [u for u in range(units) if u not in Z_FIRST]
    steps = len(x_first) + 6
    for step in range(steps - 2):
        for lag, act in x_lags:
            if max(0, -lag) <= step - lag < len(x_first):
                act(x_first[step - lag])
        for lag, act in z_lags:
            for u in Z_FIRST:
                if step == lag:
                    act(u)
    for u in range(MID_CHUNKS):
        gather_end(u)
    gather_first(x_first[-1])
    backward_tiles(0, 0, 2 * share)
    gather_far(x_first[-2])
    for u in Z_FIRST:
        gather_far(u)
    backward_tiles(0, 2 * share, 2 * share)
    core_out(1)
    core_out(0)
    gather_far(x_first[-1])
    z_first(1)
    y_out(0)
    for u in range(MID_CHUNKS, units):
        gather_end(u)
    backward_tiles(1, 0, 2 * share)
    y_merge(0)
    backward_tiles(1, 2 * share, 2 * share)
    core_out(3)
    core_out(2)
    z_then_y(1)
    z_first(3)
    y_out(2)
    y_merge(1)
    z_out(0)
    scaled(1)
    scaled(0)
    spread_weight(0)
    y_merge(2)
    z_then_y(3)
    z_out(2)
    y_merge(3)
    scaled(2)
    scaled(3)
    spread_weight(1)
    sum_weight(0)
    share_out("px", 0, px_ref, x_group)
    feature_product()
    share_in("px", 0, px_ref, x_group)
    share_out("pz", 0, pz_ref, zh_group)
    sum_weight(1)
    share_out("px", 1, px_ref, x_group)
    spread_features()
    share_in("px", 1, px_ref, x_group)
    share_out("pz", 1, pz_ref, zh_group)
    share_in("pz", 0, pz_ref, zh_group)
    share_in("pz", 1, pz_ref, zh_group)
    links.wait("gf", gft_ref.at[pl.ds(0, (N_ROW - 1) * depth), :])
    links.drain()


def write_kernel(*refs):
    count = len(refs) // 2
    for i in range(count):
        refs[count + i][...] = refs[i][...]


def shards(features, weight, degrees, tile_values, tile_row, tile_col, tile_count, cotangent):
    nodes, depth = features.shape
    feats, hidden = weight.shape
    wide, own = hidden // PARTS, depth // PARTS
    mine = nodes // N_ROW
    side = nodes // N_CORE
    tiles = tile_values[0, 0]
    vmem = pl.BlockSpec(memory_space=pltpu.VMEM)
    anywhere = pl.BlockSpec(memory_space=pl.ANY)

    def buffer(*shape, dtype=BF16):
        return pltpu.VMEM(shape, dtype)

    results = pl.pallas_call(
        kernel,
        out_shape=(
            jax.ShapeDtypeStruct((depth, nodes), BF16),
            jax.ShapeDtypeStruct((depth, nodes), BF16),
            jax.ShapeDtypeStruct((depth, feats), F32),
        ),
        in_specs=[anywhere, anywhere, anywhere, anywhere, vmem, vmem, vmem, anywhere],
        out_specs=(vmem, vmem, vmem),
        scratch_shapes=[
            buffer(N_ROW, depth, nodes),
            buffer(*tiles.shape),
            buffer(feats, hidden),
            buffer(hidden, feats),
            buffer(depth, nodes),
            buffer(2, nodes // TILE, TILE, dtype=I32),
            buffer(1, nodes, dtype=F32),
            buffer(1, nodes, dtype=F32),
            buffer(8, TILE, dtype=I32),
            pltpu.SMEM((8, TILE), I32),
            buffer(2, TILE, TILE, dtype=F32),
            buffer(2, TILE, TILE, dtype=F32),
            buffer(PARTS, wide, nodes),
            buffer(TILE, wide, TILE),
            buffer(wide, TILE, dtype=F32),
            buffer(PARTS, N_X, N_ZH, own, nodes),
            buffer(6, PARTS, N_X // 2, own, nodes),
            buffer(2, PARTS, N_X // 2, own, nodes),
            buffer(PARTS, N_X, own, nodes),
            buffer(6, PARTS, own, nodes // 2),
            buffer(2, PARTS, own, nodes // 2),
            buffer(N_X, N_ZH, own, nodes),
            buffer(N_X, N_ZH, own, nodes),
            buffer(PARTS, wide, nodes),
            buffer(hidden, side),
            buffer(N_Y, N_ZL, hidden, mine),
            buffer(6, N_ZL, hidden // 2, mine),
            buffer(2, N_ZL, hidden // 2, mine),
            buffer(N_Y, hidden, mine),
            buffer(N_Y, hidden, mine),
            buffer(hidden, mine),
            buffer(feats, mine),
            buffer(PARTS, wide, feats),
            buffer(PARTS, N_ROW, own, feats),
            buffer(2, PARTS, own, feats),
            buffer(N_X - 1, PARTS, own, feats),
            buffer(N_ZH - 1, PARTS, own, feats),
            pltpu.SemaphoreType.DMA((7,)),
            pltpu.SemaphoreType.DMA((SENDS,)),
            pltpu.SemaphoreType.DMA((RECEIVES,)),
        ],
        compiler_params=pltpu.CompilerParams(
            collective_id=0, has_side_effects=True, vmem_limit_bytes=VMEM_BYTES
        ),
        name="layer",
    )(
        features.T,
        weight,
        degrees.reshape(-1, TILE),
        tiles,
        tile_row[0],
        tile_col[0],
        tile_count,
        cotangent.T,
    )
    output, grad_features, grad_weight = pl.pallas_call(
        write_kernel,
        out_shape=tuple(jax.ShapeDtypeStruct(r.shape, r.dtype) for r in results),
        in_specs=[vmem] * len(results),
        out_specs=(vmem,) * len(results),
        name="write",
    )(*results)
    return (output.T, grad_features.T, grad_weight.T)


def solution(mesh):
    in_specs = (
        P("col", "row"),
        P(),
        P(),
        P("row", "col", None, None, None),
        P("row", "col", None),
        P("row", "col", None),
        P("row", "col"),
        P("row", "col"),
    )
    out_specs = (P("row", "col"), P("col", "row"), P(None, "row"))
    return jax.shard_map(shards, mesh=mesh, in_specs=in_specs, out_specs=out_specs, check_vma=False)
```
